32 devices in a mesh: dp: 4 (over z), seq: 8 (over y, x, core).
Axes of the slice: x: 2, y: 2, z: 4, core: 2. Of those that a mesh axis runs over, the one named last changes fastest.
Arguments:
- tokens: bfloat16 [64, 4, 2560], P('dp'), may hold values from -6 to 6
- attn_gain: float32 [2560], replicated, may hold values from 0.1 to 1.9
- qkv_weight: bfloat16 [3072, 2560], P(('seq', 'dp'))
- out_weight: bfloat16 [2560, 2560], P(('seq', 'dp')), may hold values from -0.125 to 0.125
- mlp_gain: float32 [2560], replicated, may hold values from 0.1 to 1.9
- gate_up: bfloat16 [2, 7680, 2560], P(None, 'seq'), may hold values from -0.125 to 0.125
- down_weight: bfloat16 [7680, 2560], P('seq'), may hold values from -0.0625 to 0.0625
- kv_pool: bfloat16 [2048, 128, 512], P(('dp', 'seq')), may hold values from -6 to 6
- cache_len: int32 [64], P('dp'), may hold values from 1 to 16384, as said below
- page_table: int32 [64, 16], P('dp'), may hold values from 0 to 511, as said below
Outputs:
- layer_out: bfloat16 [64, 4, 2560], P('dp')
- written_pool: bfloat16 [2048, 128, 512], P(('dp', 'seq'))
The draws below stay inside these ranges and needn't reach their ends.
Inputs may be any that keep to these rules, and one draw needn't show every extreme that they name: `cache_len`: some request of the whole batch has exactly 16384 cached tokens; lengths under 2048 occur. `page_table`: within the 16 requests of one dp index all entries differ. Slot s lies on seq index s // 64; in every dp index some seq index holds exactly 64 of its pages.
All inputs are finite; a program needn't handle non-finite values.
Results may differ from the reference program's by a relative error of at most 0.018.
Values may be sent and summed in bfloat16 or wider, within the bound.
No kernel may reach another device: no remote copies, remote signals or barrier semaphores. Data moves between devices by JAX's collectives and lax.ppermute only.
A program may use at most 128 MiB of HBM per device.

```python
import jax
import jax.numpy as jnp
from jax import lax

D = 2560
H = 10
HD = 256
FF = 7680
WIN = 2048
PAGE = 128
NEW = 4
MAXLEN = 16384
R_DEV = 16
NP = 16
REQ = 64
P_DEV = 64
POOL = 2048
N_SEQ = 8


def draw_qkv_weight(key, part):
    first_key = jax.random.fold_in(key, 0)
    spread = D ** (-0.5)
    return (jax.random.normal(first_key, ((H + 2) * HD, D), jnp.float32) * spread).astype(jnp.bfloat16)


def draw_cache_len(key, part):
    pick_key, short_key, long_key, spot_key = jax.random.split(key, 4)
    short_len = jax.random.randint(short_key, (REQ,), 1, WIN + 1)
    long_len = jax.random.randint(long_key, (REQ,), WIN, MAXLEN + 1)
    lengths = jnp.where(jax.random.randint(pick_key, (REQ,), 0, 2) == 0, short_len, long_len)
    chosen = jax.random.randint(spot_key, (), 0, REQ)
    return jnp.where(jnp.arange(REQ) == chosen, MAXLEN, lengths).astype(jnp.int32)


def draw_page_table(key, part):
    group_slots = P_DEV * N_SEQ
    wanted = R_DEV * NP

    def one_group(group_key):
        bias_key, hot_key, noise_key, order_key = jax.random.split(group_key, 4)
        bias = jax.random.randint(bias_key, (N_SEQ,), 0, 4)
        hottest = jax.random.randint(hot_key, (), 0, N_SEQ)
        bias = jnp.where(jnp.arange(N_SEQ) == hottest, 8, bias)
        noise = jax.random.randint(noise_key, (group_slots,), 0, 1024)
        slot_ids = jnp.arange(group_slots, dtype=jnp.int32)
        owner_dev = slot_ids // P_DEV
        score = (bias[owner_dev] * 1024 + noise) * group_slots + slot_ids
        unused, picked = lax.top_k(score, wanted)
        shuffled = jax.random.permutation(order_key, picked)
        return shuffled.reshape(R_DEV, NP).astype(jnp.int32)
    group_keys = jax.random.split(key, REQ // R_DEV)
    return jax.vmap(one_group)(group_keys).reshape(REQ, NP).astype(jnp.int32)


def levels(own_key, dims, pieces, low, top_value):
    def one(position, blocks):
        heights = jax.random.uniform(jax.random.fold_in(jax.random.fold_in(own_key, 6), position), (blocks,), jnp.float32, low / len(pieces), top_value / len(pieces))
        return jnp.repeat(jnp.exp(heights), dims[position] // blocks).reshape((-1,) + (1,) * (len(dims) - position - 1))

    level = one(*pieces[0])
    for cut in pieces[1:]:
        level = level * one(*cut)
    return level


def scatter_about(own_key, shape, deviation, limit, pieces=(), kind=jnp.bfloat16):
    entries = jax.random.normal(own_key, shape, jnp.float32) * deviation
    if len(pieces) > 0:
        entries = levels(own_key, shape, pieces, -0.22, 0.18) * entries
    return jnp.clip(entries, min=-limit, max=limit).astype(kind)


def setup_inputs(seed: int = 0) -> dict:
    keys = jax.random.split(jax.random.key(seed), 11)
    return {
        "tokens": scatter_about(keys[0], (REQ, NEW, D), 1.0, 6.0, ((0, 4),)),
        "attn_gain": jnp.clip(1.0 + 0.18 * jax.random.normal(keys[1], (D,), jnp.float32), 0.1, 1.9),
        "qkv_weight": draw_qkv_weight(jax.random.fold_in(keys[10], 71), 0),
        "out_weight": scatter_about(keys[3], (D, H * HD), (H * HD) ** -0.5, 0.125, ((0, 32),)),
        "mlp_gain": jnp.clip(1.0 + 0.18 * jax.random.normal(keys[4], (D,), jnp.float32), 0.1, 1.9),
        "gate_up": scatter_about(keys[5], (2, FF, D), D ** -0.5, 0.125, ((1, 8),)),
        "down_weight": scatter_about(keys[6], (FF, D), FF ** -0.5, 0.0625, ((0, 8),)),
        "kv_pool": scatter_about(keys[7], (POOL, PAGE, 2 * HD), 1.0, 6.0, ((0, 32),)),
        "cache_len": draw_cache_len(jax.random.fold_in(keys[10], 71), 0),
        "page_table": draw_page_table(jax.random.fold_in(keys[10], 71), 0),
    }


def rms_norm(values, gains):
    floats = values.astype(jnp.float32)
    return floats * lax.rsqrt(lax.optimization_barrier(jnp.mean(floats * floats, axis=-1, keepdims=True)) + 1e-06) * gains

def rotate(values, positions):
    quarter = values.shape[-1] // 4
    freq_index = jnp.arange(quarter).astype(jnp.float32)
    inverse = 10000.0 ** (-freq_index / quarter)
    angles = positions[..., None] * inverse
    first = values[..., :quarter]
    second = values[..., quarter:2 * quarter]
    others = values[..., 2 * quarter:]
    cosine = jnp.cos(angles)
    sine = jnp.sin(angles)
    return jnp.concatenate([first * cosine - second * sine, second * cosine + first * sine, others], axis=-1)

def reference(tokens, attn_gain, qkv_weight, out_weight, mlp_gain, gate_up, down_weight, kv_pool, cache_len, page_table):
    group_slots = P_DEV * N_SEQ
    scale = HD ** (-0.5)
    normed = rms_norm(tokens, attn_gain).astype(jnp.bfloat16).reshape(REQ * NEW, D)
    projected = jnp.dot(normed, qkv_weight.T, preferred_element_type=jnp.float32).astype(jnp.bfloat16)
    projected = projected.reshape(REQ, NEW, (H + 2) * HD)
    positions_int = cache_len[:, None] + jnp.arange(NEW, dtype=jnp.int32)[None, :]
    positions = positions_int.astype(jnp.float32)
    queries = rotate(projected[:, :, :H * HD].astype(jnp.float32).reshape(REQ, NEW, H, HD), positions[:, :, None]).astype(jnp.bfloat16)
    keys_new = rotate(projected[:, :, H * HD:(H + 1) * HD].astype(jnp.float32), positions).astype(jnp.bfloat16)
    values_new = projected[:, :, (H + 1) * HD:]

    def attend(request):
        group = request // R_DEV
        rows_index = group * group_slots + page_table[request]
        cached = kv_pool[rows_index].reshape(WIN, 2 * HD)
        length = cache_len[request]
        cycle = jnp.arange(WIN, dtype=jnp.int32)
        key_pos = length - 1 - jnp.mod(length - 1 - cycle, WIN)
        query_pos = length + jnp.arange(NEW, dtype=jnp.int32)
        keys_all = jnp.concatenate([cached[:, :HD], keys_new[request]], axis=0).astype(jnp.float32)
        vals_all = jnp.concatenate([cached[:, HD:], values_new[request]], axis=0).astype(jnp.float32)
        seen_cached = (key_pos[None, :] >= 0) & (key_pos[None, :] > query_pos[:, None] - WIN)
        seen_new = jnp.arange(NEW)[None, :] <= jnp.arange(NEW)[:, None]
        visible = jnp.concatenate([seen_cached, seen_new], axis=1)[:, None, :]
        scores = jnp.einsum('thd,kd->thk', queries[request].astype(jnp.float32), keys_all) * scale
        peak = lax.optimization_barrier(jnp.max(jnp.where(visible, scores, -jnp.inf), axis=-1, keepdims=True))
        weights = jnp.where(visible, jnp.exp(scores - peak), 0.0)
        denominator = lax.optimization_barrier(jnp.sum(weights, axis=-1, keepdims=True))
        rounded = lax.optimization_barrier(weights.astype(jnp.bfloat16)).astype(jnp.float32)
        mixed = jnp.einsum('thk,kd->thd', rounded, vals_all) / denominator
        return mixed.reshape(NEW, H * HD)
    attended = lax.map(attend, jnp.arange(REQ, dtype=jnp.int32)).astype(jnp.bfloat16).reshape(REQ * NEW, H * HD)
    heads_out = jnp.dot(attended, out_weight.T, preferred_element_type=jnp.float32).astype(jnp.bfloat16)
    residual = (tokens.reshape(REQ * NEW, D).astype(jnp.float32) + heads_out.astype(jnp.float32)).astype(jnp.bfloat16)
    hidden_in = rms_norm(residual, mlp_gain).astype(jnp.bfloat16)
    gate = jnp.dot(hidden_in, gate_up[0].T, preferred_element_type=jnp.float32)
    upward = jnp.dot(hidden_in, gate_up[1].T, preferred_element_type=jnp.float32)
    hidden = (jax.nn.gelu(gate, approximate=True) * upward).astype(jnp.bfloat16)
    down_sum = jnp.dot(hidden, down_weight, preferred_element_type=jnp.float32)
    layer_out = (residual.astype(jnp.float32) + down_sum).astype(jnp.bfloat16).reshape(REQ, NEW, D)
    page_index = jnp.mod(positions_int // PAGE, NP).astype(jnp.int32)
    slot_taken = jnp.take_along_axis(page_table, page_index, axis=1)
    group_index = (jnp.arange(REQ, dtype=jnp.int32) // R_DEV)[:, None]
    target = group_index * group_slots + slot_taken
    offset = jnp.mod(positions_int, PAGE).astype(jnp.int32)
    written_pool = kv_pool.at[target, offset].set(jnp.concatenate([keys_new, values_new], axis=-1))
    return (layer_out, written_pool)
```

```python
import functools

import jax
import jax.numpy as jnp
from jax import lax
from jax.experimental import pallas as pl
from jax.experimental.pallas import tpu as pltpu
from jax.sharding import PartitionSpec as P

f32 = jnp.float32
bf16 = jnp.bfloat16
low_fill = -1e30
floor_peak = -1e29
contract = (((1,), (1,)), ((), ()))


def rms_norm(values, gains):
    floats = values.astype(f32)
    return floats * lax.rsqrt(jnp.mean(floats * floats, axis=-1, keepdims=True) + 1e-06) * gains


def swap(values, axis, size, mask):
    return lax.ppermute(values, axis, [(i, i ^ mask) for i in range(size)])


def tree_sum(terms):
    while len(terms) > 1:
        terms = [terms[i] + terms[i + 1] for i in range(0, len(terms), 2)]
    return terms[0]


def copy_kernel(parts, source, target, sems):
    count = source.shape[0] // parts
    copies = [
        pltpu.make_async_copy(
            source.at[pl.ds(i * count, count)], target.at[pl.ds(i * count, count)], sems.at[i]
        )
        for i in range(parts)
    ]
    for copy in copies:
        copy.start()
    for copy in copies:
        copy.wait()


def copy_pool(kv_pool):
    parts = min(16, kv_pool.shape[0])
    return pl.pallas_call(
        functools.partial(copy_kernel, parts),
        out_shape=jax.ShapeDtypeStruct(kv_pool.shape, kv_pool.dtype),
        in_specs=[pl.BlockSpec(memory_space=pl.ANY)],
        out_specs=pl.BlockSpec(memory_space=pl.ANY),
        scratch_shapes=[pltpu.SemaphoreType.DMA((parts,))],
        cost_estimate=pl.CostEstimate(
            flops=0, bytes_accessed=2 * kv_pool.size * 2, transcendentals=0
        ),
        name="copy_pool",
    )(kv_pool)


def split_three(values):
    high = values.astype(bf16).astype(f32)
    middle = (values - high).astype(bf16).astype(f32)
    low = (values - high - middle).astype(bf16).astype(f32)
    return high, middle, low


def diagonal(rows):
    return lax.broadcasted_iota(jnp.int32, (rows, 128), 0) == lax.broadcasted_iota(
        jnp.int32, (rows, 128), 1
    )


def pack_logs(columns, rows):
    eye = diagonal(rows)
    lines = [
        jnp.sum(jnp.where(eye, jnp.broadcast_to(c, (rows, 128)), 0.0), axis=0, keepdims=True)
        for c in columns
    ]
    lines += [jnp.zeros((1, 128), f32)] * (8 - len(lines))
    high, middle, low = split_three(jnp.concatenate(lines, axis=0))
    return jnp.concatenate(
        [
            jnp.concatenate([high, middle], axis=1),
            jnp.concatenate([low, jnp.zeros((8, 128), f32)], axis=1),
        ],
        axis=0,
    )


def unpack_logs(block):
    return block[0:8, 0:128] + block[0:8, 128:256] + block[8:16, 0:128]


def merge_parts(packs, requests, rows):
    total = requests * rows
    bodies = [ref[...].astype(f32) for ref in packs]
    logs = [unpack_logs(body[total : total + 16]) for body in bodies]
    eye = diagonal(rows)
    results, columns = [], []
    for r in range(requests):
        cols = [
            jnp.sum(
                jnp.where(eye, jnp.broadcast_to(log[r : r + 1, :], (rows, 128)), 0.0),
                axis=1,
                keepdims=True,
            )
            for log in logs
        ]
        top = functools.reduce(jnp.maximum, cols)
        scales = [jnp.exp(c - top) for c in cols]
        norm = functools.reduce(jnp.add, scales)
        parts = [
            body[r * rows : (r + 1) * rows] * scale for body, scale in zip(bodies, scales)
        ]
        results.append(functools.reduce(jnp.add, parts) / norm)
        columns.append(top + jnp.log(norm))
    return results, columns


def pair_kernel(requests, rows, mine, other, out):
    results, columns = merge_parts([mine, other], requests, rows)
    body = jnp.concatenate(results + [pack_logs(columns, rows)], axis=0)
    out[...] = body.astype(bf16)


def merge_pair(mine, other, requests, rows):
    return pl.pallas_call(
        functools.partial(pair_kernel, requests, rows),
        out_shape=jax.ShapeDtypeStruct(mine.shape, bf16),
        name="merge_pair",
    )(mine, other)


def final_kernel(count, requests, rows, heads, *refs):
    packs, out, scratch_low, scratch_high = refs[:count], refs[count], refs[-2], refs[-1]
    results, unused = merge_parts(packs, requests, rows)
    body = jnp.concatenate(results, axis=0)
    scratch_low[...] = body[:, 0:128]
    scratch_high[...] = body[:, 128:256]
    lines = requests * rows // heads
    for h in range(heads):
        low = scratch_low[pl.ds(h, lines, stride=heads), :]
        high = scratch_high[pl.ds(h, lines, stride=heads), :]
        out[:, h * 256 : (h + 1) * 256] = jnp.concatenate([low, high], axis=1).astype(bf16)


def merge_final(packs, requests, rows, heads):
    lines = requests * rows // heads
    return pl.pallas_call(
        functools.partial(final_kernel, len(packs), requests, rows, heads),
        out_shape=jax.ShapeDtypeStruct((lines, heads * 256), bf16),
        scratch_shapes=[pltpu.VMEM((requests * rows, 128), f32)] * 2,
        name="merge_final",
    )(*packs)


def attention_kernel(
    dims,
    slots,
    patches,
    lengths,
    place,
    cosine,
    sine,
    projected,
    pool,
    pool_copy,
    packed,
    pool_out,
    buffer,
    query_low,
    query_high,
    fresh,
    peak,
    norm,
    total,
    patch_buffer,
    in_sems,
    patch_sems,
):
    requests, new_count, heads, pages, page_len, window, chunk, n_seq = dims
    rows = new_count * heads
    lines = requests * new_count
    chunks = pages // chunk
    loads = [
        pltpu.make_async_copy(
            pool.at[pl.ds(i * chunk, chunk)], buffer.at[pl.ds(i * chunk, chunk)], in_sems.at[i]
        )
        for i in range(chunks)
    ]
    for load in loads:
        load.start()

    cos = cosine[...]
    sin = sine[...]

    def turned(block):
        x = projected[:, block * 128 : (block + 1) * 128].astype(f32)
        return (x * cos + pltpu.roll(x, 64, 1) * sin).astype(bf16).astype(f32)

    for h in range(heads):
        query_low[pl.ds(h, lines, stride=heads), :] = turned(2 * h)
        query_high[pl.ds(h, lines, stride=heads), :] = projected[
            :, h * 256 + 128 : h * 256 + 256
        ].astype(f32)
    fresh[:, 0:128] = turned(2 * heads).astype(bf16)
    fresh[:, 128:512] = projected[:, heads * 256 + 128 : heads * 256 + 512]

    peak[...] = jnp.full(peak.shape, floor_peak, f32)
    norm[...] = jnp.zeros(norm.shape, f32)
    total[...] = jnp.zeros(total.shape, f32)

    token_of = lax.broadcasted_iota(jnp.int32, (rows, 1), 0) // heads
    lane = lax.broadcasted_iota(jnp.int32, (1, page_len), 1)
    scale = 256.0 ** (-0.5)

    def query_of(r):
        span = pl.ds(pl.multiple_of(r * rows, 8), rows)
        return jnp.concatenate([query_low[span, :], query_high[span, :]], axis=1).astype(bf16)

    def part(query, keys, values, visible):
        scores = lax.dot_general(query, keys, contract, preferred_element_type=f32) * scale
        scores = jnp.where(visible, scores, low_fill)
        top = jnp.maximum(jnp.max(scores, axis=1, keepdims=True), floor_peak)
        weights = jnp.exp(scores - top)
        amount = jnp.sum(weights, axis=1, keepdims=True)
        mixed = jnp.dot(weights.astype(bf16), values, preferred_element_type=f32)
        return top, amount, mixed

    def add(r, top, amount, mixed):
        span = pl.ds(pl.multiple_of(r * rows, 8), rows)
        old = peak[span, :]
        high = jnp.maximum(old, top)
        keep = jnp.exp(old - high)
        take = jnp.exp(top - high)
        peak[span, :] = high
        norm[span, :] = norm[span, :] * keep + amount * take
        total[span, :] = total[span, :] * jnp.concatenate(
            [keep, keep], axis=1
        ) + mixed * jnp.concatenate([take, take], axis=1)

    me = place[0]
    fresh_lane = lax.broadcasted_iota(jnp.int32, (1, lines), 1)
    for step in range(-(-requests // n_seq)):
        r = me + step * n_seq

        @pl.when(r < requests)
        def _():
            index = fresh_lane - r * new_count
            seen = (index >= 0) & (index <= token_of)
            add(r, *part(query_of(r), fresh[:, 0:256], fresh[:, 256:512], seen))

    def one_chunk(c, carry):
        pltpu.make_async_copy(
            pool.at[pl.ds(c * chunk, chunk)], buffer.at[pl.ds(c * chunk, chunk)], in_sems.at[c]
        ).wait()
        parts = []
        for k in range(chunk):
            page = c * chunk + k
            r = slots[0, page]
            length = slots[1, page]
            start = slots[2, page] * page_len
            age = jnp.bitwise_and(length - 1 - start - lane, window - 1)
            limit = jnp.minimum(length - 1, window - 2 - token_of)
            parts.append(
                (
                    r,
                    part(
                        query_of(r),
                        buffer[page, :, 0:256],
                        buffer[page, :, 256:512],
                        age <= limit,
                    ),
                )
            )
        for r, values in parts:
            add(r, *values)
        return carry

    lax.fori_loop(0, chunks, one_chunk, 0)

    def patch_copy(i):
        row = pl.multiple_of(patches[1, i] * 16, 16)
        return pltpu.make_async_copy(
            patch_buffer.at[i],
            pool_out.at[jnp.maximum(patches[0, i], 0), pl.ds(row, 16)],
            patch_sems.at[i],
        )

    def write_patch(i, carry):
        slot = patches[0, i]

        @pl.when(slot >= 0)
        def _():
            r = i // 2
            row = pl.multiple_of(patches[1, i] * 16, 16)
            old = buffer[slot, pl.ds(row, 16), :]
            cycle = patches[2, i] * page_len + row
            line = lax.broadcasted_iota(jnp.int32, (16, lines), 0)
            token = jnp.bitwise_and(cycle + line - lengths[r], window - 1)
            column = lax.broadcasted_iota(jnp.int32, (16, lines), 1)
            pick = (token < new_count) & (column == r * new_count + token)
            new = jnp.dot(pick.astype(f32).astype(bf16), fresh[...], preferred_element_type=f32)
            row_token = jnp.bitwise_and(
                cycle + lax.broadcasted_iota(jnp.int32, (16, 1), 0) - lengths[r], window - 1
            )
            patch_buffer[i] = jnp.where(row_token < new_count, new, old.astype(f32)).astype(bf16)
            patch_copy(i).start()

        return carry

    lax.fori_loop(0, 2 * requests, write_patch, 0)

    half = requests // 2
    for side in range(2):
        logs = []
        for k in range(half):
            r = side * half + k
            span = slice(r * rows, (r + 1) * rows)
            amount = norm[span, :]
            some = amount > 0.0
            safe = jnp.where(some, amount, 1.0)
            logs.append(jnp.where(some, peak[span, :] + jnp.log(safe), low_fill))
            inverse = jnp.where(some, 1.0 / safe, 0.0)
            total[span, :] = total[span, :] * jnp.concatenate([inverse, inverse], axis=1)
        packed[side, 0 : half * rows, :] = total[
            side * half * rows : (side + 1) * half * rows, :
        ].astype(bf16)
        packed[side, half * rows : half * rows + 16, :] = pack_logs(logs, rows).astype(bf16)

    def wait_patch(i, carry):
        @pl.when(patches[0, i] >= 0)
        def _():
            patch_copy(i).wait()

        return carry

    lax.fori_loop(0, 2 * requests, wait_patch, 0)


def attention(dims, slots, patches, lengths, place, cosine, sine, projected, pool, pool_copy):
    requests, new_count, heads, pages, page_len, window, chunk, n_seq = dims
    rows = new_count * heads
    lines = requests * new_count
    smem = pl.BlockSpec(memory_space=pltpu.SMEM)
    vmem = pl.BlockSpec(memory_space=pltpu.VMEM)
    hbm = pl.BlockSpec(memory_space=pl.ANY)
    return pl.pallas_call(
        functools.partial(attention_kernel, dims),
        out_shape=(
            jax.ShapeDtypeStruct((2, requests // 2 * rows + 16, 256), bf16),
            jax.ShapeDtypeStruct(pool.shape, pool.dtype),
        ),
        in_specs=[smem, smem, smem, smem, vmem, vmem, vmem, hbm, hbm],
        out_specs=(vmem, hbm),
        scratch_shapes=[
            pltpu.VMEM(pool.shape, bf16),
            pltpu.VMEM((requests * rows, 128), f32),
            pltpu.VMEM((requests * rows, 128), f32),
            pltpu.VMEM((lines, 512), bf16),
            pltpu.VMEM((requests * rows, 128), f32),
            pltpu.VMEM((requests * rows, 128), f32),
            pltpu.VMEM((requests * rows, 256), f32),
            pltpu.VMEM((2 * requests, 16, 512), bf16),
            pltpu.SemaphoreType.DMA((pages // chunk,)),
            pltpu.SemaphoreType.DMA((2 * requests,)),
        ],
        input_output_aliases={8: 1},
        compiler_params=pltpu.CompilerParams(vmem_limit_bytes=24 * 1024 * 1024),
        cost_estimate=pl.CostEstimate(
            flops=4 * pages * rows * page_len * 256,
            bytes_accessed=pool.size * 2,
            transcendentals=pages * rows * page_len,
        ),
        name="page_attention",
    )(slots, patches, lengths, place, cosine, sine, projected, pool, pool_copy)


def body(
    n_dp,
    n_seq,
    tokens,
    attn_gain,
    qkv_weight,
    out_weight,
    mlp_gain,
    gate_up,
    down_weight,
    kv_pool,
    cache_len,
    page_table,
):
    seq_index = lax.axis_index("seq")
    dp_index = lax.axis_index("dp")
    core = seq_index % 2
    chips = n_seq // 2
    requests, new_count, width = tokens.shape
    pages, page_len, pair_width = kv_pool.shape
    head_dim = pair_width // 2
    heads = out_weight.shape[1] // head_dim
    page_count = page_table.shape[1]
    window = page_count * page_len
    lines = requests * new_count
    half = lines // 2
    rows = new_count * heads

    def ordered(mine, other, axis=0):
        return jnp.where(
            core == 0,
            jnp.concatenate([mine, other], axis=axis),
            jnp.concatenate([other, mine], axis=axis),
        )

    out_local = lax.all_gather(out_weight, "dp", axis=0, tiled=True)

    stream = tokens.reshape(lines, width)
    my_half = jnp.where(core == 0, stream[:half], stream[half:])
    far = list(range(2, n_dp, 2))
    far_halves = [swap(my_half, "dp", n_dp, k) for k in far]
    partner_weight = swap(qkv_weight, "dp", n_dp, 1)
    pool_copy = copy_pool(kv_pool)
    far_half = jnp.concatenate(far_halves, axis=0)
    far_other = swap(far_half, "seq", n_seq, 1)
    groups = [stream]
    for i in range(len(far)):
        groups += [far_half[i * half : (i + 1) * half], far_other[i * half : (i + 1) * half]]
    normed = rms_norm(jnp.concatenate(groups, axis=0), attn_gain).astype(bf16)
    by_mine = lax.dot_general(normed, qkv_weight, contract, preferred_element_type=f32)
    by_partner = lax.dot_general(normed, partner_weight, contract, preferred_element_type=f32)
    products = jnp.where(
        dp_index % 2 == 0,
        jnp.concatenate([by_mine, by_partner], axis=1),
        jnp.concatenate([by_partner, by_mine], axis=1),
    ).astype(bf16)
    blocks = [products[:lines]]
    for i, k in enumerate(far):
        back = swap(products[(i + 1) * lines : (i + 2) * lines], "dp", n_dp, k)
        blocks.append(ordered(back[:half], back[half:]))
    pair = dp_index // 2
    columns = []
    for j in range(n_dp // 2):
        block = blocks[0]
        for k in range(1, n_dp // 2):
            block = jnp.where((pair ^ k) == j, blocks[k], block)
        columns.append(block)
    projected = lax.all_gather(
        jnp.concatenate(columns, axis=1), "seq", axis=1, tiled=True
    )

    positions_int = cache_len[:, None] + jnp.arange(new_count, dtype=jnp.int32)[None, :]
    quarter = head_dim // 4
    inverse = 10000.0 ** (-jnp.arange(quarter).astype(f32) / quarter)
    angles = positions_int.reshape(lines, 1).astype(f32) * inverse
    cosine = jnp.cos(angles)
    sine = jnp.sin(angles)
    cosine = jnp.concatenate([cosine, cosine], axis=1)
    sine = jnp.concatenate([-sine, sine], axis=1)
    slot_ids = seq_index * pages + jnp.arange(pages, dtype=jnp.int32)
    matches = page_table[None, :, :] == slot_ids[:, None, None]
    number = jnp.arange(page_count, dtype=jnp.int32)[None, None, :]
    owner = jnp.arange(requests, dtype=jnp.int32)[None, :, None]
    slots = jnp.stack(
        [
            jnp.sum(jnp.where(matches, owner, 0), axis=(1, 2)),
            jnp.sum(jnp.where(matches, cache_len[None, :, None], 0), axis=(1, 2)),
            jnp.sum(jnp.where(matches, number, 0), axis=(1, 2)),
        ]
    )
    ends = jnp.stack([cache_len, cache_len + (new_count - 1)], axis=1)
    end_page = (ends // page_len) % page_count
    end_block = (ends % page_len) // 16
    hit = end_page[:, :, None] == jnp.arange(page_count, dtype=jnp.int32)[None, None, :]
    end_slot = jnp.sum(jnp.where(hit, page_table[:, None, :], 0), axis=2) - seq_index * pages
    good = (end_slot >= 0) & (end_slot < pages)
    same = (end_page[:, 0] == end_page[:, 1]) & (end_block[:, 0] == end_block[:, 1])
    good = good & jnp.stack([jnp.ones_like(same), ~same], axis=1)
    patches = jnp.stack(
        [
            jnp.where(good, end_slot, -1).reshape(-1),
            end_block.reshape(-1),
            end_page.reshape(-1),
        ]
    )

    dims = (requests, new_count, heads, pages, page_len, window, min(8, pages), n_seq)
    packed, written_pool = attention(
        dims,
        slots,
        patches,
        cache_len,
        seq_index.reshape(1),
        cosine,
        sine,
        projected,
        kv_pool,
        pool_copy,
    )

    side = requests // 2
    mine = jnp.where(core == 0, packed[0], packed[1])
    theirs = jnp.where(core == 0, packed[1], packed[0])
    merged = merge_pair(mine, swap(theirs, "seq", n_seq, 1), side, rows)
    packs = [merged] + [swap(merged, "seq", n_seq, 2 * c) for c in range(1, chips)]
    attended_half = merge_final(packs, side, rows, heads)
    attended = ordered(attended_half, swap(attended_half, "seq", n_seq, 1))

    heads_part = lax.dot_general(
        attended, out_local, contract, preferred_element_type=f32
    ).astype(bf16)
    heads_out = lax.all_gather(heads_part, "seq", axis=1, tiled=True)
    residual = (stream.astype(f32) + heads_out.astype(f32)).astype(bf16)
    hidden_in = rms_norm(residual, mlp_gain).astype(bf16)
    gate_and_up = jnp.einsum("rd,gfd->grf", hidden_in, gate_up, preferred_element_type=f32)
    hidden = (jax.nn.gelu(gate_and_up[0], approximate=True) * gate_and_up[1]).astype(bf16)
    partial_sum = jnp.dot(hidden, down_weight, preferred_element_type=f32)

    keep = jnp.where(core == 0, partial_sum[:half], partial_sum[half:])
    give = jnp.where(core == 0, partial_sum[half:], partial_sum[:half]).astype(bf16)
    chip_sum = (keep + swap(give, "seq", n_seq, 1).astype(f32)).astype(bf16)
    terms = [chip_sum] + [swap(chip_sum, "seq", n_seq, 2 * c) for c in range(1, chips)]
    full_half = tree_sum([term.astype(f32) for term in terms])
    my_residual = jnp.where(core == 0, residual[:half], residual[half:])
    out_half = (my_residual.astype(f32) + full_half).astype(bf16)
    layer_out = ordered(out_half, swap(out_half, "seq", n_seq, 1))
    return layer_out.reshape(requests, new_count, width), written_pool


def solution(mesh):
    in_specs = (
        P("dp", None, None),
        P(),
        P(("seq", "dp"), None),
        P(("seq", "dp"), None),
        P(),
        P(None, "seq", None),
        P("seq", None),
        P(("dp", "seq"), None, None),
        P("dp"),
        P("dp", None),
    )
    out_specs = (P("dp", None, None), P(("dp", "seq"), None, None))
    return jax.shard_map(
        functools.partial(body, mesh.shape["dp"], mesh.shape["seq"]),
        mesh=mesh,
        in_specs=in_specs,
        out_specs=out_specs,
        check_vma=False,
    )
```

```python
import functools

import jax
import jax.numpy as jnp
from jax import lax
from jax.experimental import pallas as pl
from jax.experimental.pallas import tpu as pltpu
from jax.sharding import PartitionSpec as P

f32 = jnp.float32
bf16 = jnp.bfloat16
low_fill = -1e30
floor_peak = -1e29
contract = (((1,), (1,)), ((), ()))


def rms_norm(values, gains):
    floats = values.astype(f32)
    return floats * lax.rsqrt(jnp.mean(floats * floats, axis=-1, keepdims=True) + 1e-06) * gains


def swap(values, axis, size, mask):
    return lax.ppermute(values, axis, [(i, i ^ mask) for i in range(size)])


def tree_sum(terms):
    while len(terms) > 1:
        terms = [terms[i] + terms[i + 1] for i in range(0, len(terms), 2)]
    return terms[0]


def copy_kernel(parts, source, target, buffer, in_sems, out_sems):
    count = source.shape[0] // parts
    spans = [pl.ds(i * count, count) for i in range(parts)]
    loads = [
        pltpu.make_async_copy(source.at[span], buffer.at[span], in_sems.at[i])
        for i, span in enumerate(spans)
    ]
    stores = [
        pltpu.make_async_copy(buffer.at[span], target.at[span], out_sems.at[i])
        for i, span in enumerate(spans)
    ]
    for load in loads:
        load.start()
    for load, store in zip(loads, stores):
        load.wait()
        store.start()
    for store in stores:
        store.wait()


def copy_pool(kv_pool):
    parts = min(16, kv_pool.shape[0])
    hbm = pl.BlockSpec(memory_space=pltpu.HBM)
    return pl.pallas_call(
        functools.partial(copy_kernel, parts),
        out_shape=pltpu.HBM(kv_pool.shape, kv_pool.dtype),
        in_specs=[hbm],
        out_specs=hbm,
        scratch_shapes=[
            pltpu.VMEM(kv_pool.shape, kv_pool.dtype),
            pltpu.SemaphoreType.DMA((parts,)),
            pltpu.SemaphoreType.DMA((parts,)),
        ],
        compiler_params=pltpu.CompilerParams(vmem_limit_bytes=24 * 1024 * 1024),
        cost_estimate=pl.CostEstimate(
            flops=0, bytes_accessed=2 * kv_pool.size * 2, transcendentals=0
        ),
        name="copy_pool",
    )(kv_pool)


def split_three(values):
    high = values.astype(bf16).astype(f32)
    middle = (values - high).astype(bf16).astype(f32)
    low = (values - high - middle).astype(bf16).astype(f32)
    return high, middle, low


def diagonal(rows):
    return lax.broadcasted_iota(jnp.int32, (rows, 128), 0) == lax.broadcasted_iota(
        jnp.int32, (rows, 128), 1
    )


def pack_logs(columns, rows):
    eye = diagonal(rows)
    lines = [
        jnp.sum(jnp.where(eye, jnp.broadcast_to(c, (rows, 128)), 0.0), axis=0, keepdims=True)
        for c in columns
    ]
    lines += [jnp.zeros((1, 128), f32)] * (8 - len(lines))
    high, middle, low = split_three(jnp.concatenate(lines, axis=0))
    return jnp.concatenate(
        [
            jnp.concatenate([high, middle], axis=1),
            jnp.concatenate([low, jnp.zeros((8, 128), f32)], axis=1),
        ],
        axis=0,
    )


def unpack_logs(block):
    return block[0:8, 0:128] + block[0:8, 128:256] + block[8:16, 0:128]


def merge_parts(packs, requests, rows):
    total = requests * rows
    bodies = [ref[...].astype(f32) for ref in packs]
    logs = [unpack_logs(body[total : total + 16]) for body in bodies]
    eye = diagonal(rows)
    results, columns = [], []
    for r in range(requests):
        cols = [
            jnp.sum(
                jnp.where(eye, jnp.broadcast_to(log[r : r + 1, :], (rows, 128)), 0.0),
                axis=1,
                keepdims=True,
            )
            for log in logs
        ]
        top = functools.reduce(jnp.maximum, cols)
        scales = [jnp.exp(c - top) for c in cols]
        norm = functools.reduce(jnp.add, scales)
        parts = [
            body[r * rows : (r + 1) * rows] * scale for body, scale in zip(bodies, scales)
        ]
        results.append(functools.reduce(jnp.add, parts) / norm)
        columns.append(top + jnp.log(norm))
    return results, columns


def pair_kernel(requests, rows, mine, other, out):
    results, columns = merge_parts([mine, other], requests, rows)
    body = jnp.concatenate(results + [pack_logs(columns, rows)], axis=0)
    out[...] = body.astype(bf16)


def merge_pair(mine, other, requests, rows):
    return pl.pallas_call(
        functools.partial(pair_kernel, requests, rows),
        out_shape=jax.ShapeDtypeStruct(mine.shape, bf16),
        in_specs=[pl.BlockSpec(memory_space=pltpu.VMEM)] * 2,
        out_specs=pl.BlockSpec(memory_space=pltpu.VMEM),
        name="merge_pair",
    )(mine, other)


def final_kernel(count, requests, rows, heads, *refs):
    packs, out, scratch_low, scratch_high = refs[:count], refs[count], refs[-2], refs[-1]
    results, unused = merge_parts(packs, requests, rows)
    body = jnp.concatenate(results, axis=0)
    scratch_low[...] = body[:, 0:128]
    scratch_high[...] = body[:, 128:256]
    lines = requests * rows // heads
    for h in range(heads):
        low = scratch_low[pl.ds(h, lines, stride=heads), :]
        high = scratch_high[pl.ds(h, lines, stride=heads), :]
        out[:, h * 256 : (h + 1) * 256] = jnp.concatenate([low, high], axis=1).astype(bf16)


def merge_final(packs, requests, rows, heads):
    lines = requests * rows // heads
    return pl.pallas_call(
        functools.partial(final_kernel, len(packs), requests, rows, heads),
        out_shape=jax.ShapeDtypeStruct((lines, heads * 256), bf16),
        in_specs=[pl.BlockSpec(memory_space=pltpu.VMEM)] * len(packs),
        out_specs=pl.BlockSpec(memory_space=pltpu.VMEM),
        scratch_shapes=[pltpu.VMEM((requests * rows, 128), f32)] * 2,
        name="merge_final",
    )(*packs)


def attention_kernel(
    dims,
    slots,
    patches,
    lengths,
    place,
    cosine,
    sine,
    projected,
    pool,
    pool_copy,
    mine,
    theirs,
    pool_out,
    buffer,
    query_low,
    query_high,
    queries,
    fresh,
    peak,
    norm,
    total,
    patch_buffer,
    in_sems,
    patch_sems,
):
    requests, new_count, heads, pages, page_len, window, chunk, n_seq = dims
    rows = new_count * heads
    lines = requests * new_count

    def load(c):
        span = pl.ds(c * chunk, chunk)
        return pltpu.make_async_copy(pool.at[span], buffer.at[span], in_sems.at[c])

    for c in range(pages // chunk):
        load(c).start()

    cos = cosine[...]
    sin = sine[...]

    def turned(block):
        x = projected[:, block * 128 : (block + 1) * 128].astype(f32)
        return (x * cos + pltpu.roll(x, 64, 1) * sin).astype(bf16).astype(f32)

    for h in range(heads):
        query_low[pl.ds(h, lines, stride=heads), :] = turned(2 * h)
        query_high[pl.ds(h, lines, stride=heads), :] = projected[
            :, h * 256 + 128 : h * 256 + 256
        ].astype(f32)
    fresh[:, 0:128] = turned(2 * heads).astype(bf16)
    fresh[:, 128:512] = projected[:, heads * 256 + 128 : heads * 256 + 512]

    peak[...] = jnp.full(peak.shape, floor_peak, f32)
    norm[...] = jnp.zeros(norm.shape, f32)
    total[...] = jnp.zeros(total.shape, f32)

    token_of = lax.broadcasted_iota(jnp.int32, (rows, 1), 0) // heads
    lane = lax.broadcasted_iota(jnp.int32, (1, page_len), 1)
    scale = 256.0 ** (-0.5)

    for r in range(requests):
        span = slice(r * rows, (r + 1) * rows)
        queries[r, 0:rows, :] = jnp.concatenate(
            [query_low[span, :], query_high[span, :]], axis=1
        ).astype(bf16)

    def score(r, keys):
        return lax.dot_general(queries[r, 0:rows, :], keys, contract, preferred_element_type=f32)

    def weigh(scores, visible):
        scores = jnp.where(visible, scores * scale, low_fill)
        top = jnp.maximum(jnp.max(scores, axis=1, keepdims=True), floor_peak)
        weights = jnp.exp(scores - top)
        return top, jnp.sum(weights, axis=1, keepdims=True), weights.astype(bf16)

    def mix(weights, values):
        return jnp.dot(weights, values, preferred_element_type=f32)

    def add(r, top, amount, mixed):
        span = pl.ds(pl.multiple_of(r * rows, 8), rows)
        old = peak[span, :]
        high = jnp.maximum(old, top)
        keep = jnp.exp(old - high)
        take = jnp.exp(top - high)
        peak[span, :] = high
        norm[span, :] = norm[span, :] * keep + amount * take
        total[span, :] = total[span, :] * jnp.concatenate(
            [keep, keep], axis=1
        ) + mixed * jnp.concatenate([take, take], axis=1)

    me = place[0]
    fresh_lane = lax.broadcasted_iota(jnp.int32, (1, lines), 1)
    for step in range(-(-requests // n_seq)):
        r = me + step * n_seq

        @pl.when(r < requests)
        def _():
            index = fresh_lane - r * new_count
            seen = (index >= 0) & (index <= token_of)
            top, amount, weights = weigh(score(r, fresh[:, 0:256]), seen)
            add(r, top, amount, mix(weights, fresh[:, 256:512]))

    def one_chunk(c, carry):
        load(c).wait()
        numbers = [c * chunk + k for k in range(chunk)]
        owners = [slots[0, page] for page in numbers]
        scores = [score(r, buffer[page, :, 0:256]) for r, page in zip(owners, numbers)]
        weighed = []
        for page, values in zip(numbers, scores):
            length = slots[1, page]
            start = slots[2, page] * page_len
            age = jnp.bitwise_and(length - 1 - start - lane, window - 1)
            limit = jnp.minimum(length - 1, window - 2 - token_of)
            weighed.append(weigh(values, age <= limit))
        mixed = [
            mix(weights, buffer[page, :, 256:512])
            for page, (top, amount, weights) in zip(numbers, weighed)
        ]
        for r, (top, amount, weights), values in zip(owners, weighed, mixed):
            add(r, top, amount, values)
        return carry

    lax.fori_loop(0, pages // chunk, one_chunk, 0)

    def patch_copy(i):
        row = pl.multiple_of(patches[1, i] * 16, 16)
        return pltpu.make_async_copy(
            patch_buffer.at[i],
            pool_out.at[jnp.maximum(patches[0, i], 0), pl.ds(row, 16)],
            patch_sems.at[i],
        )

    def write_patch(i, carry):
        slot = patches[0, i]

        @pl.when(slot >= 0)
        def _():
            r = i // 2
            row = pl.multiple_of(patches[1, i] * 16, 16)
            old = buffer[slot, pl.ds(row, 16), :]
            cycle = patches[2, i] * page_len + row
            line = lax.broadcasted_iota(jnp.int32, (16, lines), 0)
            token = jnp.bitwise_and(cycle + line - lengths[r], window - 1)
            column = lax.broadcasted_iota(jnp.int32, (16, lines), 1)
            pick = (token < new_count) & (column == r * new_count + token)
            new = jnp.dot(pick.astype(f32).astype(bf16), fresh[...], preferred_element_type=f32)
            row_token = jnp.bitwise_and(
                cycle + lax.broadcasted_iota(jnp.int32, (16, 1), 0) - lengths[r], window - 1
            )
            patch_buffer[i] = jnp.where(row_token < new_count, new, old.astype(f32)).astype(bf16)
            patch_copy(i).start()

        return carry

    lax.fori_loop(0, 2 * requests, write_patch, 0)

    half = requests // 2
    core = place[1]
    for side, out in ((core, mine), (1 - core, theirs)):
        logs = []
        for k in range(half):
            span = pl.ds(pl.multiple_of((side * half + k) * rows, 8), rows)
            amount = norm[span, :]
            some = amount > 0.0
            safe = jnp.where(some, amount, 1.0)
            logs.append(jnp.where(some, peak[span, :] + jnp.log(safe), low_fill))
            inverse = jnp.where(some, 1.0 / safe, 0.0)
            total[span, :] = total[span, :] * jnp.concatenate([inverse, inverse], axis=1)
        span = pl.ds(pl.multiple_of(side * half * rows, 8), half * rows)
        out[0 : half * rows, :] = total[span, :].astype(bf16)
        out[half * rows : half * rows + 16, :] = pack_logs(logs, rows).astype(bf16)

    def wait_patch(i, carry):
        @pl.when(patches[0, i] >= 0)
        def _():
            patch_copy(i).wait()

        return carry

    lax.fori_loop(0, 2 * requests, wait_patch, 0)


def attention(dims, slots, patches, lengths, place, cosine, sine, projected, pool, pool_copy):
    requests, new_count, heads, pages, page_len, window, chunk, n_seq = dims
    rows = new_count * heads
    lines = requests * new_count
    smem = pl.BlockSpec(memory_space=pltpu.SMEM)
    vmem = pl.BlockSpec(memory_space=pltpu.VMEM)
    hbm = pl.BlockSpec(memory_space=pltpu.HBM)
    return pl.pallas_call(
        functools.partial(attention_kernel, dims),
        out_shape=(
            jax.ShapeDtypeStruct((requests // 2 * rows + 16, 256), bf16),
            jax.ShapeDtypeStruct((requests // 2 * rows + 16, 256), bf16),
            pltpu.HBM(pool.shape, pool.dtype),
        ),
        in_specs=[smem, smem, smem, smem, vmem, vmem, vmem, hbm, hbm],
        out_specs=(vmem, vmem, hbm),
        scratch_shapes=[
            pltpu.VMEM(pool.shape, bf16),
            pltpu.VMEM((requests * rows, 128), f32),
            pltpu.VMEM((requests * rows, 128), f32),
            pltpu.VMEM((requests, -(-rows // 16) * 16, 256), bf16),
            pltpu.VMEM((lines, 512), bf16),
            pltpu.VMEM((requests * rows, 128), f32),
            pltpu.VMEM((requests * rows, 128), f32),
            pltpu.VMEM((requests * rows, 256), f32),
            pltpu.VMEM((2 * requests, 16, 512), bf16),
            pltpu.SemaphoreType.DMA((pages // chunk,)),
            pltpu.SemaphoreType.DMA((2 * requests,)),
        ],
        input_output_aliases={8: 2},
        compiler_params=pltpu.CompilerParams(vmem_limit_bytes=24 * 1024 * 1024),
        cost_estimate=pl.CostEstimate(
            flops=4 * pages * rows * page_len * 256,
            bytes_accessed=pool.size * 2,
            transcendentals=pages * rows * page_len,
        ),
        name="page_attention",
    )(slots, patches, lengths, place, cosine, sine, projected, pool, pool_copy)


def body(
    n_dp,
    n_seq,
    tokens,
    attn_gain,
    qkv_weight,
    out_weight,
    mlp_gain,
    gate_up,
    down_weight,
    kv_pool,
    cache_len,
    page_table,
):
    seq_index = lax.axis_index("seq")
    dp_index = lax.axis_index("dp")
    core = seq_index % 2
    chips = n_seq // 2
    requests, new_count, width = tokens.shape
    pages, page_len, pair_width = kv_pool.shape
    head_dim = pair_width // 2
    heads = out_weight.shape[1] // head_dim
    page_count = page_table.shape[1]
    window = page_count * page_len
    lines = requests * new_count
    half = lines // 2
    rows = new_count * heads

    def ordered(mine, other, axis=0):
        return jnp.where(
            core == 0,
            jnp.concatenate([mine, other], axis=axis),
            jnp.concatenate([other, mine], axis=axis),
        )

    stream = tokens.reshape(lines, width)
    partner_weight = swap(qkv_weight, "dp", n_dp, 1)
    own_normed = rms_norm(stream, attn_gain).astype(bf16)
    my_half = jnp.where(core == 0, own_normed[:half], own_normed[half:])
    far = list(range(2, n_dp, 2))
    far_halves = [swap(my_half, "dp", n_dp, k) for k in far]
    held_pool = pltpu.with_memory_space_constraint(kv_pool, pltpu.HBM)
    pool_copy = copy_pool(held_pool)
    far_half = jnp.concatenate(far_halves, axis=0)
    far_other = swap(far_half, "seq", n_seq, 1)
    groups = [own_normed]
    for i in range(len(far)):
        groups += [far_half[i * half : (i + 1) * half], far_other[i * half : (i + 1) * half]]
    partner_weight, pool_copy = lax.optimization_barrier((partner_weight, pool_copy))
    normed = jnp.concatenate(groups, axis=0)
    by_mine = lax.dot_general(normed, qkv_weight, contract, preferred_element_type=f32)
    by_partner = lax.dot_general(normed, partner_weight, contract, preferred_element_type=f32)
    products = jnp.where(
        dp_index % 2 == 0,
        jnp.concatenate([by_mine, by_partner], axis=1),
        jnp.concatenate([by_partner, by_mine], axis=1),
    ).astype(bf16)
    out_mine, far_half = lax.optimization_barrier((out_weight, far_half))
    out_blocks = {0: out_mine, 1: swap(out_mine, "dp", n_dp, 1)}
    for k in far:
        out_blocks[k] = swap(out_mine, "dp", n_dp, k)
    blocks = [products[:lines]]
    for i, k in enumerate(far):
        back = swap(products[(i + 1) * lines : (i + 2) * lines], "dp", n_dp, k)
        blocks.append(ordered(back[:half], back[half:]))
    pair = dp_index // 2
    columns = []
    for j in range(n_dp // 2):
        block = blocks[0]
        for k in range(1, n_dp // 2):
            block = jnp.where((pair ^ k) == j, blocks[k], block)
        columns.append(block)
    projected = lax.all_gather(
        jnp.concatenate(columns, axis=1), "seq", axis=1, tiled=True
    )

    positions_int = cache_len[:, None] + jnp.arange(new_count, dtype=jnp.int32)[None, :]
    quarter = head_dim // 4
    inverse = 10000.0 ** (-jnp.arange(quarter).astype(f32) / quarter)
    angles = positions_int.reshape(lines, 1).astype(f32) * inverse
    cosine = jnp.cos(angles)
    sine = jnp.sin(angles)
    cosine = jnp.concatenate([cosine, cosine], axis=1)
    sine = jnp.concatenate([-sine, sine], axis=1)
    slot_ids = seq_index * pages + jnp.arange(pages, dtype=jnp.int32)
    matches = page_table[None, :, :] == slot_ids[:, None, None]
    number = jnp.arange(page_count, dtype=jnp.int32)[None, None, :]
    owner = jnp.arange(requests, dtype=jnp.int32)[None, :, None]
    slots = jnp.stack(
        [
            jnp.sum(jnp.where(matches, owner, 0), axis=(1, 2)),
            jnp.sum(jnp.where(matches, cache_len[None, :, None], 0), axis=(1, 2)),
            jnp.sum(jnp.where(matches, number, 0), axis=(1, 2)),
        ]
    )
    ends = jnp.stack([cache_len, cache_len + (new_count - 1)], axis=1)
    end_page = (ends // page_len) % page_count
    end_block = (ends % page_len) // 16
    hit = end_page[:, :, None] == jnp.arange(page_count, dtype=jnp.int32)[None, None, :]
    end_slot = jnp.sum(jnp.where(hit, page_table[:, None, :], 0), axis=2) - seq_index * pages
    good = (end_slot >= 0) & (end_slot < pages)
    same = (end_page[:, 0] == end_page[:, 1]) & (end_block[:, 0] == end_block[:, 1])
    good = good & jnp.stack([jnp.ones_like(same), ~same], axis=1)
    patches = jnp.stack(
        [
            jnp.where(good, end_slot, -1).reshape(-1),
            end_block.reshape(-1),
            end_page.reshape(-1),
        ]
    )

    dims = (requests, new_count, heads, pages, page_len, window, min(16, pages), n_seq)
    mine, theirs, written_pool = attention(
        dims,
        slots,
        patches,
        cache_len,
        jnp.stack([seq_index, core]),
        cosine,
        sine,
        projected,
        held_pool,
        pool_copy,
    )

    side = requests // 2
    merged = merge_pair(mine, swap(theirs, "seq", n_seq, 1), side, rows)
    merged, *early = lax.optimization_barrier((merged, *[out_blocks[k] for k in [1, *far]]))
    for k, block in zip([1, *far], early):
        out_blocks[k] = block
    for k in far:
        out_blocks[k ^ 1] = swap(out_blocks[k], "dp", n_dp, 1)
    packs = [merged] + [swap(merged, "seq", n_seq, 2 * c) for c in range(1, chips)]
    packs, late = lax.optimization_barrier((packs, [out_blocks[k ^ 1] for k in far]))
    for k, block in zip(far, late):
        out_blocks[k ^ 1] = block
    attended_half = merge_final(packs, side, rows, heads)
    attended = ordered(attended_half, swap(attended_half, "seq", n_seq, 1))

    by_block = [
        lax.dot_general(attended, out_blocks[k], contract, preferred_element_type=f32).astype(bf16)
        for k in range(n_dp)
    ]
    heads_part = []
    for j in range(n_dp):
        block = by_block[0]
        for k in range(1, n_dp):
            block = jnp.where((dp_index ^ k) == j, by_block[k], block)
        heads_part.append(block)
    heads_part = jnp.concatenate(heads_part, axis=1)
    heads_out = lax.all_gather(heads_part, "seq", axis=1, tiled=True)
    residual = (stream.astype(f32) + heads_out.astype(f32)).astype(bf16)
    hidden_in = rms_norm(residual, mlp_gain).astype(bf16)
    hidden_in = lax.optimization_barrier(hidden_in)
    gate_and_up = jnp.einsum("rd,gfd->grf", hidden_in, gate_up, preferred_element_type=f32)
    hidden = (jax.nn.gelu(gate_and_up[0], approximate=True) * gate_and_up[1]).astype(bf16)
    partial_sum = jnp.dot(hidden, down_weight, preferred_element_type=f32)

    keep = jnp.where(core == 0, partial_sum[:half], partial_sum[half:])
    give = jnp.where(core == 0, partial_sum[half:], partial_sum[:half]).astype(bf16)
    chip_sum = (keep + swap(give, "seq", n_seq, 1).astype(f32)).astype(bf16)
    terms = [chip_sum] + [swap(chip_sum, "seq", n_seq, 2 * c) for c in range(1, chips)]
    full_half = tree_sum([term.astype(f32) for term in terms])
    my_residual = jnp.where(core == 0, residual[:half], residual[half:])
    out_half = (my_residual.astype(f32) + full_half).astype(bf16)
    layer_out = ordered(out_half, swap(out_half, "seq", n_seq, 1))
    return layer_out.reshape(requests, new_count, width), written_pool


def solution(mesh):
    in_specs = (
        P("dp", None, None),
        P(),
        P(("seq", "dp"), None),
        P(("seq", "dp"), None),
        P(),
        P(None, "seq", None),
        P("seq", None),
        P(("dp", "seq"), None, None),
        P("dp"),
        P("dp", None),
    )
    out_specs = (P("dp", None, None), P(("dp", "seq"), None, None))
    return jax.shard_map(
        functools.partial(body, mesh.shape["dp"], mesh.shape["seq"]),
        mesh=mesh,
        in_specs=in_specs,
        out_specs=out_specs,
        check_vma=False,
    )
```

```python
import functools

import jax
import jax.numpy as jnp
from jax import lax
from jax.experimental import pallas as pl
from jax.experimental.pallas import tpu as pltpu
from jax.sharding import PartitionSpec as P

f32 = jnp.float32
bf16 = jnp.bfloat16
low_fill = -1e30
floor_peak = -1e29
contract = (((1,), (1,)), ((), ()))


def rms_norm(values, gains):
    floats = values.astype(f32)
    return floats * lax.rsqrt(jnp.mean(floats * floats, axis=-1, keepdims=True) + 1e-06) * gains


def swap(values, axis, size, mask):
    return lax.ppermute(values, axis, [(i, i ^ mask) for i in range(size)])


def tree_sum(terms):
    while len(terms) > 1:
        terms = [terms[i] + terms[i + 1] for i in range(0, len(terms), 2)]
    return terms[0]


def write_kernel(dims, parts, patches, lengths, fresh, source, target, buffer, in_sems, out_sems):
    requests, new_count, heads, pages, page_len, window, chunk, n_seq = dims
    lines = requests * new_count
    count = pages // parts
    spans = [pl.ds(i * count, count) for i in range(parts)]
    loads = [
        pltpu.make_async_copy(source.at[span], buffer.at[span], in_sems.at[i])
        for i, span in enumerate(spans)
    ]
    stores = [
        pltpu.make_async_copy(buffer.at[span], target.at[span], out_sems.at[i])
        for i, span in enumerate(spans)
    ]
    for load in loads:
        load.start()
    for load in loads:
        load.wait()

    def write_patch(i, carry):
        slot = patches[0, i]

        @pl.when(slot >= 0)
        def _():
            r = i // 2
            row = pl.multiple_of(patches[1, i] * 16, 16)
            old = buffer[slot, pl.ds(row, 16), :]
            first = patches[2, i] * page_len + row - lengths[r]
            line = lax.broadcasted_iota(jnp.int32, (16, lines), 0)
            token = jnp.bitwise_and(first + line, window - 1)
            column = lax.broadcasted_iota(jnp.int32, (16, lines), 1)
            pick = (token < new_count) & (column == r * new_count + token)
            new = jnp.dot(pick.astype(f32).astype(bf16), fresh[...], preferred_element_type=f32)
            row_token = jnp.bitwise_and(
                first + lax.broadcasted_iota(jnp.int32, (16, 1), 0), window - 1
            )
            buffer[slot, pl.ds(row, 16), :] = jnp.where(
                row_token < new_count, new, old.astype(f32)
            ).astype(bf16)

        return carry

    lax.fori_loop(0, 2 * requests, write_patch, 0)
    for store in stores:
        store.start()
    for store in stores:
        store.wait()


def write_pool(dims, patches, lengths, fresh, kv_pool):
    parts = min(16, kv_pool.shape[0])
    smem = pl.BlockSpec(memory_space=pltpu.SMEM)
    hbm = pl.BlockSpec(memory_space=pltpu.HBM)
    return pl.pallas_call(
        functools.partial(write_kernel, dims, parts),
        out_shape=pltpu.HBM(kv_pool.shape, kv_pool.dtype),
        in_specs=[smem, smem, pl.BlockSpec(memory_space=pltpu.VMEM), hbm],
        out_specs=hbm,
        scratch_shapes=[
            pltpu.VMEM(kv_pool.shape, kv_pool.dtype),
            pltpu.SemaphoreType.DMA((parts,)),
            pltpu.SemaphoreType.DMA((parts,)),
        ],
        compiler_params=pltpu.CompilerParams(vmem_limit_bytes=12 * 1024 * 1024),
        cost_estimate=pl.CostEstimate(
            flops=0, bytes_accessed=2 * kv_pool.size * 2, transcendentals=0
        ),
        name="write_pool",
    )(patches, lengths, fresh, kv_pool)


def split_three(values):
    high = values.astype(bf16).astype(f32)
    middle = (values - high).astype(bf16).astype(f32)
    low = (values - high - middle).astype(bf16).astype(f32)
    return high, middle, low


def diagonal(rows):
    return lax.broadcasted_iota(jnp.int32, (rows, 128), 0) == lax.broadcasted_iota(
        jnp.int32, (rows, 128), 1
    )


def pack_logs(columns, rows):
    eye = diagonal(rows)
    lines = [
        jnp.sum(jnp.where(eye, jnp.broadcast_to(c, (rows, 128)), 0.0), axis=0, keepdims=True)
        for c in columns
    ]
    lines += [jnp.zeros((1, 128), f32)] * (8 - len(lines))
    high, middle, low = split_three(jnp.concatenate(lines, axis=0))
    return jnp.concatenate(
        [
            jnp.concatenate([high, middle], axis=1),
            jnp.concatenate([low, jnp.zeros((8, 128), f32)], axis=1),
        ],
        axis=0,
    )


def unpack_logs(block):
    return block[0:8, 0:128] + block[0:8, 128:256] + block[8:16, 0:128]


def merge_parts(packs, requests, rows):
    total = requests * rows
    bodies = [ref[...].astype(f32) for ref in packs]
    logs = [unpack_logs(body[total : total + 16]) for body in bodies]
    eye = diagonal(rows)
    results, columns = [], []
    for r in range(requests):
        cols = [
            jnp.sum(
                jnp.where(eye, jnp.broadcast_to(log[r : r + 1, :], (rows, 128)), 0.0),
                axis=1,
                keepdims=True,
            )
            for log in logs
        ]
        top = functools.reduce(jnp.maximum, cols)
        scales = [jnp.exp(c - top) for c in cols]
        norm = functools.reduce(jnp.add, scales)
        parts = [
            body[r * rows : (r + 1) * rows] * scale for body, scale in zip(bodies, scales)
        ]
        results.append(functools.reduce(jnp.add, parts) / norm)
        columns.append(top + jnp.log(norm))
    return results, columns


def pair_kernel(requests, rows, mine, other, out):
    results, columns = merge_parts([mine, other], requests, rows)
    body = jnp.concatenate(results + [pack_logs(columns, rows)], axis=0)
    out[...] = body.astype(bf16)


def merge_pair(mine, other, requests, rows):
    return pl.pallas_call(
        functools.partial(pair_kernel, requests, rows),
        out_shape=jax.ShapeDtypeStruct(mine.shape, bf16),
        in_specs=[pl.BlockSpec(memory_space=pltpu.VMEM)] * 2,
        out_specs=pl.BlockSpec(memory_space=pltpu.VMEM),
        compiler_params=pltpu.CompilerParams(vmem_limit_bytes=8 * 1024 * 1024),
        name="merge_pair",
    )(mine, other)


def final_kernel(count, requests, rows, heads, *refs):
    packs, out, scratch_low, scratch_high = refs[:count], refs[count + 1], refs[-2], refs[-1]
    results, unused = merge_parts(packs, requests, rows)
    body = jnp.concatenate(results, axis=0)
    scratch_low[...] = body[:, 0:128]
    scratch_high[...] = body[:, 128:256]
    lines = requests * rows // heads
    for h in range(heads):
        low = scratch_low[pl.ds(h, lines, stride=heads), :]
        high = scratch_high[pl.ds(h, lines, stride=heads), :]
        out[:, h * 256 : (h + 1) * 256] = jnp.concatenate([low, high], axis=1).astype(bf16)


def merge_final(packs, token, requests, rows, heads):
    lines = requests * rows // heads
    return pl.pallas_call(
        functools.partial(final_kernel, len(packs), requests, rows, heads),
        out_shape=jax.ShapeDtypeStruct((lines, heads * 256), bf16),
        in_specs=[pl.BlockSpec(memory_space=pltpu.VMEM)] * (len(packs) + 1),
        out_specs=pl.BlockSpec(memory_space=pltpu.VMEM),
        scratch_shapes=[pltpu.VMEM((requests * rows, 128), f32)] * 2,
        compiler_params=pltpu.CompilerParams(vmem_limit_bytes=8 * 1024 * 1024),
        name="merge_final",
    )(*packs, token)


def attention_kernel(
    dims,
    slots,
    place,
    cosine,
    sine,
    projected,
    pool,
    mine,
    theirs,
    fresh,
    buffer,
    query_low,
    query_high,
    queries,
    peak,
    norm,
    total,
    in_sems,
):
    requests, new_count, heads, pages, page_len, window, chunk, n_seq = dims
    rows = new_count * heads
    lines = requests * new_count

    def load(c):
        span = pl.ds(c * chunk, chunk)
        return pltpu.make_async_copy(pool.at[span], buffer.at[span], in_sems.at[c])

    for c in range(pages // chunk):
        load(c).start()

    cos = cosine[...]
    sin = sine[...]

    def turned(block):
        x = projected[:, block * 128 : (block + 1) * 128].astype(f32)
        return (x * cos + pltpu.roll(x, 64, 1) * sin).astype(bf16).astype(f32)

    for h in range(heads):
        query_low[pl.ds(h, lines, stride=heads), :] = turned(2 * h)
        query_high[pl.ds(h, lines, stride=heads), :] = projected[
            :, h * 256 + 128 : h * 256 + 256
        ].astype(f32)
    fresh[:, 0:128] = turned(2 * heads).astype(bf16)
    fresh[:, 128:512] = projected[:, heads * 256 + 128 : heads * 256 + 512]

    peak[...] = jnp.full(peak.shape, floor_peak, f32)
    norm[...] = jnp.zeros(norm.shape, f32)
    total[...] = jnp.zeros(total.shape, f32)

    token_of = lax.broadcasted_iota(jnp.int32, (rows, 1), 0) // heads
    lane = lax.broadcasted_iota(jnp.int32, (1, page_len), 1)
    scale = 256.0 ** (-0.5)

    for r in range(requests):
        span = slice(r * rows, (r + 1) * rows)
        queries[r, 0:rows, :] = jnp.concatenate(
            [query_low[span, :], query_high[span, :]], axis=1
        ).astype(bf16)

    def score(r, keys):
        return lax.dot_general(queries[r, 0:rows, :], keys, contract, preferred_element_type=f32)

    def weigh(scores, visible):
        scores = jnp.where(visible, scores * scale, low_fill)
        top = jnp.maximum(jnp.max(scores, axis=1, keepdims=True), floor_peak)
        weights = jnp.exp(scores - top)
        return top, jnp.sum(weights, axis=1, keepdims=True), weights.astype(bf16)

    def mix(weights, values):
        return jnp.dot(weights, values, preferred_element_type=f32)

    def add(r, top, amount, mixed):
        span = pl.ds(pl.multiple_of(r * rows, 8), rows)
        old = peak[span, :]
        high = jnp.maximum(old, top)
        keep = jnp.exp(old - high)
        take = jnp.exp(top - high)
        peak[span, :] = high
        norm[span, :] = norm[span, :] * keep + amount * take
        total[span, :] = total[span, :] * jnp.concatenate(
            [keep, keep], axis=1
        ) + mixed * jnp.concatenate([take, take], axis=1)

    me = place[0]
    fresh_lane = lax.broadcasted_iota(jnp.int32, (1, lines), 1)
    for step in range(-(-requests // n_seq)):
        r = me + step * n_seq

        @pl.when(r < requests)
        def _():
            index = fresh_lane - r * new_count
            seen = (index >= 0) & (index <= token_of)
            top, amount, weights = weigh(score(r, fresh[:, 0:256]), seen)
            add(r, top, amount, mix(weights, fresh[:, 256:512]))

    def one_chunk(c, carry):
        load(c).wait()
        numbers = [c * chunk + k for k in range(chunk)]
        owners = [slots[0, page] for page in numbers]
        scores = [score(r, buffer[page, :, 0:256]) for r, page in zip(owners, numbers)]
        weighed = []
        for page, values in zip(numbers, scores):
            length = slots[1, page]
            start = slots[2, page] * page_len
            age = jnp.bitwise_and(length - 1 - start - lane, window - 1)
            limit = jnp.minimum(length - 1, window - 2 - token_of)
            weighed.append(weigh(values, age <= limit))
        mixed = [
            mix(weights, buffer[page, :, 256:512])
            for page, (top, amount, weights) in zip(numbers, weighed)
        ]
        for r, (top, amount, weights), values in zip(owners, weighed, mixed):
            add(r, top, amount, values)
        return carry

    lax.fori_loop(0, pages // chunk, one_chunk, 0)

    half = requests // 2
    core = place[1]
    for side, out in ((core, mine), (1 - core, theirs)):
        logs = []
        for k in range(half):
            span = pl.ds(pl.multiple_of((side * half + k) * rows, 8), rows)
            amount = norm[span, :]
            some = amount > 0.0
            safe = jnp.where(some, amount, 1.0)
            logs.append(jnp.where(some, peak[span, :] + jnp.log(safe), low_fill))
            inverse = jnp.where(some, 1.0 / safe, 0.0)
            total[span, :] = total[span, :] * jnp.concatenate([inverse, inverse], axis=1)
        span = pl.ds(pl.multiple_of(side * half * rows, 8), half * rows)
        out[0 : half * rows, :] = total[span, :].astype(bf16)
        out[half * rows : half * rows + 16, :] = pack_logs(logs, rows).astype(bf16)


def attention(dims, slots, place, cosine, sine, projected, pool):
    requests, new_count, heads, pages, page_len, window, chunk, n_seq = dims
    rows = new_count * heads
    smem = pl.BlockSpec(memory_space=pltpu.SMEM)
    vmem = pl.BlockSpec(memory_space=pltpu.VMEM)
    pack = jax.ShapeDtypeStruct((requests // 2 * rows + 16, 256), bf16)
    return pl.pallas_call(
        functools.partial(attention_kernel, dims),
        out_shape=(pack, pack, jax.ShapeDtypeStruct((requests * new_count, 512), bf16)),
        in_specs=[smem, smem, vmem, vmem, vmem, pl.BlockSpec(memory_space=pltpu.HBM)],
        out_specs=(vmem, vmem, vmem),
        scratch_shapes=[
            pltpu.VMEM(pool.shape, bf16),
            pltpu.VMEM((requests * rows, 128), f32),
            pltpu.VMEM((requests * rows, 128), f32),
            pltpu.VMEM((requests, -(-rows // 16) * 16, 256), bf16),
            pltpu.VMEM((requests * rows, 128), f32),
            pltpu.VMEM((requests * rows, 128), f32),
            pltpu.VMEM((requests * rows, 256), f32),
            pltpu.SemaphoreType.DMA((pages // chunk,)),
        ],
        compiler_params=pltpu.CompilerParams(vmem_limit_bytes=20 * 1024 * 1024),
        cost_estimate=pl.CostEstimate(
            flops=4 * pages * rows * page_len * 256,
            bytes_accessed=pool.size * 2,
            transcendentals=pages * rows * page_len,
        ),
        name="page_attention",
    )(slots, place, cosine, sine, projected, pool)


def project_kernel(count, place, mine, other, *refs):
    blocks, out = refs[:count], refs[count]
    core, plane = place[1], place[2]
    low = jnp.where(core == 0, mine[...], other[...])
    high = jnp.where(core == 0, other[...], mine[...])
    attended = jnp.concatenate([low, high], axis=0)
    products = [
        lax.dot_general(attended, block[...], contract, preferred_element_type=f32)
        for block in blocks
    ]
    columns = []
    for j in range(count):
        column = products[0]
        for k in range(1, count):
            column = jnp.where((plane ^ k) == j, products[k], column)
        columns.append(column)
    out[...] = jnp.concatenate(columns, axis=1).astype(bf16)


def project_out(place, mine, other, blocks):
    vmem = pl.BlockSpec(memory_space=pltpu.VMEM)
    shape = (2 * mine.shape[0], len(blocks) * blocks[0].shape[0])
    return pl.pallas_call(
        functools.partial(project_kernel, len(blocks)),
        out_shape=jax.ShapeDtypeStruct(shape, bf16),
        in_specs=[pl.BlockSpec(memory_space=pltpu.SMEM)] + [vmem] * (2 + len(blocks)),
        out_specs=vmem,
        compiler_params=pltpu.CompilerParams(vmem_limit_bytes=8 * 1024 * 1024),
        name="project_out",
    )(place, mine, other, *blocks)


def fetch_kernel(parts, gate_up, down, after, gates, downs, token, sems):
    units = down.shape[0]
    size = units // parts
    copies = []
    for i in range(parts):
        span = pl.ds(i * size, size)
        copies.append(pltpu.make_async_copy(gate_up.at[0, span], gates.at[0, span], sems.at[0, i]))
        copies.append(pltpu.make_async_copy(gate_up.at[1, span], gates.at[1, span], sems.at[1, i]))
        copies.append(pltpu.make_async_copy(down.at[span], downs.at[span], sems.at[2, i]))
    for copy in copies:
        copy.start()
    token[...] = jnp.zeros(token.shape, f32)
    for copy in copies:
        copy.wait()


def fetch_weights(gate_up, down, after):
    parts = max(c for c in (1, 2, 3, 4) if down.shape[0] % (16 * c) == 0)
    hbm = pl.BlockSpec(memory_space=pltpu.HBM)
    anywhere = pl.BlockSpec(memory_space=pl.ANY)
    return pl.pallas_call(
        functools.partial(fetch_kernel, parts),
        out_shape=(
            jax.ShapeDtypeStruct(gate_up.shape, bf16),
            jax.ShapeDtypeStruct(down.shape, bf16),
            jax.ShapeDtypeStruct((8, 128), f32),
        ),
        in_specs=[hbm, hbm, anywhere],
        out_specs=(anywhere, anywhere, pl.BlockSpec(memory_space=pltpu.VMEM)),
        scratch_shapes=[pltpu.SemaphoreType.DMA((3, parts))],
        compiler_params=pltpu.CompilerParams(vmem_limit_bytes=2 * 1024 * 1024),
        cost_estimate=pl.CostEstimate(
            flops=0, bytes_accessed=2 * (gate_up.size + down.size), transcendentals=0
        ),
        name="fetch_weights",
    )(
        pltpu.with_memory_space_constraint(gate_up, pltpu.HBM),
        pltpu.with_memory_space_constraint(down, pltpu.HBM),
        after,
    )


def mlp_kernel(
    chunk, place, stream, heads_out, gain, gates, downs, keep, give, kept_residual, residual, total
):
    units, width = downs.shape
    count = units // chunk
    gathered = jnp.concatenate(
        [heads_out[i].astype(f32) for i in range(heads_out.shape[0])], axis=1
    )
    summed = stream[...].astype(f32) + gathered
    residual[...] = summed.astype(bf16).astype(f32)
    floats = residual[...]
    spread = lax.rsqrt(jnp.mean(floats * floats, axis=-1, keepdims=True) + 1e-06)
    inputs = (floats * spread * gain[...]).astype(bf16)
    root = (2.0 / 3.141592653589793) ** 0.5

    def rise(c):
        span = slice(c * chunk, (c + 1) * chunk)
        gate = lax.dot_general(inputs, gates[0, span, :], contract, preferred_element_type=f32)
        up = lax.dot_general(inputs, gates[1, span, :], contract, preferred_element_type=f32)
        inner = root * (gate + 0.044715 * (gate * gate * gate))
        return (0.5 * gate * (1.0 + jnp.tanh(inner)) * up).astype(bf16)

    def fall(c, hidden):
        span = slice(c * chunk, (c + 1) * chunk)
        product = jnp.dot(hidden, downs[span, :], preferred_element_type=f32)
        if c == 0:
            total[...] = product
        else:
            total[...] += product

    before = rise(0)
    for c in range(1, count):
        after = rise(c)
        fall(c - 1, before)
        before = after
    fall(count - 1, before)
    half = total.shape[0] // 2
    core = place[1]
    mine = pl.ds(pl.multiple_of(core * half, 8), half)
    keep[...] = total[mine, :]
    kept_residual[...] = residual[mine, :].astype(bf16)
    give[...] = total[pl.ds(pl.multiple_of((1 - core) * half, 8), half), :].astype(bf16)


def feed_forward(place, stream, heads_out, gain, gates, downs):
    lines, width = stream.shape
    units = downs.shape[0]
    chunk = max(c for c in range(16, 256, 16) if units % c == 0)
    vmem = pl.BlockSpec(memory_space=pltpu.VMEM)
    return pl.pallas_call(
        functools.partial(mlp_kernel, chunk),
        out_shape=(
            jax.ShapeDtypeStruct((lines // 2, width), f32),
            jax.ShapeDtypeStruct((lines // 2, width), bf16),
            jax.ShapeDtypeStruct((lines // 2, width), bf16),
        ),
        in_specs=[pl.BlockSpec(memory_space=pltpu.SMEM)] + [vmem] * 5,
        out_specs=(vmem, vmem, vmem),
        scratch_shapes=[pltpu.VMEM((lines, width), f32), pltpu.VMEM((lines, width), f32)],
        compiler_params=pltpu.CompilerParams(vmem_limit_bytes=12 * 1024 * 1024),
        name="feed_forward",
    )(place, stream, heads_out, gain.reshape(1, width), gates, downs)


def body(
    n_dp,
    n_seq,
    tokens,
    attn_gain,
    qkv_weight,
    out_weight,
    mlp_gain,
    gate_up,
    down_weight,
    kv_pool,
    cache_len,
    page_table,
):
    seq_index = lax.axis_index("seq")
    dp_index = lax.axis_index("dp")
    core = seq_index % 2
    chips = n_seq // 2
    requests, new_count, width = tokens.shape
    pages, page_len, pair_width = kv_pool.shape
    head_dim = pair_width // 2
    heads = out_weight.shape[1] // head_dim
    page_count = page_table.shape[1]
    window = page_count * page_len
    lines = requests * new_count
    half = lines // 2
    rows = new_count * heads

    def ordered(mine, other, axis=0):
        return jnp.where(
            core == 0,
            jnp.concatenate([mine, other], axis=axis),
            jnp.concatenate([other, mine], axis=axis),
        )

    stream = tokens.reshape(lines, width)
    partner_weight = swap(qkv_weight, "dp", n_dp, 1)
    far = list(range(2, n_dp, 2))
    quarter_lines = lines // 4
    quarter_index = seq_index % 4
    my_quarter = lax.dynamic_slice_in_dim(stream, quarter_index * quarter_lines, quarter_lines)
    far_parts = jnp.concatenate([swap(my_quarter, "dp", n_dp, k) for k in far], axis=0)
    far_pairs = [far_parts, swap(far_parts, "seq", n_seq, 2)]
    far_mine = jnp.concatenate(far_pairs, axis=0)
    far_other = swap(far_mine, "seq", n_seq, 1)
    held_pool = pltpu.with_memory_space_constraint(kv_pool, pltpu.HBM)
    groups = [stream]
    stride = len(far) * quarter_lines
    for i in range(len(far)):
        for source in (far_mine, far_other):
            for start in (i * quarter_lines, stride + i * quarter_lines):
                groups.append(source[start : start + quarter_lines])
    normed = rms_norm(jnp.concatenate(groups, axis=0), attn_gain).astype(bf16)
    by_mine = lax.dot_general(normed, qkv_weight, contract, preferred_element_type=f32)
    by_partner = lax.dot_general(normed, partner_weight, contract, preferred_element_type=f32)
    products = jnp.where(
        dp_index % 2 == 0,
        jnp.concatenate([by_mine, by_partner], axis=1),
        jnp.concatenate([by_partner, by_mine], axis=1),
    ).astype(bf16)
    blocks = [products[:lines]]
    for i, k in enumerate(far):
        back = swap(products[(i + 1) * lines : (i + 2) * lines], "dp", n_dp, k)
        pieces = {
            m: back[n * quarter_lines : (n + 1) * quarter_lines] for n, m in enumerate((0, 2, 1, 3))
        }
        natural = []
        for j in range(4):
            piece = pieces[0]
            for m in (1, 2, 3):
                piece = jnp.where((quarter_index ^ m) == j, pieces[m], piece)
            natural.append(piece)
        blocks.append(jnp.concatenate(natural, axis=0))
    out_mine, blocks = lax.optimization_barrier((out_weight, blocks))
    out_blocks = {0: out_mine, 1: swap(out_mine, "dp", n_dp, 1)}
    for k in far:
        out_blocks[k] = swap(out_mine, "dp", n_dp, k)
    pair = dp_index // 2
    columns = []
    for j in range(n_dp // 2):
        block = blocks[0]
        for k in range(1, n_dp // 2):
            block = jnp.where((pair ^ k) == j, blocks[k], block)
        columns.append(block)
    projected = lax.all_gather(
        jnp.concatenate(columns, axis=1), "seq", axis=1, tiled=True
    )

    positions_int = cache_len[:, None] + jnp.arange(new_count, dtype=jnp.int32)[None, :]
    quarter = head_dim // 4
    inverse = 10000.0 ** (-jnp.arange(quarter).astype(f32) / quarter)
    angles = positions_int.reshape(lines, 1).astype(f32) * inverse
    cosine = jnp.cos(angles)
    sine = jnp.sin(angles)
    cosine = jnp.concatenate([cosine, cosine], axis=1)
    sine = jnp.concatenate([-sine, sine], axis=1)
    slot_ids = seq_index * pages + jnp.arange(pages, dtype=jnp.int32)
    matches = page_table[None, :, :] == slot_ids[:, None, None]
    number = jnp.arange(page_count, dtype=jnp.int32)[None, None, :]
    owner = jnp.arange(requests, dtype=jnp.int32)[None, :, None]
    slots = jnp.stack(
        [
            jnp.sum(jnp.where(matches, owner, 0), axis=(1, 2)),
            jnp.sum(jnp.where(matches, cache_len[None, :, None], 0), axis=(1, 2)),
            jnp.sum(jnp.where(matches, number, 0), axis=(1, 2)),
        ]
    )
    ends = jnp.stack([cache_len, cache_len + (new_count - 1)], axis=1)
    end_page = (ends // page_len) % page_count
    end_block = (ends % page_len) // 16
    hit = end_page[:, :, None] == jnp.arange(page_count, dtype=jnp.int32)[None, None, :]
    end_slot = jnp.sum(jnp.where(hit, page_table[:, None, :], 0), axis=2) - seq_index * pages
    good = (end_slot >= 0) & (end_slot < pages)
    same = (end_page[:, 0] == end_page[:, 1]) & (end_block[:, 0] == end_block[:, 1])
    good = good & jnp.stack([jnp.ones_like(same), ~same], axis=1)
    patches = jnp.stack(
        [
            jnp.where(good, end_slot, -1).reshape(-1),
            end_block.reshape(-1),
            end_page.reshape(-1),
        ]
    )

    dims = (requests, new_count, heads, pages, page_len, window, min(16, pages), n_seq)
    place, slots, patches, lengths = lax.optimization_barrier(
        (jnp.stack([seq_index, core, dp_index]), slots, patches, cache_len)
    )
    mine, theirs, fresh = attention(dims, slots, place, cosine, sine, projected, held_pool)
    written_pool = write_pool(dims, patches, lengths, fresh, held_pool)

    side = requests // 2
    merged = merge_pair(mine, swap(theirs, "seq", n_seq, 1), side, rows)
    merged, *early = lax.optimization_barrier((merged, *[out_blocks[k] for k in [1, *far]]))
    for k, block in zip([1, *far], early):
        out_blocks[k] = block
    for k in far:
        out_blocks[k ^ 1] = swap(out_blocks[k], "dp", n_dp, 1)
    packs = [merged] + [swap(merged, "seq", n_seq, 2 * c) for c in range(1, chips)]
    gates, downs, token = fetch_weights(gate_up, down_weight, merged)
    packs, late = lax.optimization_barrier((packs, [out_blocks[k ^ 1] for k in far]))
    for k, block in zip(far, late):
        out_blocks[k ^ 1] = block
    attended_half = merge_final(packs, token, side, rows, heads)
    heads_part = project_out(
        place,
        attended_half,
        swap(attended_half, "seq", n_seq, 1),
        [out_blocks[k] for k in range(n_dp)],
    )
    heads_out = lax.all_gather(heads_part, "seq", axis=0)
    keep, give, my_residual = feed_forward(
        place, stream, heads_out, mlp_gain, gates, downs
    )
    chip_sum = (keep + swap(give, "seq", n_seq, 1).astype(f32)).astype(bf16)
    terms = [chip_sum] + [swap(chip_sum, "seq", n_seq, 2 * c) for c in range(1, chips)]
    terms, written_pool = lax.optimization_barrier((terms, written_pool))
    full_half = tree_sum([term.astype(f32) for term in terms])
    out_half = (my_residual.astype(f32) + full_half).astype(bf16)
    layer_out = ordered(out_half, swap(out_half, "seq", n_seq, 1))
    return layer_out.reshape(requests, new_count, width), written_pool


def solution(mesh):
    in_specs = (
        P("dp", None, None),
        P(),
        P(("seq", "dp"), None),
        P(("seq", "dp"), None),
        P(),
        P(None, "seq", None),
        P("seq", None),
        P(("dp", "seq"), None, None),
        P("dp"),
        P("dp", None),
    )
    out_specs = (P("dp", None, None), P(("dp", "seq"), None, None))
    return jax.shard_map(
        functools.partial(body, mesh.shape["dp"], mesh.shape["seq"]),
        mesh=mesh,
        in_specs=in_specs,
        out_specs=out_specs,
        check_vma=False,
    )
```

```python
import functools

import jax
import jax.numpy as jnp
from jax import lax
from jax.experimental import pallas as pl
from jax.experimental.pallas import tpu as pltpu
from jax.sharding import PartitionSpec as P

f32 = jnp.float32
bf16 = jnp.bfloat16
low_fill = -1e30
floor_peak = -1e29
contract = (((1,), (1,)), ((), ()))


def rms_norm(values, gains):
    floats = values.astype(f32)
    return floats * lax.rsqrt(jnp.mean(floats * floats, axis=-1, keepdims=True) + 1e-06) * gains


def swap(values, axis, size, mask):
    return lax.ppermute(values, axis, [(i, i ^ mask) for i in range(size)])


def tree_sum(terms):
    while len(terms) > 1:
        terms = [terms[i] + terms[i + 1] for i in range(0, len(terms), 2)]
    return terms[0]


def gather_pieces(values, n_seq):
    if n_seq > 8:
        return [lax.all_gather(values, "seq", axis=0)]
    pieces = {0: values}
    for mask in range(2, n_seq, 2):
        pieces[mask] = swap(values, "seq", n_seq, mask)
    for mask in range(0, n_seq, 2):
        pieces[mask + 1] = swap(pieces[mask], "seq", n_seq, 1)
    return [pieces[mask] for mask in range(n_seq)]


def place_pieces(me, refs, scratch):
    if len(refs) == 1:
        return refs[0]
    for mask, ref in enumerate(refs):
        scratch[jnp.bitwise_xor(me, mask)] = ref[...]
    return scratch


def write_kernel(dims, parts, patches, lengths, fresh, source, target, buffer, in_sems, out_sems):
    requests, new_count, heads, pages, page_len, window, chunk, n_seq = dims
    lines = requests * new_count
    count = pages // parts
    spans = [pl.ds(i * count, count) for i in range(parts)]
    loads = [
        pltpu.make_async_copy(source.at[span], buffer.at[span], in_sems.at[i])
        for i, span in enumerate(spans)
    ]
    stores = [
        pltpu.make_async_copy(buffer.at[span], target.at[span], out_sems.at[i])
        for i, span in enumerate(spans)
    ]
    for load in loads:
        load.start()
    for load in loads:
        load.wait()

    def write_patch(i, carry):
        slot = patches[0, i]

        @pl.when(slot >= 0)
        def _():
            r = i // 2
            row = pl.multiple_of(patches[1, i] * 16, 16)
            old = buffer[slot, pl.ds(row, 16), :]
            first = patches[2, i] * page_len + row - lengths[r]
            line = lax.broadcasted_iota(jnp.int32, (16, lines), 0)
            token = jnp.bitwise_and(first + line, window - 1)
            column = lax.broadcasted_iota(jnp.int32, (16, lines), 1)
            pick = (token < new_count) & (column == r * new_count + token)
            new = jnp.dot(pick.astype(f32).astype(bf16), fresh[...], preferred_element_type=f32)
            row_token = jnp.bitwise_and(
                first + lax.broadcasted_iota(jnp.int32, (16, 1), 0), window - 1
            )
            buffer[slot, pl.ds(row, 16), :] = jnp.where(
                row_token < new_count, new, old.astype(f32)
            ).astype(bf16)

        return carry

    lax.fori_loop(0, 2 * requests, write_patch, 0)
    for store in stores:
        store.start()
    for store in stores:
        store.wait()


def write_pool(dims, patches, lengths, fresh, kv_pool):
    parts = min(16, kv_pool.shape[0])
    smem = pl.BlockSpec(memory_space=pltpu.SMEM)
    hbm = pl.BlockSpec(memory_space=pltpu.HBM)
    return pl.pallas_call(
        functools.partial(write_kernel, dims, parts),
        out_shape=pltpu.HBM(kv_pool.shape, kv_pool.dtype),
        in_specs=[smem, smem, pl.BlockSpec(memory_space=pltpu.VMEM), hbm],
        out_specs=hbm,
        scratch_shapes=[
            pltpu.VMEM(kv_pool.shape, kv_pool.dtype),
            pltpu.SemaphoreType.DMA((parts,)),
            pltpu.SemaphoreType.DMA((parts,)),
        ],
        compiler_params=pltpu.CompilerParams(vmem_limit_bytes=12 * 1024 * 1024),
        cost_estimate=pl.CostEstimate(
            flops=0, bytes_accessed=2 * kv_pool.size * 2, transcendentals=0
        ),
        name="write_pool",
    )(patches, lengths, fresh, kv_pool)


def split_three(values):
    high = values.astype(bf16).astype(f32)
    middle = (values - high).astype(bf16).astype(f32)
    low = (values - high - middle).astype(bf16).astype(f32)
    return high, middle, low


def diagonal(rows):
    return lax.broadcasted_iota(jnp.int32, (rows, 128), 0) == lax.broadcasted_iota(
        jnp.int32, (rows, 128), 1
    )


def pack_logs(columns, rows):
    eye = diagonal(rows)
    lines = [
        jnp.sum(jnp.where(eye, jnp.broadcast_to(c, (rows, 128)), 0.0), axis=0, keepdims=True)
        for c in columns
    ]
    lines += [jnp.zeros((1, 128), f32)] * (8 - len(lines))
    high, middle, low = split_three(jnp.concatenate(lines, axis=0))
    return jnp.concatenate(
        [
            jnp.concatenate([high, middle], axis=1),
            jnp.concatenate([low, jnp.zeros((8, 128), f32)], axis=1),
        ],
        axis=0,
    )


def unpack_logs(block):
    return block[0:8, 0:128] + block[0:8, 128:256] + block[8:16, 0:128]


def merge_parts(packs, requests, rows):
    total = requests * rows
    bodies = [ref[...].astype(f32) for ref in packs]
    logs = [unpack_logs(body[total : total + 16]) for body in bodies]
    eye = diagonal(rows)
    results, columns = [], []
    for r in range(requests):
        cols = [
            jnp.sum(
                jnp.where(eye, jnp.broadcast_to(log[r : r + 1, :], (rows, 128)), 0.0),
                axis=1,
                keepdims=True,
            )
            for log in logs
        ]
        top = functools.reduce(jnp.maximum, cols)
        scales = [jnp.exp(c - top) for c in cols]
        norm = functools.reduce(jnp.add, scales)
        parts = [
            body[r * rows : (r + 1) * rows] * scale for body, scale in zip(bodies, scales)
        ]
        results.append(functools.reduce(jnp.add, parts) / norm)
        columns.append(top + jnp.log(norm))
    return results, columns


def pair_kernel(requests, rows, mine, other, out):
    results, columns = merge_parts([mine, other], requests, rows)
    body = jnp.concatenate(results + [pack_logs(columns, rows)], axis=0)
    out[...] = body.astype(bf16)


def merge_pair(mine, other, requests, rows):
    return pl.pallas_call(
        functools.partial(pair_kernel, requests, rows),
        out_shape=jax.ShapeDtypeStruct(mine.shape, bf16),
        in_specs=[pl.BlockSpec(memory_space=pltpu.VMEM)] * 2,
        out_specs=pl.BlockSpec(memory_space=pltpu.VMEM),
        compiler_params=pltpu.CompilerParams(vmem_limit_bytes=8 * 1024 * 1024),
        name="merge_pair",
    )(mine, other)


def final_kernel(count, requests, rows, heads, *refs):
    packs, out, scratch_low, scratch_high = refs[:count], refs[count + 1], refs[-2], refs[-1]
    results, unused = merge_parts(packs, requests, rows)
    body = jnp.concatenate(results, axis=0)
    scratch_low[...] = body[:, 0:128]
    scratch_high[...] = body[:, 128:256]
    lines = requests * rows // heads
    for h in range(heads):
        low = scratch_low[pl.ds(h, lines, stride=heads), :]
        high = scratch_high[pl.ds(h, lines, stride=heads), :]
        out[:, h * 256 : (h + 1) * 256] = jnp.concatenate([low, high], axis=1).astype(bf16)


def merge_final(packs, token, requests, rows, heads):
    lines = requests * rows // heads
    return pl.pallas_call(
        functools.partial(final_kernel, len(packs), requests, rows, heads),
        out_shape=jax.ShapeDtypeStruct((lines, heads * 256), bf16),
        in_specs=[pl.BlockSpec(memory_space=pltpu.VMEM)] * (len(packs) + 1),
        out_specs=pl.BlockSpec(memory_space=pltpu.VMEM),
        scratch_shapes=[pltpu.VMEM((requests * rows, 128), f32)] * 2,
        compiler_params=pltpu.CompilerParams(vmem_limit_bytes=8 * 1024 * 1024),
        name="merge_final",
    )(*packs, token)


def attention_kernel(dims, count, slots, place, cosine, sine, *refs):
    requests, new_count, heads, pages, page_len, window, chunk, n_seq = dims
    pieces, refs = refs[:count], refs[count:]
    pool, mine, theirs, fresh, buffer, gathered, projected = refs[:7]
    query_low, query_high, queries, peak, norm, total, in_sems = refs[7:]
    rows = new_count * heads
    lines = requests * new_count

    def load(c):
        span = pl.ds(c * chunk, chunk)
        return pltpu.make_async_copy(pool.at[span], buffer.at[span], in_sems.at[c])

    for c in range(pages // chunk):
        load(c).start()

    ordered_pieces = place_pieces(place[0], pieces, gathered)
    part_columns = projected.shape[1] // n_seq
    for i in range(n_seq):
        projected[:, i * part_columns : (i + 1) * part_columns] = ordered_pieces[i]
    cos = cosine[...]
    sin = sine[...]

    def turned(block):
        x = projected[:, block * 128 : (block + 1) * 128].astype(f32)
        return (x * cos + pltpu.roll(x, 64, 1) * sin).astype(bf16).astype(f32)

    for h in range(heads):
        query_low[pl.ds(h, lines, stride=heads), :] = turned(2 * h)
        query_high[pl.ds(h, lines, stride=heads), :] = projected[
            :, h * 256 + 128 : h * 256 + 256
        ].astype(f32)
    fresh[:, 0:128] = turned(2 * heads).astype(bf16)
    fresh[:, 128:512] = projected[:, heads * 256 + 128 : heads * 256 + 512]

    peak[...] = jnp.full(peak.shape, floor_peak, f32)
    norm[...] = jnp.zeros(norm.shape, f32)
    total[...] = jnp.zeros(total.shape, f32)

    token_of = lax.broadcasted_iota(jnp.int32, (rows, 1), 0) // heads
    lane = lax.broadcasted_iota(jnp.int32, (1, page_len), 1)
    scale = 256.0 ** (-0.5)

    for r in range(requests):
        span = slice(r * rows, (r + 1) * rows)
        queries[r, 0:rows, :] = jnp.concatenate(
            [query_low[span, :], query_high[span, :]], axis=1
        ).astype(bf16)

    def score(r, keys):
        return lax.dot_general(queries[r, 0:rows, :], keys, contract, preferred_element_type=f32)

    def weigh(scores, visible):
        scores = jnp.where(visible, scores * scale, low_fill)
        top = jnp.maximum(jnp.max(scores, axis=1, keepdims=True), floor_peak)
        weights = jnp.exp(scores - top)
        return top, jnp.sum(weights, axis=1, keepdims=True), weights.astype(bf16)

    def mix(weights, values):
        return jnp.dot(weights, values, preferred_element_type=f32)

    def add(r, top, amount, mixed):
        span = pl.ds(pl.multiple_of(r * rows, 8), rows)
        old = peak[span, :]
        high = jnp.maximum(old, top)
        keep = jnp.exp(old - high)
        take = jnp.exp(top - high)
        peak[span, :] = high
        norm[span, :] = norm[span, :] * keep + amount * take
        total[span, :] = total[span, :] * jnp.concatenate(
            [keep, keep], axis=1
        ) + mixed * jnp.concatenate([take, take], axis=1)

    me = place[0]
    fresh_lane = lax.broadcasted_iota(jnp.int32, (1, lines), 1)
    for step in range(-(-requests // n_seq)):
        r = me + step * n_seq

        @pl.when(r < requests)
        def _():
            index = fresh_lane - r * new_count
            seen = (index >= 0) & (index <= token_of)
            top, amount, weights = weigh(score(r, fresh[:, 0:256]), seen)
            add(r, top, amount, mix(weights, fresh[:, 256:512]))

    def chunk_scores(c):
        load(c).wait()
        numbers = range(c * chunk, (c + 1) * chunk)
        return [score(slots[0, page], buffer[page, :, 0:256]) for page in numbers]

    ahead = chunk_scores(0)
    for c in range(pages // chunk):
        scores = ahead
        if (c + 1) * chunk < pages:
            ahead = chunk_scores(c + 1)
        numbers = range(c * chunk, (c + 1) * chunk)
        weighed = []
        for page, values in zip(numbers, scores):
            length = slots[1, page]
            start = slots[2, page] * page_len
            age = jnp.bitwise_and(length - 1 - start - lane, window - 1)
            limit = jnp.minimum(length - 1, window - 2 - token_of)
            weighed.append(weigh(values, age <= limit))
        mixed = [
            mix(weights, buffer[page, :, 256:512])
            for page, (top, amount, weights) in zip(numbers, weighed)
        ]
        for page, (top, amount, weights), values in zip(numbers, weighed, mixed):
            add(slots[0, page], top, amount, values)

    half = requests // 2
    core = place[1]
    for side, out in ((core, mine), (1 - core, theirs)):
        logs = []
        for k in range(half):
            span = pl.ds(pl.multiple_of((side * half + k) * rows, 8), rows)
            amount = norm[span, :]
            some = amount > 0.0
            safe = jnp.where(some, amount, 1.0)
            logs.append(jnp.where(some, peak[span, :] + jnp.log(safe), low_fill))
            inverse = jnp.where(some, 1.0 / safe, 0.0)
            total[span, :] = total[span, :] * jnp.concatenate([inverse, inverse], axis=1)
        span = pl.ds(pl.multiple_of(side * half * rows, 8), half * rows)
        out[0 : half * rows, :] = total[span, :].astype(bf16)
        out[half * rows : half * rows + 16, :] = pack_logs(logs, rows).astype(bf16)


def attention(dims, slots, place, cosine, sine, pieces, pool):
    requests, new_count, heads, pages, page_len, window, chunk, n_seq = dims
    part_columns = pieces[0].shape[-1]
    lines = requests * new_count
    rows = new_count * heads
    smem = pl.BlockSpec(memory_space=pltpu.SMEM)
    vmem = pl.BlockSpec(memory_space=pltpu.VMEM)
    pack = jax.ShapeDtypeStruct((requests // 2 * rows + 16, 256), bf16)
    return pl.pallas_call(
        functools.partial(attention_kernel, dims, len(pieces)),
        out_shape=(pack, pack, jax.ShapeDtypeStruct((requests * new_count, 512), bf16)),
        in_specs=[smem, smem, vmem, vmem]
        + [vmem] * len(pieces)
        + [pl.BlockSpec(memory_space=pltpu.HBM)],
        out_specs=(vmem, vmem, vmem),
        scratch_shapes=[
            pltpu.VMEM(pool.shape, bf16),
            pltpu.VMEM((n_seq, lines, part_columns), bf16),
            pltpu.VMEM((lines, n_seq * part_columns), bf16),
            pltpu.VMEM((requests * rows, 128), f32),
            pltpu.VMEM((requests * rows, 128), f32),
            pltpu.VMEM((requests, -(-rows // 16) * 16, 256), bf16),
            pltpu.VMEM((requests * rows, 128), f32),
            pltpu.VMEM((requests * rows, 128), f32),
            pltpu.VMEM((requests * rows, 256), f32),
            pltpu.SemaphoreType.DMA((pages // chunk,)),
        ],
        compiler_params=pltpu.CompilerParams(vmem_limit_bytes=20 * 1024 * 1024),
        cost_estimate=pl.CostEstimate(flops=0, bytes_accessed=1024, transcendentals=0),
        name="page_attention",
    )(slots, place, cosine, sine, *pieces, pool)


def project_kernel(count, place, mine, other, *refs):
    blocks, out = refs[:count], refs[count]
    core, plane = place[1], place[2]
    low = jnp.where(core == 0, mine[...], other[...])
    high = jnp.where(core == 0, other[...], mine[...])
    attended = jnp.concatenate([low, high], axis=0)
    products = [
        lax.dot_general(attended, block[...], contract, preferred_element_type=f32)
        for block in blocks
    ]
    columns = []
    for j in range(count):
        column = products[0]
        for k in range(1, count):
            column = jnp.where((plane ^ k) == j, products[k], column)
        columns.append(column)
    out[...] = jnp.concatenate(columns, axis=1).astype(bf16)


def project_out(place, mine, other, blocks):
    vmem = pl.BlockSpec(memory_space=pltpu.VMEM)
    shape = (2 * mine.shape[0], len(blocks) * blocks[0].shape[0])
    return pl.pallas_call(
        functools.partial(project_kernel, len(blocks)),
        out_shape=jax.ShapeDtypeStruct(shape, bf16),
        in_specs=[pl.BlockSpec(memory_space=pltpu.SMEM)] + [vmem] * (2 + len(blocks)),
        out_specs=vmem,
        compiler_params=pltpu.CompilerParams(vmem_limit_bytes=8 * 1024 * 1024),
        name="project_out",
    )(place, mine, other, *blocks)


def fetch_kernel(parts, gate_up, down, after, gates, downs, token, sems):
    units = down.shape[0]
    size = units // parts
    copies = []
    for i in range(parts):
        span = pl.ds(i * size, size)
        copies.append(pltpu.make_async_copy(gate_up.at[0, span], gates.at[0, span], sems.at[0, i]))
        copies.append(pltpu.make_async_copy(gate_up.at[1, span], gates.at[1, span], sems.at[1, i]))
        copies.append(pltpu.make_async_copy(down.at[span], downs.at[span], sems.at[2, i]))
    for copy in copies:
        copy.start()
    token[...] = jnp.zeros(token.shape, f32)
    for copy in copies:
        copy.wait()


def fetch_weights(gate_up, down, after):
    parts = max(c for c in (1, 2, 3, 4) if down.shape[0] % (16 * c) == 0)
    hbm = pl.BlockSpec(memory_space=pltpu.HBM)
    anywhere = pl.BlockSpec(memory_space=pl.ANY)
    return pl.pallas_call(
        functools.partial(fetch_kernel, parts),
        out_shape=(
            jax.ShapeDtypeStruct(gate_up.shape, bf16),
            jax.ShapeDtypeStruct(down.shape, bf16),
            jax.ShapeDtypeStruct((8, 128), f32),
        ),
        in_specs=[hbm, hbm, anywhere],
        out_specs=(anywhere, anywhere, pl.BlockSpec(memory_space=pltpu.VMEM)),
        scratch_shapes=[pltpu.SemaphoreType.DMA((3, parts))],
        compiler_params=pltpu.CompilerParams(vmem_limit_bytes=2 * 1024 * 1024),
        cost_estimate=pl.CostEstimate(
            flops=0, bytes_accessed=2 * (gate_up.size + down.size), transcendentals=0
        ),
        name="fetch_weights",
    )(
        pltpu.with_memory_space_constraint(gate_up, pltpu.HBM),
        pltpu.with_memory_space_constraint(down, pltpu.HBM),
        after,
    )


def mlp_kernel(chunk, pieces, place, stream, gain, gates, downs, *refs):
    heads_out, refs = refs[:pieces], refs[pieces:]
    keep, give, kept_residual, residual, total, heads_scratch = refs
    units, width = downs.shape
    heads_out = place_pieces(place[0], heads_out, heads_scratch)
    count = units // chunk
    gathered = jnp.concatenate(
        [heads_out[i].astype(f32) for i in range(heads_out.shape[0])], axis=1
    )
    summed = stream[...].astype(f32) + gathered
    residual[...] = summed.astype(bf16).astype(f32)
    floats = residual[...]
    spread = lax.rsqrt(jnp.mean(floats * floats, axis=-1, keepdims=True) + 1e-06)
    inputs = (floats * spread * gain[...]).astype(bf16)
    root = (2.0 / 3.141592653589793) ** 0.5

    def rise(c):
        span = slice(c * chunk, (c + 1) * chunk)
        gate = lax.dot_general(inputs, gates[0, span, :], contract, preferred_element_type=f32)
        up = lax.dot_general(inputs, gates[1, span, :], contract, preferred_element_type=f32)
        inner = root * (gate + 0.044715 * (gate * gate * gate))
        return (0.5 * gate * (1.0 + jnp.tanh(inner)) * up).astype(bf16)

    def fall(c, hidden):
        span = slice(c * chunk, (c + 1) * chunk)
        product = jnp.dot(hidden, downs[span, :], preferred_element_type=f32)
        if c == 0:
            total[...] = product
        else:
            total[...] += product

    before = rise(0)
    for c in range(1, count):
        after = rise(c)
        fall(c - 1, before)
        before = after
    fall(count - 1, before)
    half = total.shape[0] // 2
    core = place[1]
    mine = pl.ds(pl.multiple_of(core * half, 8), half)
    keep[...] = total[mine, :]
    kept_residual[...] = residual[mine, :].astype(bf16)
    give[...] = total[pl.ds(pl.multiple_of((1 - core) * half, 8), half), :].astype(bf16)


def feed_forward(n_seq, place, stream, heads_out, gain, gates, downs):
    lines, width = stream.shape
    units = downs.shape[0]
    chunk = max(c for c in range(16, 256, 16) if units % c == 0)
    vmem = pl.BlockSpec(memory_space=pltpu.VMEM)
    return pl.pallas_call(
        functools.partial(mlp_kernel, chunk, len(heads_out)),
        out_shape=(
            jax.ShapeDtypeStruct((lines // 2, width), f32),
            jax.ShapeDtypeStruct((lines // 2, width), bf16),
            jax.ShapeDtypeStruct((lines // 2, width), bf16),
        ),
        in_specs=[pl.BlockSpec(memory_space=pltpu.SMEM)] + [vmem] * (4 + len(heads_out)),
        out_specs=(vmem, vmem, vmem),
        scratch_shapes=[
            pltpu.VMEM((lines, width), f32),
            pltpu.VMEM((lines, width), f32),
            pltpu.VMEM((n_seq, lines, width // n_seq), bf16),
        ],
        compiler_params=pltpu.CompilerParams(vmem_limit_bytes=12 * 1024 * 1024),
        name="feed_forward",
    )(place, stream, gain.reshape(1, width), gates, downs, *heads_out)


def body(
    n_dp,
    n_seq,
    tokens,
    attn_gain,
    qkv_weight,
    out_weight,
    mlp_gain,
    gate_up,
    down_weight,
    kv_pool,
    cache_len,
    page_table,
):
    seq_index = lax.axis_index("seq")
    dp_index = lax.axis_index("dp")
    core = seq_index % 2
    chips = n_seq // 2
    requests, new_count, width = tokens.shape
    pages, page_len, pair_width = kv_pool.shape
    head_dim = pair_width // 2
    heads = out_weight.shape[1] // head_dim
    page_count = page_table.shape[1]
    window = page_count * page_len
    lines = requests * new_count
    half = lines // 2
    rows = new_count * heads

    def ordered(mine, other, axis=0):
        return jnp.where(
            core == 0,
            jnp.concatenate([mine, other], axis=axis),
            jnp.concatenate([other, mine], axis=axis),
        )

    stream = tokens.reshape(lines, width)
    partner_weight = swap(qkv_weight, "dp", n_dp, 1)
    far = list(range(2, n_dp, 2))
    quarter_lines = lines // 4
    quarter_index = seq_index % 4
    my_quarter = lax.dynamic_slice_in_dim(stream, quarter_index * quarter_lines, quarter_lines)
    far_parts = jnp.concatenate([swap(my_quarter, "dp", n_dp, k) for k in far], axis=0)
    out_first, far_parts = lax.optimization_barrier((out_weight, far_parts))
    out_neighbour = swap(out_first, "dp", n_dp, 1)
    far_pairs = [far_parts, swap(far_parts, "seq", n_seq, 2)]
    far_mine = jnp.concatenate(far_pairs, axis=0)
    far_other = swap(far_mine, "seq", n_seq, 1)
    held_pool = pltpu.with_memory_space_constraint(kv_pool, pltpu.HBM)
    groups = [stream]
    stride = len(far) * quarter_lines
    for i in range(len(far)):
        for source in (far_mine, far_other):
            for start in (i * quarter_lines, stride + i * quarter_lines):
                groups.append(source[start : start + quarter_lines])
    normed = rms_norm(jnp.concatenate(groups, axis=0), attn_gain).astype(bf16)
    by_mine = lax.dot_general(normed, qkv_weight, contract, preferred_element_type=f32)
    by_partner = lax.dot_general(normed, partner_weight, contract, preferred_element_type=f32)
    products = jnp.where(
        dp_index % 2 == 0,
        jnp.concatenate([by_mine, by_partner], axis=1),
        jnp.concatenate([by_partner, by_mine], axis=1),
    ).astype(bf16)
    out_early, products = lax.optimization_barrier((out_weight, products))
    out_blocks = {k: swap(out_early, "dp", n_dp, k) for k in far}
    blocks = [products[:lines]]
    for i, k in enumerate(far):
        back = swap(products[(i + 1) * lines : (i + 2) * lines], "dp", n_dp, k)
        pieces = {
            m: back[n * quarter_lines : (n + 1) * quarter_lines] for n, m in enumerate((0, 2, 1, 3))
        }
        natural = []
        for j in range(4):
            piece = pieces[0]
            for m in (1, 2, 3):
                piece = jnp.where((quarter_index ^ m) == j, pieces[m], piece)
            natural.append(piece)
        blocks.append(jnp.concatenate(natural, axis=0))
    pair = dp_index // 2
    columns = []
    for j in range(n_dp // 2):
        block = blocks[0]
        for k in range(1, n_dp // 2):
            block = jnp.where((pair ^ k) == j, blocks[k], block)
        columns.append(block)
    pieces = gather_pieces(jnp.concatenate(columns, axis=1), n_seq)
    out_blocks[0] = out_weight
    out_blocks[1] = out_neighbour

    positions_int = cache_len[:, None] + jnp.arange(new_count, dtype=jnp.int32)[None, :]
    quarter = head_dim // 4
    inverse = 10000.0 ** (-jnp.arange(quarter).astype(f32) / quarter)
    angles = positions_int.reshape(lines, 1).astype(f32) * inverse
    cosine = jnp.cos(angles)
    sine = jnp.sin(angles)
    cosine = jnp.concatenate([cosine, cosine], axis=1)
    sine = jnp.concatenate([-sine, sine], axis=1)
    slot_ids = seq_index * pages + jnp.arange(pages, dtype=jnp.int32)
    matches = page_table[None, :, :] == slot_ids[:, None, None]
    number = jnp.arange(page_count, dtype=jnp.int32)[None, None, :]
    owner = jnp.arange(requests, dtype=jnp.int32)[None, :, None]
    slots = jnp.stack(
        [
            jnp.sum(jnp.where(matches, owner, 0), axis=(1, 2)),
            jnp.sum(jnp.where(matches, cache_len[None, :, None], 0), axis=(1, 2)),
            jnp.sum(jnp.where(matches, number, 0), axis=(1, 2)),
        ]
    )
    ends = jnp.stack([cache_len, cache_len + (new_count - 1)], axis=1)
    end_page = (ends // page_len) % page_count
    end_block = (ends % page_len) // 16
    hit = end_page[:, :, None] == jnp.arange(page_count, dtype=jnp.int32)[None, None, :]
    end_slot = jnp.sum(jnp.where(hit, page_table[:, None, :], 0), axis=2) - seq_index * pages
    good = (end_slot >= 0) & (end_slot < pages)
    same = (end_page[:, 0] == end_page[:, 1]) & (end_block[:, 0] == end_block[:, 1])
    good = good & jnp.stack([jnp.ones_like(same), ~same], axis=1)
    patches = jnp.stack(
        [
            jnp.where(good, end_slot, -1).reshape(-1),
            end_block.reshape(-1),
            end_page.reshape(-1),
        ]
    )

    dims = (requests, new_count, heads, pages, page_len, window, min(16, pages), n_seq)
    place, slots, patches, lengths = lax.optimization_barrier(
        (jnp.stack([seq_index, core, dp_index]), slots, patches, cache_len)
    )
    mine, theirs, fresh = attention(dims, slots, place, cosine, sine, pieces, held_pool)
    written_pool = write_pool(dims, patches, lengths, fresh, held_pool)

    side = requests // 2
    merged = merge_pair(mine, swap(theirs, "seq", n_seq, 1), side, rows)
    merged, *early = lax.optimization_barrier((merged, *[out_blocks[k] for k in [1, *far]]))
    for k, block in zip([1, *far], early):
        out_blocks[k] = block
    for k in far:
        out_blocks[k ^ 1] = swap(out_blocks[k], "dp", n_dp, 1)
    packs = [merged] + [swap(merged, "seq", n_seq, 2 * c) for c in range(1, chips)]
    gates, downs, token = fetch_weights(gate_up, down_weight, merged)
    packs, late = lax.optimization_barrier((packs, [out_blocks[k ^ 1] for k in far]))
    for k, block in zip(far, late):
        out_blocks[k ^ 1] = block
    attended_half = merge_final(packs, token, side, rows, heads)
    heads_part = project_out(
        place,
        attended_half,
        swap(attended_half, "seq", n_seq, 1),
        [out_blocks[k] for k in range(n_dp)],
    )
    heads_out = gather_pieces(heads_part, n_seq)
    keep, give, my_residual = feed_forward(
        n_seq, place, stream, heads_out, mlp_gain, gates, downs
    )
    chip_sum = (keep + swap(give, "seq", n_seq, 1).astype(f32)).astype(bf16)
    terms = [chip_sum] + [swap(chip_sum, "seq", n_seq, 2 * c) for c in range(1, chips)]
    terms, written_pool = lax.optimization_barrier((terms, written_pool))
    full_half = tree_sum([term.astype(f32) for term in terms])
    out_half = (my_residual.astype(f32) + full_half).astype(bf16)
    out_half = out_half.reshape(requests // 2, new_count, width)
    return ordered(out_half, swap(out_half, "seq", n_seq, 1)), written_pool


def solution(mesh):
    in_specs = (
        P("dp", None, None),
        P(),
        P(("seq", "dp"), None),
        P(("seq", "dp"), None),
        P(),
        P(None, "seq", None),
        P("seq", None),
        P(("dp", "seq"), None, None),
        P("dp"),
        P("dp", None),
    )
    out_specs = (P("dp", None, None), P(("dp", "seq"), None, None))
    return jax.shard_map(
        functools.partial(body, mesh.shape["dp"], mesh.shape["seq"]),
        mesh=mesh,
        in_specs=in_specs,
        out_specs=out_specs,
        check_vma=False,
    )
```

```python
import functools

import jax
import jax.numpy as jnp
from jax import lax
from jax.experimental import pallas as pl
from jax.experimental.pallas import tpu as pltpu
from jax.sharding import PartitionSpec as P

f32 = jnp.float32
bf16 = jnp.bfloat16
low_fill = -1e30
floor_peak = -1e29
contract = (((1,), (1,)), ((), ()))


def rms_norm(values, gains):
    floats = values.astype(f32)
    return floats * lax.rsqrt(jnp.mean(floats * floats, axis=-1, keepdims=True) + 1e-06) * gains


def swap(values, axis, size, mask):
    return lax.ppermute(values, axis, [(i, i ^ mask) for i in range(size)])


def tree_sum(terms):
    while len(terms) > 1:
        terms = [terms[i] + terms[i + 1] for i in range(0, len(terms), 2)]
    return terms[0]


def gather_pieces(values, n_seq):
    if n_seq > 8:
        return [lax.all_gather(values, "seq", axis=0)]
    pieces = {0: values}
    for mask in range(2, n_seq, 2):
        pieces[mask] = swap(values, "seq", n_seq, mask)
    for mask in range(0, n_seq, 2):
        pieces[mask + 1] = swap(pieces[mask], "seq", n_seq, 1)
    return [pieces[mask] for mask in range(n_seq)]


def place_pieces(me, refs, scratch):
    if len(refs) == 1:
        return refs[0]
    for mask, ref in enumerate(refs):
        scratch[jnp.bitwise_xor(me, mask)] = ref[...]
    return scratch


def write_kernel(dims, parts, patches, lengths, fresh, source, target, buffer, in_sems, out_sems):
    requests, new_count, heads, pages, page_len, window, chunk, n_seq = dims
    lines = requests * new_count
    count = pages // parts
    spans = [pl.ds(i * count, count) for i in range(parts)]
    loads = [
        pltpu.make_async_copy(source.at[span], buffer.at[span], in_sems.at[i])
        for i, span in enumerate(spans)
    ]
    stores = [
        pltpu.make_async_copy(buffer.at[span], target.at[span], out_sems.at[i])
        for i, span in enumerate(spans)
    ]
    for load in loads:
        load.start()
    for load in loads:
        load.wait()

    def write_patch(i, carry):
        slot = patches[0, i]

        @pl.when(slot >= 0)
        def _():
            r = i // 2
            row = pl.multiple_of(patches[1, i] * 16, 16)
            old = buffer[slot, pl.ds(row, 16), :]
            first = patches[2, i] * page_len + row - lengths[r]
            line = lax.broadcasted_iota(jnp.int32, (16, lines), 0)
            token = jnp.bitwise_and(first + line, window - 1)
            column = lax.broadcasted_iota(jnp.int32, (16, lines), 1)
            pick = (token < new_count) & (column == r * new_count + token)
            new = jnp.dot(pick.astype(f32).astype(bf16), fresh[...], preferred_element_type=f32)
            row_token = jnp.bitwise_and(
                first + lax.broadcasted_iota(jnp.int32, (16, 1), 0), window - 1
            )
            buffer[slot, pl.ds(row, 16), :] = jnp.where(
                row_token < new_count, new, old.astype(f32)
            ).astype(bf16)

        return carry

    lax.fori_loop(0, 2 * requests, write_patch, 0)
    for store in stores:
        store.start()
    for store in stores:
        store.wait()


def write_pool(dims, patches, lengths, fresh, kv_pool):
    parts = min(16, kv_pool.shape[0])
    smem = pl.BlockSpec(memory_space=pltpu.SMEM)
    hbm = pl.BlockSpec(memory_space=pltpu.HBM)
    return pl.pallas_call(
        functools.partial(write_kernel, dims, parts),
        out_shape=pltpu.HBM(kv_pool.shape, kv_pool.dtype),
        in_specs=[smem, smem, pl.BlockSpec(memory_space=pltpu.VMEM), hbm],
        out_specs=hbm,
        scratch_shapes=[
            pltpu.VMEM(kv_pool.shape, kv_pool.dtype),
            pltpu.SemaphoreType.DMA((parts,)),
            pltpu.SemaphoreType.DMA((parts,)),
        ],
        compiler_params=pltpu.CompilerParams(vmem_limit_bytes=12 * 1024 * 1024),
        cost_estimate=pl.CostEstimate(
            flops=0, bytes_accessed=2 * kv_pool.size * 2, transcendentals=0
        ),
        name="write_pool",
    )(patches, lengths, fresh, kv_pool)


def split_three(values):
    high = values.astype(bf16).astype(f32)
    middle = (values - high).astype(bf16).astype(f32)
    low = (values - high - middle).astype(bf16).astype(f32)
    return high, middle, low


def diagonal(rows):
    return lax.broadcasted_iota(jnp.int32, (rows, 128), 0) == lax.broadcasted_iota(
        jnp.int32, (rows, 128), 1
    )


def pack_logs(columns, rows):
    eye = diagonal(rows)
    lines = [
        jnp.sum(jnp.where(eye, jnp.broadcast_to(c, (rows, 128)), 0.0), axis=0, keepdims=True)
        for c in columns
    ]
    lines += [jnp.zeros((1, 128), f32)] * (8 - len(lines))
    high, middle, low = split_three(jnp.concatenate(lines, axis=0))
    return jnp.concatenate(
        [
            jnp.concatenate([high, middle], axis=1),
            jnp.concatenate([low, jnp.zeros((8, 128), f32)], axis=1),
        ],
        axis=0,
    )


def unpack_logs(block):
    return block[0:8, 0:128] + block[0:8, 128:256] + block[8:16, 0:128]


def merge_parts(packs, requests, rows):
    total = requests * rows
    bodies = [ref[...].astype(f32) for ref in packs]
    logs = [unpack_logs(body[total : total + 16]) for body in bodies]
    eye = diagonal(rows)
    results, columns = [], []
    for r in range(requests):
        cols = [
            jnp.sum(
                jnp.where(eye, jnp.broadcast_to(log[r : r + 1, :], (rows, 128)), 0.0),
                axis=1,
                keepdims=True,
            )
            for log in logs
        ]
        top = functools.reduce(jnp.maximum, cols)
        scales = [jnp.exp(c - top) for c in cols]
        norm = functools.reduce(jnp.add, scales)
        parts = [
            body[r * rows : (r + 1) * rows] * scale for body, scale in zip(bodies, scales)
        ]
        results.append(functools.reduce(jnp.add, parts) / norm)
        columns.append(top + jnp.log(norm))
    return results, columns


def pair_kernel(requests, rows, mine, other, out):
    results, columns = merge_parts([mine, other], requests, rows)
    body = jnp.concatenate(results + [pack_logs(columns, rows)], axis=0)
    out[...] = body.astype(bf16)


def merge_pair(mine, other, requests, rows):
    return pl.pallas_call(
        functools.partial(pair_kernel, requests, rows),
        out_shape=jax.ShapeDtypeStruct(mine.shape, bf16),
        in_specs=[pl.BlockSpec(memory_space=pltpu.VMEM)] * 2,
        out_specs=pl.BlockSpec(memory_space=pltpu.VMEM),
        compiler_params=pltpu.CompilerParams(vmem_limit_bytes=8 * 1024 * 1024),
        name="merge_pair",
    )(mine, other)


def final_kernel(count, requests, rows, heads, *refs):
    packs, out, scratch_low, scratch_high = refs[:count], refs[count + 1], refs[-2], refs[-1]
    results, unused = merge_parts(packs, requests, rows)
    body = jnp.concatenate(results, axis=0)
    scratch_low[...] = body[:, 0:128]
    scratch_high[...] = body[:, 128:256]
    lines = requests * rows // heads
    for h in range(heads):
        low = scratch_low[pl.ds(h, lines, stride=heads), :]
        high = scratch_high[pl.ds(h, lines, stride=heads), :]
        out[:, h * 256 : (h + 1) * 256] = jnp.concatenate([low, high], axis=1).astype(bf16)


def merge_final(packs, token, requests, rows, heads):
    lines = requests * rows // heads
    return pl.pallas_call(
        functools.partial(final_kernel, len(packs), requests, rows, heads),
        out_shape=jax.ShapeDtypeStruct((lines, heads * 256), bf16),
        in_specs=[pl.BlockSpec(memory_space=pltpu.VMEM)] * (len(packs) + 1),
        out_specs=pl.BlockSpec(memory_space=pltpu.VMEM),
        scratch_shapes=[pltpu.VMEM((requests * rows, 128), f32)] * 2,
        compiler_params=pltpu.CompilerParams(vmem_limit_bytes=8 * 1024 * 1024),
        name="merge_final",
    )(*packs, token)


def attention_kernel(dims, count, slots, place, cosine, sine, *refs):
    requests, new_count, heads, pages, page_len, window, chunk, n_seq = dims
    pieces, refs = refs[:count], refs[count:]
    pool, mine, theirs, fresh, buffer, gathered, projected = refs[:7]
    query_low, query_high, queries, peak, norm, total, in_sems = refs[7:]
    rows = new_count * heads
    lines = requests * new_count

    def load(c):
        span = pl.ds(c * chunk, chunk)
        return pltpu.make_async_copy(pool.at[span], buffer.at[span], in_sems.at[c])

    for c in range(pages // chunk):
        load(c).start()

    ordered_pieces = place_pieces(place[0], pieces, gathered)
    part_columns = projected.shape[1] // n_seq
    for i in range(n_seq):
        projected[:, i * part_columns : (i + 1) * part_columns] = ordered_pieces[i]
    cos = cosine[...]
    sin = sine[...]

    def turned(block):
        x = projected[:, block * 128 : (block + 1) * 128].astype(f32)
        return (x * cos + pltpu.roll(x, 64, 1) * sin).astype(bf16).astype(f32)

    for h in range(heads):
        query_low[pl.ds(h, lines, stride=heads), :] = turned(2 * h)
        query_high[pl.ds(h, lines, stride=heads), :] = projected[
            :, h * 256 + 128 : h * 256 + 256
        ].astype(f32)
    fresh[:, 0:128] = turned(2 * heads).astype(bf16)
    fresh[:, 128:512] = projected[:, heads * 256 + 128 : heads * 256 + 512]

    peak[...] = jnp.full(peak.shape, floor_peak, f32)
    norm[...] = jnp.zeros(norm.shape, f32)
    total[...] = jnp.zeros(total.shape, f32)

    token_of = lax.broadcasted_iota(jnp.int32, (rows, 1), 0) // heads
    lane = lax.broadcasted_iota(jnp.int32, (1, page_len), 1)
    scale = 256.0 ** (-0.5)

    for r in range(requests):
        span = slice(r * rows, (r + 1) * rows)
        queries[r, 0:rows, :] = jnp.concatenate(
            [query_low[span, :], query_high[span, :]], axis=1
        ).astype(bf16)

    def score(r, keys):
        return lax.dot_general(queries[r, 0:rows, :], keys, contract, preferred_element_type=f32)

    def weigh(scores, visible):
        scores = jnp.where(visible, scores * scale, low_fill)
        top = jnp.maximum(jnp.max(scores, axis=1, keepdims=True), floor_peak)
        weights = jnp.exp(scores - top)
        return top, jnp.sum(weights, axis=1, keepdims=True), weights.astype(bf16)

    def mix(weights, values):
        return jnp.dot(weights, values, preferred_element_type=f32)

    def add(r, top, amount, mixed):
        span = pl.ds(pl.multiple_of(r * rows, 8), rows)
        old = peak[span, :]
        high = jnp.maximum(old, top)
        keep = jnp.exp(old - high)
        take = jnp.exp(top - high)
        peak[span, :] = high
        norm[span, :] = norm[span, :] * keep + amount * take
        total[span, :] = total[span, :] * jnp.concatenate(
            [keep, keep], axis=1
        ) + mixed * jnp.concatenate([take, take], axis=1)

    me = place[0]
    fresh_lane = lax.broadcasted_iota(jnp.int32, (1, lines), 1)
    for step in range(-(-requests // n_seq)):
        r = me + step * n_seq

        @pl.when(r < requests)
        def _():
            index = fresh_lane - r * new_count
            seen = (index >= 0) & (index <= token_of)
            top, amount, weights = weigh(score(r, fresh[:, 0:256]), seen)
            add(r, top, amount, mix(weights, fresh[:, 256:512]))

    def chunk_scores(c):
        load(c).wait()
        numbers = range(c * chunk, (c + 1) * chunk)
        return [score(slots[0, page], buffer[page, :, 0:256]) for page in numbers]

    ahead = chunk_scores(0)
    for c in range(pages // chunk):
        scores = ahead
        if (c + 1) * chunk < pages:
            ahead = chunk_scores(c + 1)
        numbers = range(c * chunk, (c + 1) * chunk)
        weighed = []
        for page, values in zip(numbers, scores):
            length = slots[1, page]
            start = slots[2, page] * page_len
            age = jnp.bitwise_and(length - 1 - start - lane, window - 1)
            limit = jnp.minimum(length - 1, window - 2 - token_of)
            weighed.append(weigh(values, age <= limit))
        mixed = [
            mix(weights, buffer[page, :, 256:512])
            for page, (top, amount, weights) in zip(numbers, weighed)
        ]
        for page, (top, amount, weights), values in zip(numbers, weighed, mixed):
            add(slots[0, page], top, amount, values)

    half = requests // 2
    core = place[1]
    for side, out in ((core, mine), (1 - core, theirs)):
        logs = []
        for k in range(half):
            span = pl.ds(pl.multiple_of((side * half + k) * rows, 8), rows)
            amount = norm[span, :]
            some = amount > 0.0
            safe = jnp.where(some, amount, 1.0)
            logs.append(jnp.where(some, peak[span, :] + jnp.log(safe), low_fill))
            inverse = jnp.where(some, 1.0 / safe, 0.0)
            total[span, :] = total[span, :] * jnp.concatenate([inverse, inverse], axis=1)
        span = pl.ds(pl.multiple_of(side * half * rows, 8), half * rows)
        out[0 : half * rows, :] = total[span, :].astype(bf16)
        out[half * rows : half * rows + 16, :] = pack_logs(logs, rows).astype(bf16)


def attention(dims, slots, place, cosine, sine, pieces, pool):
    requests, new_count, heads, pages, page_len, window, chunk, n_seq = dims
    part_columns = pieces[0].shape[-1]
    lines = requests * new_count
    rows = new_count * heads
    smem = pl.BlockSpec(memory_space=pltpu.SMEM)
    vmem = pl.BlockSpec(memory_space=pltpu.VMEM)
    pack = jax.ShapeDtypeStruct((requests // 2 * rows + 16, 256), bf16)
    return pl.pallas_call(
        functools.partial(attention_kernel, dims, len(pieces)),
        out_shape=(pack, pack, jax.ShapeDtypeStruct((requests * new_count, 512), bf16)),
        in_specs=[smem, smem, vmem, vmem]
        + [vmem] * len(pieces)
        + [pl.BlockSpec(memory_space=pltpu.HBM)],
        out_specs=(vmem, vmem, vmem),
        scratch_shapes=[
            pltpu.VMEM(pool.shape, bf16),
            pltpu.VMEM((n_seq, lines, part_columns), bf16),
            pltpu.VMEM((lines, n_seq * part_columns), bf16),
            pltpu.VMEM((requests * rows, 128), f32),
            pltpu.VMEM((requests * rows, 128), f32),
            pltpu.VMEM((requests, -(-rows // 16) * 16, 256), bf16),
            pltpu.VMEM((requests * rows, 128), f32),
            pltpu.VMEM((requests * rows, 128), f32),
            pltpu.VMEM((requests * rows, 256), f32),
            pltpu.SemaphoreType.DMA((pages // chunk,)),
        ],
        compiler_params=pltpu.CompilerParams(vmem_limit_bytes=20 * 1024 * 1024),
        cost_estimate=pl.CostEstimate(flops=0, bytes_accessed=1024, transcendentals=0),
        name="page_attention",
    )(slots, place, cosine, sine, *pieces, pool)


def project_kernel(count, place, mine, other, *refs):
    blocks, out = refs[:count], refs[count]
    core, plane = place[1], place[2]
    low = jnp.where(core == 0, mine[...], other[...])
    high = jnp.where(core == 0, other[...], mine[...])
    attended = jnp.concatenate([low, high], axis=0)
    products = [
        lax.dot_general(attended, block[...], contract, preferred_element_type=f32)
        for block in blocks
    ]
    columns = []
    for j in range(count):
        column = products[0]
        for k in range(1, count):
            column = jnp.where((plane ^ k) == j, products[k], column)
        columns.append(column)
    out[...] = jnp.concatenate(columns, axis=1).astype(bf16)


def project_out(place, mine, other, blocks):
    vmem = pl.BlockSpec(memory_space=pltpu.VMEM)
    shape = (2 * mine.shape[0], len(blocks) * blocks[0].shape[0])
    return pl.pallas_call(
        functools.partial(project_kernel, len(blocks)),
        out_shape=jax.ShapeDtypeStruct(shape, bf16),
        in_specs=[pl.BlockSpec(memory_space=pltpu.SMEM)] + [vmem] * (2 + len(blocks)),
        out_specs=vmem,
        compiler_params=pltpu.CompilerParams(vmem_limit_bytes=8 * 1024 * 1024),
        name="project_out",
    )(place, mine, other, *blocks)


def fetch_kernel(parts, gate_up, down, after, gates, downs, token, sems):
    units = down.shape[0]
    size = units // parts
    copies = []
    for i in range(parts):
        span = pl.ds(i * size, size)
        copies.append(pltpu.make_async_copy(gate_up.at[0, span], gates.at[0, span], sems.at[0, i]))
        copies.append(pltpu.make_async_copy(gate_up.at[1, span], gates.at[1, span], sems.at[1, i]))
        copies.append(pltpu.make_async_copy(down.at[span], downs.at[span], sems.at[2, i]))
    for copy in copies:
        copy.start()
    token[...] = jnp.zeros(token.shape, f32)
    for copy in copies:
        copy.wait()


def fetch_weights(gate_up, down, after):
    parts = max(c for c in (1, 2, 3, 4) if down.shape[0] % (16 * c) == 0)
    hbm = pl.BlockSpec(memory_space=pltpu.HBM)
    anywhere = pl.BlockSpec(memory_space=pl.ANY)
    return pl.pallas_call(
        functools.partial(fetch_kernel, parts),
        out_shape=(
            jax.ShapeDtypeStruct(gate_up.shape, bf16),
            jax.ShapeDtypeStruct(down.shape, bf16),
            jax.ShapeDtypeStruct((8, 128), f32),
        ),
        in_specs=[hbm, hbm, anywhere],
        out_specs=(anywhere, anywhere, pl.BlockSpec(memory_space=pltpu.VMEM)),
        scratch_shapes=[pltpu.SemaphoreType.DMA((3, parts))],
        compiler_params=pltpu.CompilerParams(vmem_limit_bytes=2 * 1024 * 1024),
        cost_estimate=pl.CostEstimate(
            flops=0, bytes_accessed=2 * (gate_up.size + down.size), transcendentals=0
        ),
        name="fetch_weights",
    )(
        pltpu.with_memory_space_constraint(gate_up, pltpu.HBM),
        pltpu.with_memory_space_constraint(down, pltpu.HBM),
        after,
    )


def mlp_kernel(chunk, pieces, place, stream, gain, gates, downs, *refs):
    heads_out, refs = refs[:pieces], refs[pieces:]
    keep, give, kept_residual, residual, total, heads_scratch = refs
    units, width = downs.shape
    heads_out = place_pieces(place[0], heads_out, heads_scratch)
    count = units // chunk
    gathered = jnp.concatenate(
        [heads_out[i].astype(f32) for i in range(heads_out.shape[0])], axis=1
    )
    summed = stream[...].astype(f32) + gathered
    residual[...] = summed.astype(bf16).astype(f32)
    floats = residual[...]
    spread = lax.rsqrt(jnp.mean(floats * floats, axis=-1, keepdims=True) + 1e-06)
    inputs = (floats * spread * gain[...]).astype(bf16)
    root = (2.0 / 3.141592653589793) ** 0.5

    def rise(c):
        span = slice(c * chunk, (c + 1) * chunk)
        gate = lax.dot_general(inputs, gates[0, span, :], contract, preferred_element_type=f32)
        up = lax.dot_general(inputs, gates[1, span, :], contract, preferred_element_type=f32)
        inner = root * (gate + 0.044715 * (gate * gate * gate))
        return (0.5 * gate * (1.0 + jnp.tanh(inner)) * up).astype(bf16)

    def fall(c, hidden):
        span = slice(c * chunk, (c + 1) * chunk)
        product = jnp.dot(hidden, downs[span, :], preferred_element_type=f32)
        if c == 0:
            total[...] = product
        else:
            total[...] += product

    before = rise(0)
    for c in range(1, count):
        after = rise(c)
        fall(c - 1, before)
        before = after
    fall(count - 1, before)
    half = total.shape[0] // 2
    core = place[1]
    mine = pl.ds(pl.multiple_of(core * half, 8), half)
    keep[...] = total[mine, :]
    kept_residual[...] = residual[mine, :].astype(bf16)
    give[...] = total[pl.ds(pl.multiple_of((1 - core) * half, 8), half), :].astype(bf16)


def feed_forward(n_seq, place, stream, heads_out, gain, gates, downs):
    lines, width = stream.shape
    units = downs.shape[0]
    chunk = max(c for c in range(16, 512, 16) if units % c == 0)
    vmem = pl.BlockSpec(memory_space=pltpu.VMEM)
    return pl.pallas_call(
        functools.partial(mlp_kernel, chunk, len(heads_out)),
        out_shape=(
            jax.ShapeDtypeStruct((lines // 2, width), f32),
            jax.ShapeDtypeStruct((lines // 2, width), bf16),
            jax.ShapeDtypeStruct((lines // 2, width), bf16),
        ),
        in_specs=[pl.BlockSpec(memory_space=pltpu.SMEM)] + [vmem] * (4 + len(heads_out)),
        out_specs=(vmem, vmem, vmem),
        scratch_shapes=[
            pltpu.VMEM((lines, width), f32),
            pltpu.VMEM((lines, width), f32),
            pltpu.VMEM((n_seq, lines, width // n_seq), bf16),
        ],
        compiler_params=pltpu.CompilerParams(vmem_limit_bytes=12 * 1024 * 1024),
        name="feed_forward",
    )(place, stream, gain.reshape(1, width), gates, downs, *heads_out)


def body(
    n_dp,
    n_seq,
    tokens,
    attn_gain,
    qkv_weight,
    out_weight,
    mlp_gain,
    gate_up,
    down_weight,
    kv_pool,
    cache_len,
    page_table,
):
    seq_index = lax.axis_index("seq")
    dp_index = lax.axis_index("dp")
    core = seq_index % 2
    chips = n_seq // 2
    requests, new_count, width = tokens.shape
    pages, page_len, pair_width = kv_pool.shape
    head_dim = pair_width // 2
    heads = out_weight.shape[1] // head_dim
    page_count = page_table.shape[1]
    window = page_count * page_len
    lines = requests * new_count
    half = lines // 2
    rows = new_count * heads

    def ordered(mine, other, axis=0):
        return jnp.where(
            core == 0,
            jnp.concatenate([mine, other], axis=axis),
            jnp.concatenate([other, mine], axis=axis),
        )

    stream = tokens.reshape(lines, width)
    partner_weight = swap(qkv_weight, "dp", n_dp, 1)
    far = list(range(2, n_dp, 2))
    quarter_lines = lines // 4
    quarter_index = seq_index % 4
    some = requests // 4
    my_quarter = lax.dynamic_slice_in_dim(tokens, quarter_index * some, some)
    far_parts = jnp.concatenate([swap(my_quarter, "dp", n_dp, k) for k in far], axis=0)
    cache_len, page_table, far_parts = lax.optimization_barrier((cache_len, page_table, far_parts))
    far_pairs = [far_parts, swap(far_parts, "seq", n_seq, 2)]
    far_mine = jnp.concatenate(far_pairs, axis=0)
    far_other = swap(far_mine, "seq", n_seq, 1).reshape(-1, width)
    far_mine = far_mine.reshape(-1, width)
    held_pool = pltpu.with_memory_space_constraint(kv_pool, pltpu.HBM)
    groups = [stream]
    stride = len(far) * quarter_lines
    for i in range(len(far)):
        for source in (far_mine, far_other):
            for start in (i * quarter_lines, stride + i * quarter_lines):
                groups.append(source[start : start + quarter_lines])
    normed = rms_norm(jnp.concatenate(groups, axis=0), attn_gain).astype(bf16)
    by_mine = lax.dot_general(normed, qkv_weight, contract, preferred_element_type=f32)
    by_partner = lax.dot_general(normed, partner_weight, contract, preferred_element_type=f32)
    products = jnp.where(
        dp_index % 2 == 0,
        jnp.concatenate([by_mine, by_partner], axis=1),
        jnp.concatenate([by_partner, by_mine], axis=1),
    ).astype(bf16)
    out_early, products = lax.optimization_barrier((out_weight, products))
    out_blocks = {k: swap(out_early, "dp", n_dp, k) for k in [1, *far]}
    blocks = [products[:lines]]
    for i, k in enumerate(far):
        back = swap(products[(i + 1) * lines : (i + 2) * lines], "dp", n_dp, k)
        pieces = {
            m: back[n * quarter_lines : (n + 1) * quarter_lines] for n, m in enumerate((0, 2, 1, 3))
        }
        natural = []
        for j in range(4):
            piece = pieces[0]
            for m in (1, 2, 3):
                piece = jnp.where((quarter_index ^ m) == j, pieces[m], piece)
            natural.append(piece)
        blocks.append(jnp.concatenate(natural, axis=0))
    pair = dp_index // 2
    columns = []
    for j in range(n_dp // 2):
        block = blocks[0]
        for k in range(1, n_dp // 2):
            block = jnp.where((pair ^ k) == j, blocks[k], block)
        columns.append(block)
    pieces = gather_pieces(jnp.concatenate(columns, axis=1), n_seq)
    out_blocks[0] = out_weight

    positions_int = cache_len[:, None] + jnp.arange(new_count, dtype=jnp.int32)[None, :]
    quarter = head_dim // 4
    inverse = 10000.0 ** (-jnp.arange(quarter).astype(f32) / quarter)
    angles = positions_int.reshape(lines, 1).astype(f32) * inverse
    cosine = jnp.cos(angles)
    sine = jnp.sin(angles)
    cosine = jnp.concatenate([cosine, cosine], axis=1)
    sine = jnp.concatenate([-sine, sine], axis=1)
    slot_ids = seq_index * pages + jnp.arange(pages, dtype=jnp.int32)
    matches = page_table[None, :, :] == slot_ids[:, None, None]
    number = jnp.arange(page_count, dtype=jnp.int32)[None, None, :]
    owner = jnp.arange(requests, dtype=jnp.int32)[None, :, None]
    slots = jnp.stack(
        [
            jnp.sum(jnp.where(matches, owner, 0), axis=(1, 2)),
            jnp.sum(jnp.where(matches, cache_len[None, :, None], 0), axis=(1, 2)),
            jnp.sum(jnp.where(matches, number, 0), axis=(1, 2)),
        ]
    )
    ends = jnp.stack([cache_len, cache_len + (new_count - 1)], axis=1)
    end_page = (ends // page_len) % page_count
    end_block = (ends % page_len) // 16
    hit = end_page[:, :, None] == jnp.arange(page_count, dtype=jnp.int32)[None, None, :]
    end_slot = jnp.sum(jnp.where(hit, page_table[:, None, :], 0), axis=2) - seq_index * pages
    good = (end_slot >= 0) & (end_slot < pages)
    same = (end_page[:, 0] == end_page[:, 1]) & (end_block[:, 0] == end_block[:, 1])
    good = good & jnp.stack([jnp.ones_like(same), ~same], axis=1)
    patches = jnp.stack(
        [
            jnp.where(good, end_slot, -1).reshape(-1),
            end_block.reshape(-1),
            end_page.reshape(-1),
        ]
    )

    dims = (requests, new_count, heads, pages, page_len, window, min(16, pages), n_seq)
    place, slots, patches, lengths = lax.optimization_barrier(
        (jnp.stack([seq_index, core, dp_index]), slots, patches, cache_len)
    )
    mine, theirs, fresh = attention(dims, slots, place, cosine, sine, pieces, held_pool)
    written_pool = write_pool(dims, patches, lengths, fresh, held_pool)

    side = requests // 2
    merged = merge_pair(mine, swap(theirs, "seq", n_seq, 1), side, rows)
    merged, *early = lax.optimization_barrier((merged, *[out_blocks[k] for k in [1, *far]]))
    for k, block in zip([1, *far], early):
        out_blocks[k] = block
    for k in far:
        out_blocks[k ^ 1] = swap(out_blocks[k], "dp", n_dp, 1)
    packs = [merged] + [swap(merged, "seq", n_seq, 2 * c) for c in range(1, chips)]
    gates, downs, token = fetch_weights(gate_up, down_weight, merged)
    packs, late = lax.optimization_barrier((packs, [out_blocks[k ^ 1] for k in far]))
    for k, block in zip(far, late):
        out_blocks[k ^ 1] = block
    attended_half = merge_final(packs, token, side, rows, heads)
    heads_part = project_out(
        place,
        attended_half,
        swap(attended_half, "seq", n_seq, 1),
        [out_blocks[k] for k in range(n_dp)],
    )
    heads_out = gather_pieces(heads_part, n_seq)
    keep, give, my_residual = feed_forward(
        n_seq, place, stream, heads_out, mlp_gain, gates, downs
    )
    chip_sum = (keep + swap(give, "seq", n_seq, 1).astype(f32)).astype(bf16)
    terms = [chip_sum] + [swap(chip_sum, "seq", n_seq, 2 * c) for c in range(1, chips)]
    terms, written_pool = lax.optimization_barrier((terms, written_pool))
    full_half = tree_sum([term.astype(f32) for term in terms])
    out_half = (my_residual.astype(f32) + full_half).astype(bf16)
    out_half = out_half.reshape(requests // 2, new_count, width)
    return ordered(out_half, swap(out_half, "seq", n_seq, 1)), written_pool


def solution(mesh):
    in_specs = (
        P("dp", None, None),
        P(),
        P(("seq", "dp"), None),
        P(("seq", "dp"), None),
        P(),
        P(None, "seq", None),
        P("seq", None),
        P(("dp", "seq"), None, None),
        P("dp"),
        P("dp", None),
    )
    out_specs = (P("dp", None, None), P(("dp", "seq"), None, None))
    return jax.shard_map(
        functools.partial(body, mesh.shape["dp"], mesh.shape["seq"]),
        mesh=mesh,
        in_specs=in_specs,
        out_specs=out_specs,
        check_vma=False,
    )
```

```python
import functools

import jax
import jax.numpy as jnp
from jax import lax
from jax.experimental import pallas as pl
from jax.experimental.pallas import tpu as pltpu
from jax.sharding import PartitionSpec as P

f32 = jnp.float32
bf16 = jnp.bfloat16
low_fill = -1e30
floor_peak = -1e29
contract = (((1,), (1,)), ((), ()))


def rms_norm(values, gains):
    floats = values.astype(f32)
    return floats * lax.rsqrt(jnp.mean(floats * floats, axis=-1, keepdims=True) + 1e-06) * gains


def swap(values, axis, size, mask):
    return lax.ppermute(values, axis, [(i, i ^ mask) for i in range(size)])


def tree_sum(terms):
    while len(terms) > 1:
        terms = [terms[i] + terms[i + 1] for i in range(0, len(terms), 2)]
    return terms[0]


def gather_pieces(values, n_seq):
    if n_seq > 8:
        return [lax.all_gather(values, "seq", axis=0)]
    pieces = {0: values}
    for mask in range(2, n_seq, 2):
        pieces[mask] = swap(values, "seq", n_seq, mask)
    for mask in range(0, n_seq, 2):
        pieces[mask + 1] = swap(pieces[mask], "seq", n_seq, 1)
    return [pieces[mask] for mask in range(n_seq)]


def place_pieces(me, refs, scratch):
    if len(refs) == 1:
        return refs[0]
    for mask, ref in enumerate(refs):
        scratch[jnp.bitwise_xor(me, mask)] = ref[...]
    return scratch


def write_kernel(dims, parts, patch_source, fresh, source, target, buffer, patches, *sems):
    patch_sem, in_sems, out_sems = sems
    requests, new_count, heads, pages, page_len, window, chunk, n_seq = dims
    lines = requests * new_count
    count = pages // parts
    spans = [pl.ds(i * count, count) for i in range(parts)]
    loads = [
        pltpu.make_async_copy(source.at[span], buffer.at[span], in_sems.at[i])
        for i, span in enumerate(spans)
    ]
    stores = [
        pltpu.make_async_copy(buffer.at[span], target.at[span], out_sems.at[i])
        for i, span in enumerate(spans)
    ]
    patch_load = pltpu.make_async_copy(patch_source, patches, patch_sem)
    patch_load.start()
    for load in loads:
        load.start()
    patch_load.wait()

    def write_patch(part, i):
        slot = patches[0, i]

        @pl.when((slot >= part * count) & (slot < (part + 1) * count))
        def _():
            r = i // 2
            row = pl.multiple_of(patches[1, i] * 16, 16)
            old = buffer[slot, pl.ds(row, 16), :]
            first = patches[2, i] * page_len + row - patches[3, i]
            line = lax.broadcasted_iota(jnp.int32, (16, lines), 0)
            token = jnp.bitwise_and(first + line, window - 1)
            column = lax.broadcasted_iota(jnp.int32, (16, lines), 1)
            pick = (token < new_count) & (column == r * new_count + token)
            new = jnp.dot(pick.astype(f32).astype(bf16), fresh[...], preferred_element_type=f32)
            row_token = jnp.bitwise_and(
                first + lax.broadcasted_iota(jnp.int32, (16, 1), 0), window - 1
            )
            buffer[slot, pl.ds(row, 16), :] = jnp.where(
                row_token < new_count, new, old.astype(f32)
            ).astype(bf16)

    for part, (load, store) in enumerate(zip(loads, stores)):
        load.wait()
        pl.loop(0, 2 * requests)(functools.partial(write_patch, part))
        store.start()
    for store in stores:
        store.wait()


def write_pool(dims, patches, fresh, kv_pool):
    parts = 4
    hbm = pl.BlockSpec(memory_space=pltpu.HBM)
    return pl.pallas_call(
        functools.partial(write_kernel, dims, parts),
        out_shape=pltpu.HBM(kv_pool.shape, kv_pool.dtype),
        in_specs=[
            pl.BlockSpec(memory_space=pl.ANY),
            pl.BlockSpec(memory_space=pltpu.VMEM),
            hbm,
        ],
        out_specs=hbm,
        scratch_shapes=[
            pltpu.VMEM(kv_pool.shape, kv_pool.dtype),
            pltpu.SMEM(patches.shape, jnp.int32),
            pltpu.SemaphoreType.DMA,
            pltpu.SemaphoreType.DMA((parts,)),
            pltpu.SemaphoreType.DMA((parts,)),
        ],
        compiler_params=pltpu.CompilerParams(vmem_limit_bytes=12 * 1024 * 1024),
        cost_estimate=pl.CostEstimate(
            flops=0, bytes_accessed=2 * kv_pool.size * 2, transcendentals=0
        ),
        name="write_pool",
    )(patches, fresh, kv_pool)


def split_three(values):
    high = values.astype(bf16).astype(f32)
    middle = (values - high).astype(bf16).astype(f32)
    low = (values - high - middle).astype(bf16).astype(f32)
    return high, middle, low


def diagonal(rows):
    return lax.broadcasted_iota(jnp.int32, (rows, 128), 0) == lax.broadcasted_iota(
        jnp.int32, (rows, 128), 1
    )


def pack_logs(columns, rows):
    eye = diagonal(rows)
    lines = [
        jnp.sum(jnp.where(eye, jnp.broadcast_to(c, (rows, 128)), 0.0), axis=0, keepdims=True)
        for c in columns
    ]
    lines += [jnp.zeros((1, 128), f32)] * (8 - len(lines))
    high, middle, low = split_three(jnp.concatenate(lines, axis=0))
    return jnp.concatenate(
        [
            jnp.concatenate([high, middle], axis=1),
            jnp.concatenate([low, jnp.zeros((8, 128), f32)], axis=1),
        ],
        axis=0,
    )


def unpack_logs(block):
    return block[0:8, 0:128] + block[0:8, 128:256] + block[8:16, 0:128]


def merge_parts(packs, requests, rows):
    total = requests * rows
    bodies = [ref[...].astype(f32) for ref in packs]
    logs = [unpack_logs(body[total : total + 16]) for body in bodies]
    eye = diagonal(rows)
    results, columns = [], []
    for r in range(requests):
        cols = [
            jnp.sum(
                jnp.where(eye, jnp.broadcast_to(log[r : r + 1, :], (rows, 128)), 0.0),
                axis=1,
                keepdims=True,
            )
            for log in logs
        ]
        top = functools.reduce(jnp.maximum, cols)
        scales = [jnp.exp(c - top) for c in cols]
        norm = functools.reduce(jnp.add, scales)
        parts = [
            body[r * rows : (r + 1) * rows] * scale for body, scale in zip(bodies, scales)
        ]
        results.append(functools.reduce(jnp.add, parts) / norm)
        columns.append(top + jnp.log(norm))
    return results, columns


def pair_kernel(requests, rows, mine, other, out):
    results, columns = merge_parts([mine, other], requests, rows)
    body = jnp.concatenate(results + [pack_logs(columns, rows)], axis=0)
    out[...] = body.astype(bf16)


def merge_pair(mine, other, requests, rows):
    return pl.pallas_call(
        functools.partial(pair_kernel, requests, rows),
        out_shape=jax.ShapeDtypeStruct(mine.shape, bf16),
        in_specs=[pl.BlockSpec(memory_space=pltpu.VMEM)] * 2,
        out_specs=pl.BlockSpec(memory_space=pltpu.VMEM),
        compiler_params=pltpu.CompilerParams(vmem_limit_bytes=8 * 1024 * 1024),
        name="merge_pair",
    )(mine, other)


def final_kernel(count, requests, rows, heads, *refs):
    packs, out, scratch_low, scratch_high = refs[:count], refs[count + 1], refs[-2], refs[-1]
    results, unused = merge_parts(packs, requests, rows)
    body = jnp.concatenate(results, axis=0)
    scratch_low[...] = body[:, 0:128]
    scratch_high[...] = body[:, 128:256]
    lines = requests * rows // heads
    for h in range(heads):
        low = scratch_low[pl.ds(h, lines, stride=heads), :]
        high = scratch_high[pl.ds(h, lines, stride=heads), :]
        out[:, h * 256 : (h + 1) * 256] = jnp.concatenate([low, high], axis=1).astype(bf16)


def merge_final(packs, token, requests, rows, heads):
    lines = requests * rows // heads
    return pl.pallas_call(
        functools.partial(final_kernel, len(packs), requests, rows, heads),
        out_shape=jax.ShapeDtypeStruct((lines, heads * 256), bf16),
        in_specs=[pl.BlockSpec(memory_space=pltpu.VMEM)] * (len(packs) + 1),
        out_specs=pl.BlockSpec(memory_space=pltpu.VMEM),
        scratch_shapes=[pltpu.VMEM((requests * rows, 128), f32)] * 2,
        compiler_params=pltpu.CompilerParams(vmem_limit_bytes=8 * 1024 * 1024),
        name="merge_final",
    )(*packs, token)


def attention_kernel(dims, count, slot_source, cosine, sine, *refs):
    requests, new_count, heads, pages, page_len, window, chunk, n_seq = dims
    pieces, refs = refs[:count], refs[count:]
    pool, mine, theirs, fresh, buffer, gathered, projected = refs[:7]
    query_low, query_high, queries, peak, norm, total, slots, slot_sem, in_sems = refs[7:]
    slot_load = pltpu.make_async_copy(slot_source, slots, slot_sem)
    slot_load.start()
    rows = new_count * heads
    lines = requests * new_count

    def load(c):
        span = pl.ds(c * chunk, chunk)
        return pltpu.make_async_copy(pool.at[span], buffer.at[span], in_sems.at[c])

    for c in range(pages // chunk):
        load(c).start()

    me = lax.axis_index("seq")
    ordered_pieces = place_pieces(me, pieces, gathered)
    part_columns = projected.shape[1] // n_seq
    for i in range(n_seq):
        projected[:, i * part_columns : (i + 1) * part_columns] = ordered_pieces[i]
    cos = cosine[...]
    sin = sine[...]

    def turned(block):
        x = projected[:, block * 128 : (block + 1) * 128].astype(f32)
        return (x * cos + pltpu.roll(x, 64, 1) * sin).astype(bf16).astype(f32)

    for h in range(heads):
        query_low[pl.ds(h, lines, stride=heads), :] = turned(2 * h)
        query_high[pl.ds(h, lines, stride=heads), :] = projected[
            :, h * 256 + 128 : h * 256 + 256
        ].astype(f32)
    fresh[:, 0:128] = turned(2 * heads).astype(bf16)
    fresh[:, 128:512] = projected[:, heads * 256 + 128 : heads * 256 + 512]

    peak[...] = jnp.full(peak.shape, floor_peak, f32)
    norm[...] = jnp.zeros(norm.shape, f32)
    total[...] = jnp.zeros(total.shape, f32)

    token_of = lax.broadcasted_iota(jnp.int32, (rows, 1), 0) // heads
    lane = lax.broadcasted_iota(jnp.int32, (1, page_len), 1)
    scale = 256.0 ** (-0.5)

    for r in range(requests):
        span = slice(r * rows, (r + 1) * rows)
        queries[r, 0:rows, :] = jnp.concatenate(
            [query_low[span, :], query_high[span, :]], axis=1
        ).astype(bf16)

    def score(r, keys):
        return lax.dot_general(queries[r, 0:rows, :], keys, contract, preferred_element_type=f32)

    def weigh(scores, visible):
        scores = jnp.where(visible, scores * scale, low_fill)
        top = jnp.maximum(jnp.max(scores, axis=1, keepdims=True), floor_peak)
        weights = jnp.exp(scores - top)
        return top, jnp.sum(weights, axis=1, keepdims=True), weights.astype(bf16)

    def mix(weights, values):
        return jnp.dot(weights, values, preferred_element_type=f32)

    def add(r, top, amount, mixed):
        span = pl.ds(pl.multiple_of(r * rows, 8), rows)
        old = peak[span, :]
        high = jnp.maximum(old, top)
        keep = jnp.exp(old - high)
        take = jnp.exp(top - high)
        peak[span, :] = high
        norm[span, :] = norm[span, :] * keep + amount * take
        total[span, :] = total[span, :] * jnp.concatenate(
            [keep, keep], axis=1
        ) + mixed * jnp.concatenate([take, take], axis=1)

    fresh_lane = lax.broadcasted_iota(jnp.int32, (1, lines), 1)
    for step in range(-(-requests // n_seq)):
        r = me + step * n_seq

        @pl.when(r < requests)
        def _():
            index = fresh_lane - r * new_count
            seen = (index >= 0) & (index <= token_of)
            top, amount, weights = weigh(score(r, fresh[:, 0:256]), seen)
            add(r, top, amount, mix(weights, fresh[:, 256:512]))

    slot_load.wait()

    def chunk_scores(c):
        load(c).wait()
        numbers = range(c * chunk, (c + 1) * chunk)
        return [score(slots[0, page], buffer[page, :, 0:256]) for page in numbers]

    ahead = chunk_scores(0)
    for c in range(pages // chunk):
        scores = ahead
        if (c + 1) * chunk < pages:
            ahead = chunk_scores(c + 1)
        numbers = range(c * chunk, (c + 1) * chunk)
        weighed = []
        for page, values in zip(numbers, scores):
            length = slots[1, page]
            start = slots[2, page] * page_len
            age = jnp.bitwise_and(length - 1 - start - lane, window - 1)
            limit = jnp.minimum(length - 1, window - 2 - token_of)
            weighed.append(weigh(values, age <= limit))
        mixed = [
            mix(weights, buffer[page, :, 256:512])
            for page, (top, amount, weights) in zip(numbers, weighed)
        ]
        for page, (top, amount, weights), values in zip(numbers, weighed, mixed):
            add(slots[0, page], top, amount, values)

    half = requests // 2
    core = me % 2
    for side, out in ((core, mine), (1 - core, theirs)):
        logs = []
        for k in range(half):
            span = pl.ds(pl.multiple_of((side * half + k) * rows, 8), rows)
            amount = norm[span, :]
            some = amount > 0.0
            safe = jnp.where(some, amount, 1.0)
            logs.append(jnp.where(some, peak[span, :] + jnp.log(safe), low_fill))
            inverse = jnp.where(some, 1.0 / safe, 0.0)
            total[span, :] = total[span, :] * jnp.concatenate([inverse, inverse], axis=1)
        span = pl.ds(pl.multiple_of(side * half * rows, 8), half * rows)
        out[0 : half * rows, :] = total[span, :].astype(bf16)
        out[half * rows : half * rows + 16, :] = pack_logs(logs, rows).astype(bf16)


def attention(dims, slots, cosine, sine, pieces, pool):
    requests, new_count, heads, pages, page_len, window, chunk, n_seq = dims
    part_columns = pieces[0].shape[-1]
    lines = requests * new_count
    rows = new_count * heads
    vmem = pl.BlockSpec(memory_space=pltpu.VMEM)
    pack = jax.ShapeDtypeStruct((requests // 2 * rows + 16, 256), bf16)
    return pl.pallas_call(
        functools.partial(attention_kernel, dims, len(pieces)),
        out_shape=(pack, pack, jax.ShapeDtypeStruct((requests * new_count, 512), bf16)),
        in_specs=[pl.BlockSpec(memory_space=pl.ANY), vmem, vmem]
        + [vmem] * len(pieces)
        + [pl.BlockSpec(memory_space=pltpu.HBM)],
        out_specs=(vmem, vmem, vmem),
        scratch_shapes=[
            pltpu.VMEM(pool.shape, bf16),
            pltpu.VMEM((n_seq, lines, part_columns), bf16),
            pltpu.VMEM((lines, n_seq * part_columns), bf16),
            pltpu.VMEM((requests * rows, 128), f32),
            pltpu.VMEM((requests * rows, 128), f32),
            pltpu.VMEM((requests, -(-rows // 16) * 16, 256), bf16),
            pltpu.VMEM((requests * rows, 128), f32),
            pltpu.VMEM((requests * rows, 128), f32),
            pltpu.VMEM((requests * rows, 256), f32),
            pltpu.SMEM(slots.shape, jnp.int32),
            pltpu.SemaphoreType.DMA,
            pltpu.SemaphoreType.DMA((pages // chunk,)),
        ],
        compiler_params=pltpu.CompilerParams(vmem_limit_bytes=20 * 1024 * 1024),
        cost_estimate=pl.CostEstimate(flops=0, bytes_accessed=1024, transcendentals=0),
        name="page_attention",
    )(slots, cosine, sine, *pieces, pool)


def project_kernel(count, joined, mine, other, *refs):
    blocks, out, scratch = refs[:count], refs[count], refs[count + 1]
    core, plane = lax.axis_index("seq") % 2, lax.axis_index("dp")
    low = jnp.where(core == 0, mine[...], other[...])
    high = jnp.where(core == 0, other[...], mine[...])
    attended = jnp.concatenate([low, high], axis=0)
    if joined:
        rows = blocks[0].shape[0]
        for k, block in enumerate(blocks):
            span = pl.ds(pl.multiple_of((plane ^ k) * rows, 16), rows)
            scratch[span, :] = block[...]
        out[...] = lax.dot_general(
            attended, scratch[...], contract, preferred_element_type=f32
        ).astype(bf16)
        return
    products = [
        lax.dot_general(attended, block[...], contract, preferred_element_type=f32)
        for block in blocks
    ]
    columns = []
    for j in range(count):
        column = products[0]
        for k in range(1, count):
            column = jnp.where((plane ^ k) == j, products[k], column)
        columns.append(column)
    out[...] = jnp.concatenate(columns, axis=1).astype(bf16)


def project_out(mine, other, blocks):
    vmem = pl.BlockSpec(memory_space=pltpu.VMEM)
    rows, width = blocks[0].shape
    total = len(blocks) * rows
    return pl.pallas_call(
        functools.partial(project_kernel, len(blocks), rows % 16 == 0),
        out_shape=jax.ShapeDtypeStruct((2 * mine.shape[0], total), bf16),
        in_specs=[vmem] * (2 + len(blocks)),
        out_specs=vmem,
        scratch_shapes=[pltpu.VMEM((-(-total // 16) * 16, width), bf16)],
        compiler_params=pltpu.CompilerParams(vmem_limit_bytes=8 * 1024 * 1024),
        name="project_out",
    )(mine, other, *blocks)


def fetch_kernel(parts, gate_up, down, after, gates, downs, token, sems):
    units = down.shape[0]
    size = units // parts
    copies = []
    for i in range(parts):
        span = pl.ds(i * size, size)
        copies.append(pltpu.make_async_copy(gate_up.at[0, span], gates.at[0, span], sems.at[0, i]))
        copies.append(pltpu.make_async_copy(gate_up.at[1, span], gates.at[1, span], sems.at[1, i]))
        copies.append(pltpu.make_async_copy(down.at[span], downs.at[span], sems.at[2, i]))
    for copy in copies:
        copy.start()
    token[...] = jnp.zeros(token.shape, f32)
    for copy in copies:
        copy.wait()


def fetch_weights(gate_up, down, after):
    parts = max(c for c in (1, 2, 3, 4) if down.shape[0] % (16 * c) == 0)
    hbm = pl.BlockSpec(memory_space=pltpu.HBM)
    anywhere = pl.BlockSpec(memory_space=pl.ANY)
    return pl.pallas_call(
        functools.partial(fetch_kernel, parts),
        out_shape=(
            jax.ShapeDtypeStruct(gate_up.shape, bf16),
            jax.ShapeDtypeStruct(down.shape, bf16),
            jax.ShapeDtypeStruct((8, 128), f32),
        ),
        in_specs=[hbm, hbm, anywhere],
        out_specs=(anywhere, anywhere, pl.BlockSpec(memory_space=pltpu.VMEM)),
        scratch_shapes=[pltpu.SemaphoreType.DMA((3, parts))],
        compiler_params=pltpu.CompilerParams(vmem_limit_bytes=2 * 1024 * 1024),
        cost_estimate=pl.CostEstimate(
            flops=0, bytes_accessed=2 * (gate_up.size + down.size), transcendentals=0
        ),
        name="fetch_weights",
    )(
        pltpu.with_memory_space_constraint(gate_up, pltpu.HBM),
        pltpu.with_memory_space_constraint(down, pltpu.HBM),
        after,
    )


def mlp_kernel(chunk, pieces, stream, gain, gates, downs, *refs):
    heads_out, refs = refs[:pieces], refs[pieces:]
    keep, give, kept_residual, residual, total, heads_scratch = refs
    units, width = downs.shape
    me = lax.axis_index("seq")
    heads_out = place_pieces(me, heads_out, heads_scratch)
    count = units // chunk
    gathered = jnp.concatenate(
        [heads_out[i].astype(f32) for i in range(heads_out.shape[0])], axis=1
    )
    summed = stream[...].astype(f32) + gathered
    residual[...] = summed.astype(bf16).astype(f32)
    floats = residual[...]
    spread = lax.rsqrt(jnp.mean(floats * floats, axis=-1, keepdims=True) + 1e-06)
    inputs = (floats * spread * gain[...]).astype(bf16)
    root = (2.0 / 3.141592653589793) ** 0.5

    def rise(c):
        span = slice(c * chunk, (c + 1) * chunk)
        gate = lax.dot_general(inputs, gates[0, span, :], contract, preferred_element_type=f32)
        up = lax.dot_general(inputs, gates[1, span, :], contract, preferred_element_type=f32)
        inner = root * (gate + 0.044715 * (gate * gate * gate))
        return (0.5 * gate * (1.0 + jnp.tanh(inner)) * up).astype(bf16)

    def fall(c, hidden):
        span = slice(c * chunk, (c + 1) * chunk)
        product = jnp.dot(hidden, downs[span, :], preferred_element_type=f32)
        if c == 0:
            total[...] = product
        else:
            total[...] += product

    before = rise(0)
    for c in range(1, count):
        after = rise(c)
        fall(c - 1, before)
        before = after
    fall(count - 1, before)
    half = total.shape[0] // 2
    core = me % 2
    mine = pl.ds(pl.multiple_of(core * half, 8), half)
    keep[...] = total[mine, :]
    kept_residual[...] = residual[mine, :].astype(bf16)
    give[...] = total[pl.ds(pl.multiple_of((1 - core) * half, 8), half), :].astype(bf16)


def feed_forward(n_seq, stream, heads_out, gain, gates, downs):
    lines, width = stream.shape
    units = downs.shape[0]
    chunk = max(c for c in range(16, 512, 16) if units % c == 0)
    vmem = pl.BlockSpec(memory_space=pltpu.VMEM)
    return pl.pallas_call(
        functools.partial(mlp_kernel, chunk, len(heads_out)),
        out_shape=(
            jax.ShapeDtypeStruct((lines // 2, width), f32),
            jax.ShapeDtypeStruct((lines // 2, width), bf16),
            jax.ShapeDtypeStruct((lines // 2, width), bf16),
        ),
        in_specs=[vmem] * (4 + len(heads_out)),
        out_specs=(vmem, vmem, vmem),
        scratch_shapes=[
            pltpu.VMEM((lines, width), f32),
            pltpu.VMEM((lines, width), f32),
            pltpu.VMEM((n_seq, lines, width // n_seq), bf16),
        ],
        compiler_params=pltpu.CompilerParams(vmem_limit_bytes=12 * 1024 * 1024),
        name="feed_forward",
    )(stream, gain.reshape(1, width), gates, downs, *heads_out)


def body(
    n_dp,
    n_seq,
    tokens,
    attn_gain,
    qkv_weight,
    out_weight,
    mlp_gain,
    gate_up,
    down_weight,
    kv_pool,
    cache_len,
    page_table,
):
    seq_index = lax.axis_index("seq")
    dp_index = lax.axis_index("dp")
    core = seq_index % 2
    chips = n_seq // 2
    requests, new_count, width = tokens.shape
    pages, page_len, pair_width = kv_pool.shape
    head_dim = pair_width // 2
    heads = out_weight.shape[1] // head_dim
    page_count = page_table.shape[1]
    window = page_count * page_len
    lines = requests * new_count
    half = lines // 2
    rows = new_count * heads

    def ordered(mine, other, axis=0):
        return jnp.where(
            core == 0,
            jnp.concatenate([mine, other], axis=axis),
            jnp.concatenate([other, mine], axis=axis),
        )

    stream = tokens.reshape(lines, width)
    partner_weight = swap(qkv_weight, "dp", n_dp, 1)
    far = list(range(2, n_dp, 2))
    quarter_lines = lines // 4
    quarter_index = seq_index % 4
    some = requests // 4
    my_quarter = lax.dynamic_slice_in_dim(tokens, quarter_index * some, some)
    far_parts = jnp.concatenate([swap(my_quarter, "dp", n_dp, k) for k in far], axis=0)
    cache_len, page_table, far_parts = lax.optimization_barrier((cache_len, page_table, far_parts))
    far_pairs = [far_parts, swap(far_parts, "seq", n_seq, 2)]
    far_mine = jnp.concatenate(far_pairs, axis=0)
    far_other = swap(far_mine, "seq", n_seq, 1).reshape(-1, width)
    far_mine = far_mine.reshape(-1, width)
    held_pool = pltpu.with_memory_space_constraint(kv_pool, pltpu.HBM)
    groups = [stream]
    stride = len(far) * quarter_lines
    for i in range(len(far)):
        for source in (far_mine, far_other):
            for start in (i * quarter_lines, stride + i * quarter_lines):
                groups.append(source[start : start + quarter_lines])
    normed = rms_norm(jnp.concatenate(groups, axis=0), attn_gain).astype(bf16)
    by_mine = lax.dot_general(normed, qkv_weight, contract, preferred_element_type=f32)
    by_partner = lax.dot_general(normed, partner_weight, contract, preferred_element_type=f32)
    products = jnp.where(
        dp_index % 2 == 0,
        jnp.concatenate([by_mine, by_partner], axis=1),
        jnp.concatenate([by_partner, by_mine], axis=1),
    ).astype(bf16)
    out_early, products = lax.optimization_barrier((out_weight, products))
    out_blocks = {k: swap(out_early, "dp", n_dp, k) for k in [1, *far]}
    blocks = [products[:lines]]
    for i, k in enumerate(far):
        back = swap(products[(i + 1) * lines : (i + 2) * lines], "dp", n_dp, k)
        pieces = {
            m: back[n * quarter_lines : (n + 1) * quarter_lines] for n, m in enumerate((0, 2, 1, 3))
        }
        natural = []
        for j in range(4):
            piece = pieces[0]
            for m in (1, 2, 3):
                piece = jnp.where((quarter_index ^ m) == j, pieces[m], piece)
            natural.append(piece)
        blocks.append(jnp.concatenate(natural, axis=0))
    pair = dp_index // 2
    columns = []
    for j in range(n_dp // 2):
        block = blocks[0]
        for k in range(1, n_dp // 2):
            block = jnp.where((pair ^ k) == j, blocks[k], block)
        columns.append(block)
    pieces = gather_pieces(jnp.concatenate(columns, axis=1), n_seq)
    out_blocks[0] = out_weight

    positions_int = cache_len[:, None] + jnp.arange(new_count, dtype=jnp.int32)[None, :]
    quarter = head_dim // 4
    inverse = 10000.0 ** (-jnp.arange(quarter).astype(f32) / quarter)
    angles = positions_int.reshape(lines, 1).astype(f32) * inverse
    cosine = jnp.cos(angles)
    sine = jnp.sin(angles)
    cosine = jnp.concatenate([cosine, cosine], axis=1)
    sine = jnp.concatenate([-sine, sine], axis=1)
    slot_ids = seq_index * pages + jnp.arange(pages, dtype=jnp.int32)
    matches = page_table[None, :, :] == slot_ids[:, None, None]
    number = jnp.arange(page_count, dtype=jnp.int32)[None, None, :]
    owner = jnp.arange(requests, dtype=jnp.int32)[None, :, None]
    slots = jnp.stack(
        [
            jnp.sum(jnp.where(matches, owner, 0), axis=(1, 2)),
            jnp.sum(jnp.where(matches, cache_len[None, :, None], 0), axis=(1, 2)),
            jnp.sum(jnp.where(matches, number, 0), axis=(1, 2)),
        ]
    )
    ends = jnp.stack([cache_len, cache_len + (new_count - 1)], axis=1)
    end_page = (ends // page_len) % page_count
    end_block = (ends % page_len) // 16
    hit = end_page[:, :, None] == jnp.arange(page_count, dtype=jnp.int32)[None, None, :]
    end_slot = jnp.sum(jnp.where(hit, page_table[:, None, :], 0), axis=2) - seq_index * pages
    good = (end_slot >= 0) & (end_slot < pages)
    same = (end_page[:, 0] == end_page[:, 1]) & (end_block[:, 0] == end_block[:, 1])
    good = good & jnp.stack([jnp.ones_like(same), ~same], axis=1)
    patches = jnp.stack(
        [
            jnp.where(good, end_slot, -1).reshape(-1),
            end_block.reshape(-1),
            end_page.reshape(-1),
            jnp.repeat(cache_len, 2),
        ]
    )

    dims = (requests, new_count, heads, pages, page_len, window, min(16, pages), n_seq)
    slots, patches = lax.optimization_barrier((slots, patches))
    mine, theirs, fresh = attention(dims, slots, cosine, sine, pieces, held_pool)
    written_pool = write_pool(dims, patches, fresh, held_pool)

    side = requests // 2
    merged = merge_pair(mine, swap(theirs, "seq", n_seq, 1), side, rows)
    merged, *early = lax.optimization_barrier((merged, *[out_blocks[k] for k in [1, *far]]))
    for k, block in zip([1, *far], early):
        out_blocks[k] = block
    for k in far:
        out_blocks[k ^ 1] = swap(out_blocks[k], "dp", n_dp, 1)
    packs = [merged] + [swap(merged, "seq", n_seq, 2 * c) for c in range(1, chips)]
    gates, downs, token = fetch_weights(gate_up, down_weight, merged)
    packs, late = lax.optimization_barrier((packs, [out_blocks[k ^ 1] for k in far]))
    for k, block in zip(far, late):
        out_blocks[k ^ 1] = block
    attended_half = merge_final(packs, token, side, rows, heads)
    heads_part = project_out(
        attended_half,
        swap(attended_half, "seq", n_seq, 1),
        [out_blocks[k] for k in range(n_dp)],
    )
    heads_out = gather_pieces(heads_part, n_seq)
    keep, give, my_residual = feed_forward(n_seq, stream, heads_out, mlp_gain, gates, downs)
    chip_sum = (keep + swap(give, "seq", n_seq, 1).astype(f32)).astype(bf16)
    terms = [chip_sum] + [swap(chip_sum, "seq", n_seq, 2 * c) for c in range(1, chips)]
    terms, written_pool = lax.optimization_barrier((terms, written_pool))
    full_half = tree_sum([term.astype(f32) for term in terms])
    out_half = (my_residual.astype(f32) + full_half).astype(bf16)
    out_half = out_half.reshape(requests // 2, new_count, width)
    return ordered(out_half, swap(out_half, "seq", n_seq, 1)), written_pool


def solution(mesh):
    in_specs = (
        P("dp", None, None),
        P(),
        P(("seq", "dp"), None),
        P(("seq", "dp"), None),
        P(),
        P(None, "seq", None),
        P("seq", None),
        P(("dp", "seq"), None, None),
        P("dp"),
        P("dp", None),
    )
    out_specs = (P("dp", None, None), P(("dp", "seq"), None, None))
    return jax.shard_map(
        functools.partial(body, mesh.shape["dp"], mesh.shape["seq"]),
        mesh=mesh,
        in_specs=in_specs,
        out_specs=out_specs,
        check_vma=False,
    )
```

```python
import functools

import jax
import jax.numpy as jnp
from jax import lax
from jax.experimental import pallas as pl
from jax.experimental.pallas import tpu as pltpu
from jax.sharding import PartitionSpec as P

f32 = jnp.float32
bf16 = jnp.bfloat16
low_fill = -1e30
floor_peak = -1e29
contract = (((1,), (1,)), ((), ()))


def rms_norm(values, gains):
    floats = values.astype(f32)
    return floats * lax.rsqrt(jnp.mean(floats * floats, axis=-1, keepdims=True) + 1e-06) * gains


def swap(values, axis, size, mask):
    return lax.ppermute(values, axis, [(i, i ^ mask) for i in range(size)])


def tree_sum(terms):
    while len(terms) > 1:
        terms = [terms[i] + terms[i + 1] for i in range(0, len(terms), 2)]
    return terms[0]


def gather_pieces(values, n_seq):
    if n_seq > 8:
        return [lax.all_gather(values, "seq", axis=0)]
    pieces = {0: values}
    for mask in range(2, n_seq, 2):
        pieces[mask] = swap(values, "seq", n_seq, mask)
    for mask in range(0, n_seq, 2):
        pieces[mask + 1] = swap(pieces[mask], "seq", n_seq, 1)
    return [pieces[mask] for mask in range(n_seq)]


def place_pieces(me, refs, scratch):
    if len(refs) == 1:
        return refs[0]
    for mask, ref in enumerate(refs):
        scratch[jnp.bitwise_xor(me, mask)] = ref[...]
    return scratch


def write_kernel(dims, parts, patch_source, fresh, source, target, buffer, patches, *sems):
    patch_sem, in_sems, out_sems = sems
    requests, new_count, heads, pages, page_len, window, chunk, n_seq = dims
    lines = requests * new_count
    count = pages // parts
    spans = [pl.ds(i * count, count) for i in range(parts)]
    loads = [
        pltpu.make_async_copy(source.at[span], buffer.at[span], in_sems.at[i])
        for i, span in enumerate(spans)
    ]
    stores = [
        pltpu.make_async_copy(buffer.at[span], target.at[span], out_sems.at[i])
        for i, span in enumerate(spans)
    ]
    patch_load = pltpu.make_async_copy(patch_source, patches, patch_sem)
    patch_load.start()
    for load in loads:
        load.start()
    patch_load.wait()

    def write_patch(part, i):
        slot = patches[0, i]

        @pl.when((slot >= part * count) & (slot < (part + 1) * count))
        def _():
            r = i // 2
            row = pl.multiple_of(patches[1, i] * 16, 16)
            old = buffer[slot, pl.ds(row, 16), :]
            first = patches[2, i] * page_len + row - patches[3, i]
            line = lax.broadcasted_iota(jnp.int32, (16, lines), 0)
            token = jnp.bitwise_and(first + line, window - 1)
            column = lax.broadcasted_iota(jnp.int32, (16, lines), 1)
            pick = (token < new_count) & (column == r * new_count + token)
            new = jnp.dot(pick.astype(f32).astype(bf16), fresh[...], preferred_element_type=f32)
            row_token = jnp.bitwise_and(
                first + lax.broadcasted_iota(jnp.int32, (16, 1), 0), window - 1
            )
            buffer[slot, pl.ds(row, 16), :] = jnp.where(
                row_token < new_count, new, old.astype(f32)
            ).astype(bf16)

    for part, (load, store) in enumerate(zip(loads, stores)):
        load.wait()
        pl.loop(0, 2 * requests)(functools.partial(write_patch, part))
        store.start()
    for store in stores:
        store.wait()


def write_pool(dims, patches, fresh, kv_pool):
    parts = 4
    hbm = pl.BlockSpec(memory_space=pltpu.HBM)
    return pl.pallas_call(
        functools.partial(write_kernel, dims, parts),
        out_shape=pltpu.HBM(kv_pool.shape, kv_pool.dtype),
        in_specs=[
            pl.BlockSpec(memory_space=pl.ANY),
            pl.BlockSpec(memory_space=pltpu.VMEM),
            hbm,
        ],
        out_specs=hbm,
        scratch_shapes=[
            pltpu.VMEM(kv_pool.shape, kv_pool.dtype),
            pltpu.SMEM(patches.shape, jnp.int32),
            pltpu.SemaphoreType.DMA,
            pltpu.SemaphoreType.DMA((parts,)),
            pltpu.SemaphoreType.DMA((parts,)),
        ],
        compiler_params=pltpu.CompilerParams(vmem_limit_bytes=12 * 1024 * 1024),
        cost_estimate=pl.CostEstimate(
            flops=0, bytes_accessed=2 * kv_pool.size * 2, transcendentals=0
        ),
        name="write_pool",
    )(patches, fresh, kv_pool)


def split_three(values):
    high = values.astype(bf16).astype(f32)
    middle = (values - high).astype(bf16).astype(f32)
    low = (values - high - middle).astype(bf16).astype(f32)
    return high, middle, low


def diagonal(rows):
    return lax.broadcasted_iota(jnp.int32, (rows, 128), 0) == lax.broadcasted_iota(
        jnp.int32, (rows, 128), 1
    )


def pack_logs(columns, rows):
    eye = diagonal(rows)
    lines = [
        jnp.sum(jnp.where(eye, jnp.broadcast_to(c, (rows, 128)), 0.0), axis=0, keepdims=True)
        for c in columns
    ]
    lines += [jnp.zeros((1, 128), f32)] * (8 - len(lines))
    high, middle, low = split_three(jnp.concatenate(lines, axis=0))
    return jnp.concatenate(
        [
            jnp.concatenate([high, middle], axis=1),
            jnp.concatenate([low, jnp.zeros((8, 128), f32)], axis=1),
        ],
        axis=0,
    )


def unpack_logs(block):
    return block[0:8, 0:128] + block[0:8, 128:256] + block[8:16, 0:128]


def merge_parts(packs, requests, rows):
    total = requests * rows
    bodies = [ref[...].astype(f32) for ref in packs]
    logs = [unpack_logs(body[total : total + 16]) for body in bodies]
    eye = diagonal(rows)
    results, columns = [], []
    for r in range(requests):
        cols = [
            jnp.sum(
                jnp.where(eye, jnp.broadcast_to(log[r : r + 1, :], (rows, 128)), 0.0),
                axis=1,
                keepdims=True,
            )
            for log in logs
        ]
        top = functools.reduce(jnp.maximum, cols)
        scales = [jnp.exp(c - top) for c in cols]
        norm = functools.reduce(jnp.add, scales)
        parts = [
            body[r * rows : (r + 1) * rows] * scale for body, scale in zip(bodies, scales)
        ]
        results.append(functools.reduce(jnp.add, parts) / norm)
        columns.append(top + jnp.log(norm))
    return results, columns


def pair_kernel(requests, rows, mine, other, out):
    results, columns = merge_parts([mine, other], requests, rows)
    body = jnp.concatenate(results + [pack_logs(columns, rows)], axis=0)
    out[...] = body.astype(bf16)


def merge_pair(mine, other, requests, rows):
    return pl.pallas_call(
        functools.partial(pair_kernel, requests, rows),
        out_shape=jax.ShapeDtypeStruct(mine.shape, bf16),
        in_specs=[pl.BlockSpec(memory_space=pltpu.VMEM)] * 2,
        out_specs=pl.BlockSpec(memory_space=pltpu.VMEM),
        compiler_params=pltpu.CompilerParams(vmem_limit_bytes=8 * 1024 * 1024),
        name="merge_pair",
    )(mine, other)


def final_kernel(count, requests, rows, heads, *refs):
    packs, out, scratch_low, scratch_high = refs[:count], refs[count + 1], refs[-2], refs[-1]
    results, unused = merge_parts(packs, requests, rows)
    body = jnp.concatenate(results, axis=0)
    scratch_low[...] = body[:, 0:128]
    scratch_high[...] = body[:, 128:256]
    lines = requests * rows // heads
    for h in range(heads):
        low = scratch_low[pl.ds(h, lines, stride=heads), :]
        high = scratch_high[pl.ds(h, lines, stride=heads), :]
        out[:, h * 256 : (h + 1) * 256] = jnp.concatenate([low, high], axis=1).astype(bf16)


def merge_final(packs, token, requests, rows, heads):
    lines = requests * rows // heads
    return pl.pallas_call(
        functools.partial(final_kernel, len(packs), requests, rows, heads),
        out_shape=jax.ShapeDtypeStruct((lines, heads * 256), bf16),
        in_specs=[pl.BlockSpec(memory_space=pltpu.VMEM)] * (len(packs) + 1),
        out_specs=pl.BlockSpec(memory_space=pltpu.VMEM),
        scratch_shapes=[pltpu.VMEM((requests * rows, 128), f32)] * 2,
        compiler_params=pltpu.CompilerParams(vmem_limit_bytes=8 * 1024 * 1024),
        name="merge_final",
    )(*packs, token)


def attention_kernel(dims, count, slot_source, cosine, sine, *refs):
    requests, new_count, heads, pages, page_len, window, chunk, n_seq = dims
    pieces, refs = refs[:count], refs[count:]
    pool, mine, theirs, fresh, buffer, gathered, projected = refs[:7]
    query_low, query_high, queries, peak, norm, total, slots, slot_sem, in_sems = refs[7:]
    slot_load = pltpu.make_async_copy(slot_source, slots, slot_sem)
    slot_load.start()
    rows = new_count * heads
    lines = requests * new_count

    def load(c):
        span = pl.ds(c * chunk, chunk)
        return pltpu.make_async_copy(pool.at[span], buffer.at[span], in_sems.at[c])

    for c in range(pages // chunk):
        load(c).start()

    me = lax.axis_index("seq")
    ordered_pieces = place_pieces(me, pieces, gathered)
    part_columns = projected.shape[1] // n_seq
    for i in range(n_seq):
        projected[:, i * part_columns : (i + 1) * part_columns] = ordered_pieces[i]
    cos = cosine[...]
    sin = sine[...]

    def turned(block):
        x = projected[:, block * 128 : (block + 1) * 128].astype(f32)
        return (x * cos + pltpu.roll(x, 64, 1) * sin).astype(bf16).astype(f32)

    for h in range(heads):
        query_low[pl.ds(h, lines, stride=heads), :] = turned(2 * h)
        query_high[pl.ds(h, lines, stride=heads), :] = projected[
            :, h * 256 + 128 : h * 256 + 256
        ].astype(f32)
    fresh[:, 0:128] = turned(2 * heads).astype(bf16)
    fresh[:, 128:512] = projected[:, heads * 256 + 128 : heads * 256 + 512]

    peak[...] = jnp.full(peak.shape, floor_peak, f32)
    norm[...] = jnp.zeros(norm.shape, f32)
    total[...] = jnp.zeros(total.shape, f32)

    token_of = lax.broadcasted_iota(jnp.int32, (rows, 1), 0) // heads
    lane = lax.broadcasted_iota(jnp.int32, (1, page_len), 1)
    scale = 256.0 ** (-0.5)

    for r in range(requests):
        span = slice(r * rows, (r + 1) * rows)
        queries[r, 0:rows, :] = jnp.concatenate(
            [query_low[span, :], query_high[span, :]], axis=1
        ).astype(bf16)

    def score(r, keys):
        return lax.dot_general(queries[r, 0:rows, :], keys, contract, preferred_element_type=f32)

    def weigh(scores, visible):
        scores = jnp.where(visible, scores * scale, low_fill)
        top = jnp.maximum(jnp.max(scores, axis=1, keepdims=True), floor_peak)
        weights = jnp.exp(scores - top)
        return top, jnp.sum(weights, axis=1, keepdims=True), weights.astype(bf16)

    def mix(weights, values):
        return jnp.dot(weights, values, preferred_element_type=f32)

    def add(r, top, amount, mixed):
        span = pl.ds(pl.multiple_of(r * rows, 8), rows)
        old = peak[span, :]
        high = jnp.maximum(old, top)
        keep = jnp.exp(old - high)
        take = jnp.exp(top - high)
        peak[span, :] = high
        norm[span, :] = norm[span, :] * keep + amount * take
        total[span, :] = total[span, :] * jnp.concatenate(
            [keep, keep], axis=1
        ) + mixed * jnp.concatenate([take, take], axis=1)

    fresh_lane = lax.broadcasted_iota(jnp.int32, (1, lines), 1)
    for step in range(-(-requests // n_seq)):
        r = me + step * n_seq

        @pl.when(r < requests)
        def _():
            index = fresh_lane - r * new_count
            seen = (index >= 0) & (index <= token_of)
            top, amount, weights = weigh(score(r, fresh[:, 0:256]), seen)
            add(r, top, amount, mix(weights, fresh[:, 256:512]))

    slot_load.wait()

    def chunk_scores(c):
        load(c).wait()
        numbers = range(c * chunk, (c + 1) * chunk)
        return [score(slots[0, page], buffer[page, :, 0:256]) for page in numbers]

    ahead = chunk_scores(0)
    for c in range(pages // chunk):
        scores = ahead
        if (c + 1) * chunk < pages:
            ahead = chunk_scores(c + 1)
        numbers = range(c * chunk, (c + 1) * chunk)
        weighed = []
        for page, values in zip(numbers, scores):
            length = slots[1, page]
            start = slots[2, page] * page_len
            age = jnp.bitwise_and(length - 1 - start - lane, window - 1)
            limit = jnp.minimum(length - 1, window - 2 - token_of)
            weighed.append(weigh(values, age <= limit))
        mixed = [
            mix(weights, buffer[page, :, 256:512])
            for page, (top, amount, weights) in zip(numbers, weighed)
        ]
        for page, (top, amount, weights), values in zip(numbers, weighed, mixed):
            add(slots[0, page], top, amount, values)

    half = requests // 2
    core = me % 2
    for side, out in ((core, mine), (1 - core, theirs)):
        logs = []
        for k in range(half):
            span = pl.ds(pl.multiple_of((side * half + k) * rows, 8), rows)
            amount = norm[span, :]
            some = amount > 0.0
            safe = jnp.where(some, amount, 1.0)
            logs.append(jnp.where(some, peak[span, :] + jnp.log(safe), low_fill))
            inverse = jnp.where(some, 1.0 / safe, 0.0)
            total[span, :] = total[span, :] * jnp.concatenate([inverse, inverse], axis=1)
        span = pl.ds(pl.multiple_of(side * half * rows, 8), half * rows)
        out[0 : half * rows, :] = total[span, :].astype(bf16)
        out[half * rows : half * rows + 16, :] = pack_logs(logs, rows).astype(bf16)


def attention(dims, slots, cosine, sine, pieces, pool):
    requests, new_count, heads, pages, page_len, window, chunk, n_seq = dims
    part_columns = pieces[0].shape[-1]
    lines = requests * new_count
    rows = new_count * heads
    vmem = pl.BlockSpec(memory_space=pltpu.VMEM)
    pack = jax.ShapeDtypeStruct((requests // 2 * rows + 16, 256), bf16)
    return pl.pallas_call(
        functools.partial(attention_kernel, dims, len(pieces)),
        out_shape=(pack, pack, jax.ShapeDtypeStruct((requests * new_count, 512), bf16)),
        in_specs=[pl.BlockSpec(memory_space=pl.ANY), vmem, vmem]
        + [vmem] * len(pieces)
        + [pl.BlockSpec(memory_space=pltpu.HBM)],
        out_specs=(vmem, vmem, vmem),
        scratch_shapes=[
            pltpu.VMEM(pool.shape, bf16),
            pltpu.VMEM((n_seq, lines, part_columns), bf16),
            pltpu.VMEM((lines, n_seq * part_columns), bf16),
            pltpu.VMEM((requests * rows, 128), f32),
            pltpu.VMEM((requests * rows, 128), f32),
            pltpu.VMEM((requests, -(-rows // 16) * 16, 256), bf16),
            pltpu.VMEM((requests * rows, 128), f32),
            pltpu.VMEM((requests * rows, 128), f32),
            pltpu.VMEM((requests * rows, 256), f32),
            pltpu.SMEM(slots.shape, jnp.int32),
            pltpu.SemaphoreType.DMA,
            pltpu.SemaphoreType.DMA((pages // chunk,)),
        ],
        compiler_params=pltpu.CompilerParams(vmem_limit_bytes=20 * 1024 * 1024),
        cost_estimate=pl.CostEstimate(flops=0, bytes_accessed=1024, transcendentals=0),
        name="page_attention",
    )(slots, cosine, sine, *pieces, pool)


def project_kernel(count, joined, mine, other, *refs):
    blocks, out, scratch = refs[:count], refs[count], refs[count + 1]
    core, plane = lax.axis_index("seq") % 2, lax.axis_index("dp")
    low = jnp.where(core == 0, mine[...], other[...])
    high = jnp.where(core == 0, other[...], mine[...])
    attended = jnp.concatenate([low, high], axis=0)
    if joined:
        rows = blocks[0].shape[0]
        for k, block in enumerate(blocks):
            span = pl.ds(pl.multiple_of((plane ^ k) * rows, 16), rows)
            scratch[span, :] = block[...]
        out[...] = lax.dot_general(
            attended, scratch[...], contract, preferred_element_type=f32
        ).astype(bf16)
        return
    products = [
        lax.dot_general(attended, block[...], contract, preferred_element_type=f32)
        for block in blocks
    ]
    columns = []
    for j in range(count):
        column = products[0]
        for k in range(1, count):
            column = jnp.where((plane ^ k) == j, products[k], column)
        columns.append(column)
    out[...] = jnp.concatenate(columns, axis=1).astype(bf16)


def project_out(mine, other, blocks):
    vmem = pl.BlockSpec(memory_space=pltpu.VMEM)
    rows, width = blocks[0].shape
    total = len(blocks) * rows
    return pl.pallas_call(
        functools.partial(project_kernel, len(blocks), rows % 16 == 0),
        out_shape=jax.ShapeDtypeStruct((2 * mine.shape[0], total), bf16),
        in_specs=[vmem] * (2 + len(blocks)),
        out_specs=vmem,
        scratch_shapes=[pltpu.VMEM((-(-total // 16) * 16, width), bf16)],
        compiler_params=pltpu.CompilerParams(vmem_limit_bytes=8 * 1024 * 1024),
        name="project_out",
    )(mine, other, *blocks)


def fetch_kernel(parts, gate_up, down, after, gates, downs, token, sems):
    units = down.shape[0]
    size = units // parts
    copies = []
    for i in range(parts):
        span = pl.ds(i * size, size)
        copies.append(pltpu.make_async_copy(gate_up.at[0, span], gates.at[0, span], sems.at[0, i]))
        copies.append(pltpu.make_async_copy(gate_up.at[1, span], gates.at[1, span], sems.at[1, i]))
        copies.append(pltpu.make_async_copy(down.at[span], downs.at[span], sems.at[2, i]))
    for copy in copies:
        copy.start()
    token[...] = jnp.zeros(token.shape, f32)
    for copy in copies:
        copy.wait()


def fetch_weights(gate_up, down, after):
    parts = max(c for c in (1, 2, 3, 4) if down.shape[0] % (16 * c) == 0)
    hbm = pl.BlockSpec(memory_space=pltpu.HBM)
    anywhere = pl.BlockSpec(memory_space=pl.ANY)
    return pl.pallas_call(
        functools.partial(fetch_kernel, parts),
        out_shape=(
            jax.ShapeDtypeStruct(gate_up.shape, bf16),
            jax.ShapeDtypeStruct(down.shape, bf16),
            jax.ShapeDtypeStruct((8, 128), f32),
        ),
        in_specs=[hbm, hbm, anywhere],
        out_specs=(anywhere, anywhere, pl.BlockSpec(memory_space=pltpu.VMEM)),
        scratch_shapes=[pltpu.SemaphoreType.DMA((3, parts))],
        compiler_params=pltpu.CompilerParams(vmem_limit_bytes=2 * 1024 * 1024),
        cost_estimate=pl.CostEstimate(
            flops=0, bytes_accessed=2 * (gate_up.size + down.size), transcendentals=0
        ),
        name="fetch_weights",
    )(
        pltpu.with_memory_space_constraint(gate_up, pltpu.HBM),
        pltpu.with_memory_space_constraint(down, pltpu.HBM),
        after,
    )


def mlp_kernel(chunk, pieces, stream, gain, gates, downs, *refs):
    heads_out, refs = refs[:pieces], refs[pieces:]
    keep, give, kept_residual, residual, total, heads_scratch = refs
    units, width = downs.shape
    me = lax.axis_index("seq")
    heads_out = place_pieces(me, heads_out, heads_scratch)
    count = units // chunk
    gathered = jnp.concatenate(
        [heads_out[i].astype(f32) for i in range(heads_out.shape[0])], axis=1
    )
    summed = stream[...].astype(f32) + gathered
    residual[...] = summed.astype(bf16).astype(f32)
    floats = residual[...]
    spread = lax.rsqrt(jnp.mean(floats * floats, axis=-1, keepdims=True) + 1e-06)
    inputs = (floats * spread * gain[...]).astype(bf16)
    root = (2.0 / 3.141592653589793) ** 0.5

    def rise(c):
        span = slice(c * chunk, (c + 1) * chunk)
        gate = lax.dot_general(inputs, gates[0, span, :], contract, preferred_element_type=f32)
        up = lax.dot_general(inputs, gates[1, span, :], contract, preferred_element_type=f32)
        inner = root * (gate + 0.044715 * (gate * gate * gate))
        return (0.5 * gate * (1.0 + jnp.tanh(inner)) * up).astype(bf16)

    def fall(c, hidden):
        span = slice(c * chunk, (c + 1) * chunk)
        product = jnp.dot(hidden, downs[span, :], preferred_element_type=f32)
        if c == 0:
            total[...] = product
        else:
            total[...] += product

    before = rise(0)
    for c in range(1, count):
        after = rise(c)
        fall(c - 1, before)
        before = after
    fall(count - 1, before)
    half = total.shape[0] // 2
    core = me % 2
    mine = pl.ds(pl.multiple_of(core * half, 8), half)
    keep[...] = total[mine, :]
    kept_residual[...] = residual[mine, :].astype(bf16)
    give[...] = total[pl.ds(pl.multiple_of((1 - core) * half, 8), half), :].astype(bf16)


def feed_forward(n_seq, stream, heads_out, gain, gates, downs):
    lines, width = stream.shape
    units = downs.shape[0]
    chunk = max(c for c in range(16, 512, 16) if units % c == 0)
    vmem = pl.BlockSpec(memory_space=pltpu.VMEM)
    return pl.pallas_call(
        functools.partial(mlp_kernel, chunk, len(heads_out)),
        out_shape=(
            jax.ShapeDtypeStruct((lines // 2, width), f32),
            jax.ShapeDtypeStruct((lines // 2, width), bf16),
            jax.ShapeDtypeStruct((lines // 2, width), bf16),
        ),
        in_specs=[vmem] * (4 + len(heads_out)),
        out_specs=(vmem, vmem, vmem),
        scratch_shapes=[
            pltpu.VMEM((lines, width), f32),
            pltpu.VMEM((lines, width), f32),
            pltpu.VMEM((n_seq, lines, width // n_seq), bf16),
        ],
        compiler_params=pltpu.CompilerParams(vmem_limit_bytes=12 * 1024 * 1024),
        name="feed_forward",
    )(stream, gain.reshape(1, width), gates, downs, *heads_out)


def half_kernel(flip, part, *refs):
    target, sem = refs[-2], refs[-1]
    count = part.shape[0]
    side = jnp.bitwise_xor(lax.axis_index("seq") % 2, flip)
    copy = pltpu.make_async_copy(part, target.at[pl.ds(side * count, count)], sem)
    copy.start()
    copy.wait()


def write_half(flip, part, started=None):
    hbm = pl.BlockSpec(memory_space=pltpu.HBM)
    earlier = [] if started is None else [started]
    return pl.pallas_call(
        functools.partial(half_kernel, flip),
        out_shape=pltpu.HBM((2 * part.shape[0], *part.shape[1:]), part.dtype),
        in_specs=[pl.BlockSpec(memory_space=pltpu.VMEM), *[hbm for _ in earlier]],
        out_specs=hbm,
        scratch_shapes=[pltpu.SemaphoreType.DMA],
        input_output_aliases={} if started is None else {1: 0},
        compiler_params=pltpu.CompilerParams(vmem_limit_bytes=2 * 1024 * 1024),
        cost_estimate=pl.CostEstimate(flops=0, bytes_accessed=4 * part.size, transcendentals=0),
        name="write_half",
    )(part, *earlier)


def body(
    n_dp,
    n_seq,
    tokens,
    attn_gain,
    qkv_weight,
    out_weight,
    mlp_gain,
    gate_up,
    down_weight,
    kv_pool,
    cache_len,
    page_table,
):
    seq_index = lax.axis_index("seq")
    dp_index = lax.axis_index("dp")
    core = seq_index % 2
    chips = n_seq // 2
    requests, new_count, width = tokens.shape
    pages, page_len, pair_width = kv_pool.shape
    head_dim = pair_width // 2
    heads = out_weight.shape[1] // head_dim
    page_count = page_table.shape[1]
    window = page_count * page_len
    lines = requests * new_count
    half = lines // 2
    rows = new_count * heads

    stream = tokens.reshape(lines, width)
    partner_weight = swap(qkv_weight, "dp", n_dp, 1)
    far = list(range(2, n_dp, 2))
    quarter_lines = lines // 4
    quarter_index = seq_index % 4
    some = requests // 4
    my_quarter = lax.dynamic_slice_in_dim(tokens, quarter_index * some, some)
    far_parts = jnp.concatenate([swap(my_quarter, "dp", n_dp, k) for k in far], axis=0)
    cache_len, page_table, far_parts = lax.optimization_barrier((cache_len, page_table, far_parts))
    far_pairs = [far_parts, swap(far_parts, "seq", n_seq, 2)]
    far_mine = jnp.concatenate(far_pairs, axis=0)
    far_other = swap(far_mine, "seq", n_seq, 1).reshape(-1, width)
    far_mine = far_mine.reshape(-1, width)
    held_pool = pltpu.with_memory_space_constraint(kv_pool, pltpu.HBM)
    groups = [stream]
    stride = len(far) * quarter_lines
    for i in range(len(far)):
        for source in (far_mine, far_other):
            for start in (i * quarter_lines, stride + i * quarter_lines):
                groups.append(source[start : start + quarter_lines])
    normed = rms_norm(jnp.concatenate(groups, axis=0), attn_gain).astype(bf16)
    by_mine = lax.dot_general(normed, qkv_weight, contract, preferred_element_type=f32)
    by_partner = lax.dot_general(normed, partner_weight, contract, preferred_element_type=f32)
    products = jnp.where(
        dp_index % 2 == 0,
        jnp.concatenate([by_mine, by_partner], axis=1),
        jnp.concatenate([by_partner, by_mine], axis=1),
    ).astype(bf16)
    out_early, products = lax.optimization_barrier((out_weight, products))
    out_blocks = {k: swap(out_early, "dp", n_dp, k) for k in [1, *far]}
    blocks = [products[:lines]]
    for i, k in enumerate(far):
        back = swap(products[(i + 1) * lines : (i + 2) * lines], "dp", n_dp, k)
        pieces = {
            m: back[n * quarter_lines : (n + 1) * quarter_lines] for n, m in enumerate((0, 2, 1, 3))
        }
        natural = []
        for j in range(4):
            piece = pieces[0]
            for m in (1, 2, 3):
                piece = jnp.where((quarter_index ^ m) == j, pieces[m], piece)
            natural.append(piece)
        blocks.append(jnp.concatenate(natural, axis=0))
    pair = dp_index // 2
    columns = []
    for j in range(n_dp // 2):
        block = blocks[0]
        for k in range(1, n_dp // 2):
            block = jnp.where((pair ^ k) == j, blocks[k], block)
        columns.append(block)
    pieces = gather_pieces(jnp.concatenate(columns, axis=1), n_seq)
    out_blocks[0] = out_weight

    positions_int = cache_len[:, None] + jnp.arange(new_count, dtype=jnp.int32)[None, :]
    quarter = head_dim // 4
    inverse = 10000.0 ** (-jnp.arange(quarter).astype(f32) / quarter)
    angles = positions_int.reshape(lines, 1).astype(f32) * inverse
    cosine = jnp.cos(angles)
    sine = jnp.sin(angles)
    cosine = jnp.concatenate([cosine, cosine], axis=1)
    sine = jnp.concatenate([-sine, sine], axis=1)
    slot_ids = seq_index * pages + jnp.arange(pages, dtype=jnp.int32)
    matches = page_table[None, :, :] == slot_ids[:, None, None]
    number = jnp.arange(page_count, dtype=jnp.int32)[None, None, :]
    owner = jnp.arange(requests, dtype=jnp.int32)[None, :, None]
    slots = jnp.stack(
        [
            jnp.sum(jnp.where(matches, owner, 0), axis=(1, 2)),
            jnp.sum(jnp.where(matches, cache_len[None, :, None], 0), axis=(1, 2)),
            jnp.sum(jnp.where(matches, number, 0), axis=(1, 2)),
        ]
    )
    ends = jnp.stack([cache_len, cache_len + (new_count - 1)], axis=1)
    end_page = (ends // page_len) % page_count
    end_block = (ends % page_len) // 16
    hit = end_page[:, :, None] == jnp.arange(page_count, dtype=jnp.int32)[None, None, :]
    end_slot = jnp.sum(jnp.where(hit, page_table[:, None, :], 0), axis=2) - seq_index * pages
    good = (end_slot >= 0) & (end_slot < pages)
    same = (end_page[:, 0] == end_page[:, 1]) & (end_block[:, 0] == end_block[:, 1])
    good = good & jnp.stack([jnp.ones_like(same), ~same], axis=1)
    patches = jnp.stack(
        [
            jnp.where(good, end_slot, -1).reshape(-1),
            end_block.reshape(-1),
            end_page.reshape(-1),
            jnp.repeat(cache_len, 2),
        ]
    )

    dims = (requests, new_count, heads, pages, page_len, window, min(16, pages), n_seq)
    slots, patches = lax.optimization_barrier((slots, patches))
    mine, theirs, fresh = attention(dims, slots, cosine, sine, pieces, held_pool)
    written_pool = write_pool(dims, patches, fresh, held_pool)

    side = requests // 2
    merged = merge_pair(mine, swap(theirs, "seq", n_seq, 1), side, rows)
    merged, *early = lax.optimization_barrier((merged, *[out_blocks[k] for k in [1, *far]]))
    for k, block in zip([1, *far], early):
        out_blocks[k] = block
    for k in far:
        out_blocks[k ^ 1] = swap(out_blocks[k], "dp", n_dp, 1)
    packs = [merged] + [swap(merged, "seq", n_seq, 2 * c) for c in range(1, chips)]
    gates, downs, token = fetch_weights(gate_up, down_weight, merged)
    packs, late = lax.optimization_barrier((packs, [out_blocks[k ^ 1] for k in far]))
    for k, block in zip(far, late):
        out_blocks[k ^ 1] = block
    attended_half = merge_final(packs, token, side, rows, heads)
    heads_part = project_out(
        attended_half,
        swap(attended_half, "seq", n_seq, 1),
        [out_blocks[k] for k in range(n_dp)],
    )
    heads_out = gather_pieces(heads_part, n_seq)
    keep, give, my_residual = feed_forward(n_seq, stream, heads_out, mlp_gain, gates, downs)
    chip_sum = (keep + swap(give, "seq", n_seq, 1).astype(f32)).astype(bf16)
    terms = [chip_sum] + [swap(chip_sum, "seq", n_seq, 2 * c) for c in range(1, chips)]
    terms, written_pool = lax.optimization_barrier((terms, written_pool))
    full_half = tree_sum([term.astype(f32) for term in terms])
    out_half = (my_residual.astype(f32) + full_half).astype(bf16)
    out_half = out_half.reshape(requests // 2, new_count, width)
    started = write_half(0, out_half)
    layer_out = write_half(1, swap(out_half, "seq", n_seq, 1), started)
    return layer_out, written_pool


def solution(mesh):
    in_specs = (
        P("dp", None, None),
        P(),
        P(("seq", "dp"), None),
        P(("seq", "dp"), None),
        P(),
        P(None, "seq", None),
        P("seq", None),
        P(("dp", "seq"), None, None),
        P("dp"),
        P("dp", None),
    )
    out_specs = (P("dp", None, None), P(("dp", "seq"), None, None))
    return jax.shard_map(
        functools.partial(body, mesh.shape["dp"], mesh.shape["seq"]),
        mesh=mesh,
        in_specs=in_specs,
        out_specs=out_specs,
        check_vma=False,
    )
```

```python
import functools

import jax
import jax.numpy as jnp
from jax import lax
from jax.experimental import pallas as pl
from jax.experimental.pallas import tpu as pltpu
from jax.sharding import PartitionSpec as P

f32 = jnp.float32
bf16 = jnp.bfloat16
low_fill = -1e30
floor_peak = -1e29
contract = (((1,), (1,)), ((), ()))


def rms_norm(values, gains):
    floats = values.astype(f32)
    return floats * lax.rsqrt(jnp.mean(floats * floats, axis=-1, keepdims=True) + 1e-06) * gains


def swap(values, axis, size, mask):
    return lax.ppermute(values, axis, [(i, i ^ mask) for i in range(size)])


def tree_sum(terms):
    while len(terms) > 1:
        terms = [terms[i] + terms[i + 1] for i in range(0, len(terms), 2)]
    return terms[0]


def gather_pieces(values, n_seq):
    if n_seq > 8:
        return [lax.all_gather(values, "seq", axis=0)]
    pieces = {0: values}
    for mask in range(2, n_seq, 2):
        pieces[mask] = swap(values, "seq", n_seq, mask)
    for mask in range(0, n_seq, 2):
        pieces[mask + 1] = swap(pieces[mask], "seq", n_seq, 1)
    return [pieces[mask] for mask in range(n_seq)]


def place_pieces(me, refs, scratch):
    if len(refs) == 1:
        return refs[0]
    for mask, ref in enumerate(refs):
        scratch[jnp.bitwise_xor(me, mask)] = ref[...]
    return scratch


def write_kernel(dims, parts, patch_source, fresh, source, target, buffer, patches, *sems):
    patch_sem, in_sems, out_sems = sems
    requests, new_count, heads, pages, page_len, window, chunk, n_seq = dims
    lines = requests * new_count
    count = pages // parts
    spans = [pl.ds(i * count, count) for i in range(parts)]
    loads = [
        pltpu.make_async_copy(source.at[span], buffer.at[span], in_sems.at[i])
        for i, span in enumerate(spans)
    ]
    stores = [
        pltpu.make_async_copy(buffer.at[span], target.at[span], out_sems.at[i])
        for i, span in enumerate(spans)
    ]
    patch_load = pltpu.make_async_copy(patch_source, patches, patch_sem)
    patch_load.start()
    for load in loads:
        load.start()
    patch_load.wait()

    def write_patch(part, i):
        slot = patches[0, i]

        @pl.when((slot >= part * count) & (slot < (part + 1) * count))
        def _():
            r = i // 2
            row = pl.multiple_of(patches[1, i] * 16, 16)
            old = buffer[slot, pl.ds(row, 16), :]
            first = patches[2, i] * page_len + row - patches[3, i]
            line = lax.broadcasted_iota(jnp.int32, (16, lines), 0)
            token = jnp.bitwise_and(first + line, window - 1)
            column = lax.broadcasted_iota(jnp.int32, (16, lines), 1)
            pick = (token < new_count) & (column == r * new_count + token)
            new = jnp.dot(pick.astype(f32).astype(bf16), fresh[...], preferred_element_type=f32)
            row_token = jnp.bitwise_and(
                first + lax.broadcasted_iota(jnp.int32, (16, 1), 0), window - 1
            )
            buffer[slot, pl.ds(row, 16), :] = jnp.where(
                row_token < new_count, new, old.astype(f32)
            ).astype(bf16)

    for part, (load, store) in enumerate(zip(loads, stores)):
        load.wait()
        pl.loop(0, 2 * requests)(functools.partial(write_patch, part))
        store.start()
    for store in stores:
        store.wait()


def write_pool(dims, patches, fresh, kv_pool):
    parts = 4
    hbm = pl.BlockSpec(memory_space=pltpu.HBM)
    return pl.pallas_call(
        functools.partial(write_kernel, dims, parts),
        out_shape=pltpu.HBM(kv_pool.shape, kv_pool.dtype),
        in_specs=[
            pl.BlockSpec(memory_space=pl.ANY),
            pl.BlockSpec(memory_space=pltpu.VMEM),
            hbm,
        ],
        out_specs=hbm,
        scratch_shapes=[
            pltpu.VMEM(kv_pool.shape, kv_pool.dtype),
            pltpu.SMEM(patches.shape, jnp.int32),
            pltpu.SemaphoreType.DMA,
            pltpu.SemaphoreType.DMA((parts,)),
            pltpu.SemaphoreType.DMA((parts,)),
        ],
        compiler_params=pltpu.CompilerParams(vmem_limit_bytes=12 * 1024 * 1024),
        cost_estimate=pl.CostEstimate(
            flops=0, bytes_accessed=2 * kv_pool.size * 2, transcendentals=0
        ),
        name="write_pool",
    )(patches, fresh, kv_pool)


def split_three(values):
    high = values.astype(bf16).astype(f32)
    middle = (values - high).astype(bf16).astype(f32)
    low = (values - high - middle).astype(bf16).astype(f32)
    return high, middle, low


def diagonal(rows):
    return lax.broadcasted_iota(jnp.int32, (rows, 128), 0) == lax.broadcasted_iota(
        jnp.int32, (rows, 128), 1
    )


def pack_logs(columns, rows):
    eye = diagonal(rows)
    lines = [
        jnp.sum(jnp.where(eye, jnp.broadcast_to(c, (rows, 128)), 0.0), axis=0, keepdims=True)
        for c in columns
    ]
    lines += [jnp.zeros((1, 128), f32)] * (8 - len(lines))
    high, middle, low = split_three(jnp.concatenate(lines, axis=0))
    return jnp.concatenate(
        [
            jnp.concatenate([high, middle], axis=1),
            jnp.concatenate([low, jnp.zeros((8, 128), f32)], axis=1),
        ],
        axis=0,
    )


def unpack_logs(block):
    return block[0:8, 0:128] + block[0:8, 128:256] + block[8:16, 0:128]


def merge_parts(packs, requests, rows):
    total = requests * rows
    bodies = [ref[...].astype(f32) for ref in packs]
    logs = [unpack_logs(body[total : total + 16]) for body in bodies]
    eye = diagonal(rows)
    results, columns = [], []
    for r in range(requests):
        cols = [
            jnp.sum(
                jnp.where(eye, jnp.broadcast_to(log[r : r + 1, :], (rows, 128)), 0.0),
                axis=1,
                keepdims=True,
            )
            for log in logs
        ]
        top = functools.reduce(jnp.maximum, cols)
        scales = [jnp.exp(c - top) for c in cols]
        norm = functools.reduce(jnp.add, scales)
        parts = [
            body[r * rows : (r + 1) * rows] * scale for body, scale in zip(bodies, scales)
        ]
        results.append(functools.reduce(jnp.add, parts) / norm)
        columns.append(top + jnp.log(norm))
    return results, columns


def pair_kernel(requests, rows, mine, other, out):
    results, columns = merge_parts([mine, other], requests, rows)
    body = jnp.concatenate(results + [pack_logs(columns, rows)], axis=0)
    out[...] = body.astype(bf16)


def merge_pair(mine, other, requests, rows):
    return pl.pallas_call(
        functools.partial(pair_kernel, requests, rows),
        out_shape=jax.ShapeDtypeStruct(mine.shape, bf16),
        in_specs=[pl.BlockSpec(memory_space=pltpu.VMEM)] * 2,
        out_specs=pl.BlockSpec(memory_space=pltpu.VMEM),
        compiler_params=pltpu.CompilerParams(vmem_limit_bytes=8 * 1024 * 1024),
        name="merge_pair",
    )(mine, other)


def final_kernel(count, requests, rows, heads, *refs):
    packs, out, scratch_low, scratch_high = refs[:count], refs[count + 1], refs[-2], refs[-1]
    results, unused = merge_parts(packs, requests, rows)
    body = jnp.concatenate(results, axis=0)
    scratch_low[...] = body[:, 0:128]
    scratch_high[...] = body[:, 128:256]
    lines = requests * rows // heads
    for h in range(heads):
        low = scratch_low[pl.ds(h, lines, stride=heads), :]
        high = scratch_high[pl.ds(h, lines, stride=heads), :]
        out[:, h * 256 : (h + 1) * 256] = jnp.concatenate([low, high], axis=1).astype(bf16)


def merge_final(packs, token, requests, rows, heads):
    lines = requests * rows // heads
    return pl.pallas_call(
        functools.partial(final_kernel, len(packs), requests, rows, heads),
        out_shape=jax.ShapeDtypeStruct((lines, heads * 256), bf16),
        in_specs=[pl.BlockSpec(memory_space=pltpu.VMEM)] * (len(packs) + 1),
        out_specs=pl.BlockSpec(memory_space=pltpu.VMEM),
        scratch_shapes=[pltpu.VMEM((requests * rows, 128), f32)] * 2,
        compiler_params=pltpu.CompilerParams(vmem_limit_bytes=8 * 1024 * 1024),
        name="merge_final",
    )(*packs, token)


def chunk_bounds(pages, chunk):
    if pages < 2 * chunk:
        return [0, pages]
    return [0, *range(chunk // 2, pages - chunk // 2 + 1, chunk), pages]


def attention_kernel(dims, count, slot_source, cosine, sine, *refs):
    requests, new_count, heads, pages, page_len, window, chunk, n_seq = dims
    pieces, refs = refs[:count], refs[count:]
    pool, mine, theirs, fresh, buffer, gathered, projected = refs[:7]
    query_low, query_high, queries, peak, norm, total, slots, slot_sem, in_sems = refs[7:]
    slot_load = pltpu.make_async_copy(slot_source, slots, slot_sem)
    slot_load.start()
    rows = new_count * heads
    lines = requests * new_count

    bounds = chunk_bounds(pages, chunk)

    def load(c):
        span = pl.ds(bounds[c], bounds[c + 1] - bounds[c])
        return pltpu.make_async_copy(pool.at[span], buffer.at[span], in_sems.at[c])

    for c in range(len(bounds) - 1):
        load(c).start()

    me = lax.axis_index("seq")
    ordered_pieces = place_pieces(me, pieces, gathered)
    part_columns = projected.shape[1] // n_seq
    for i in range(n_seq):
        projected[:, i * part_columns : (i + 1) * part_columns] = ordered_pieces[i]
    cos = cosine[...]
    sin = sine[...]

    def turned(block):
        x = projected[:, block * 128 : (block + 1) * 128].astype(f32)
        return (x * cos + pltpu.roll(x, 64, 1) * sin).astype(bf16).astype(f32)

    for h in range(heads):
        query_low[pl.ds(h, lines, stride=heads), :] = turned(2 * h)
        query_high[pl.ds(h, lines, stride=heads), :] = projected[
            :, h * 256 + 128 : h * 256 + 256
        ].astype(f32)
    fresh[:, 0:128] = turned(2 * heads).astype(bf16)
    fresh[:, 128:512] = projected[:, heads * 256 + 128 : heads * 256 + 512]

    peak[...] = jnp.full(peak.shape, floor_peak, f32)
    norm[...] = jnp.zeros(norm.shape, f32)
    total[...] = jnp.zeros(total.shape, f32)

    token_of = lax.broadcasted_iota(jnp.int32, (rows, 1), 0) // heads
    lane = lax.broadcasted_iota(jnp.int32, (1, page_len), 1)
    scale = 256.0 ** (-0.5)

    for r in range(requests):
        span = slice(r * rows, (r + 1) * rows)
        queries[r, 0:rows, :] = jnp.concatenate(
            [query_low[span, :], query_high[span, :]], axis=1
        ).astype(bf16)

    def score(r, keys):
        return lax.dot_general(queries[r, 0:rows, :], keys, contract, preferred_element_type=f32)

    def weigh(scores, visible):
        scores = jnp.where(visible, scores * scale, low_fill)
        top = jnp.maximum(jnp.max(scores, axis=1, keepdims=True), floor_peak)
        weights = jnp.exp(scores - top)
        return top, jnp.sum(weights, axis=1, keepdims=True), weights.astype(bf16)

    def mix(weights, values):
        return jnp.dot(weights, values, preferred_element_type=f32)

    def add(r, top, amount, mixed):
        span = pl.ds(pl.multiple_of(r * rows, 8), rows)
        old = peak[span, :]
        high = jnp.maximum(old, top)
        keep = jnp.exp(old - high)
        take = jnp.exp(top - high)
        peak[span, :] = high
        norm[span, :] = norm[span, :] * keep + amount * take
        total[span, :] = total[span, :] * jnp.concatenate(
            [keep, keep], axis=1
        ) + mixed * jnp.concatenate([take, take], axis=1)

    fresh_lane = lax.broadcasted_iota(jnp.int32, (1, lines), 1)
    for step in range(-(-requests // n_seq)):
        r = me + step * n_seq

        @pl.when(r < requests)
        def _():
            index = fresh_lane - r * new_count
            seen = (index >= 0) & (index <= token_of)
            top, amount, weights = weigh(score(r, fresh[:, 0:256]), seen)
            add(r, top, amount, mix(weights, fresh[:, 256:512]))

    slot_load.wait()

    def chunk_scores(c):
        load(c).wait()
        numbers = range(bounds[c], bounds[c + 1])
        return [score(slots[0, page], buffer[page, :, 0:256]) for page in numbers]

    ahead = chunk_scores(0)
    for c in range(len(bounds) - 1):
        scores = ahead
        if c + 2 < len(bounds):
            ahead = chunk_scores(c + 1)
        numbers = range(bounds[c], bounds[c + 1])
        weighed = []
        for page, values in zip(numbers, scores):
            length = slots[1, page]
            start = slots[2, page] * page_len
            age = jnp.bitwise_and(length - 1 - start - lane, window - 1)
            limit = jnp.minimum(length - 1, window - 2 - token_of)
            weighed.append(weigh(values, age <= limit))
        mixed = [
            mix(weights, buffer[page, :, 256:512])
            for page, (top, amount, weights) in zip(numbers, weighed)
        ]
        for page, (top, amount, weights), values in zip(numbers, weighed, mixed):
            add(slots[0, page], top, amount, values)

    half = requests // 2
    core = me % 2
    for side, out in ((core, mine), (1 - core, theirs)):
        logs = []
        for k in range(half):
            span = pl.ds(pl.multiple_of((side * half + k) * rows, 8), rows)
            amount = norm[span, :]
            some = amount > 0.0
            safe = jnp.where(some, amount, 1.0)
            logs.append(jnp.where(some, peak[span, :] + jnp.log(safe), low_fill))
            inverse = jnp.where(some, 1.0 / safe, 0.0)
            total[span, :] = total[span, :] * jnp.concatenate([inverse, inverse], axis=1)
        span = pl.ds(pl.multiple_of(side * half * rows, 8), half * rows)
        out[0 : half * rows, :] = total[span, :].astype(bf16)
        out[half * rows : half * rows + 16, :] = pack_logs(logs, rows).astype(bf16)


def attention(dims, slots, cosine, sine, pieces, pool):
    requests, new_count, heads, pages, page_len, window, chunk, n_seq = dims
    part_columns = pieces[0].shape[-1]
    lines = requests * new_count
    rows = new_count * heads
    vmem = pl.BlockSpec(memory_space=pltpu.VMEM)
    pack = jax.ShapeDtypeStruct((requests // 2 * rows + 16, 256), bf16)
    return pl.pallas_call(
        functools.partial(attention_kernel, dims, len(pieces)),
        out_shape=(pack, pack, jax.ShapeDtypeStruct((requests * new_count, 512), bf16)),
        in_specs=[pl.BlockSpec(memory_space=pl.ANY), vmem, vmem]
        + [vmem] * len(pieces)
        + [pl.BlockSpec(memory_space=pltpu.HBM)],
        out_specs=(vmem, vmem, vmem),
        scratch_shapes=[
            pltpu.VMEM(pool.shape, bf16),
            pltpu.VMEM((n_seq, lines, part_columns), bf16),
            pltpu.VMEM((lines, n_seq * part_columns), bf16),
            pltpu.VMEM((requests * rows, 128), f32),
            pltpu.VMEM((requests * rows, 128), f32),
            pltpu.VMEM((requests, -(-rows // 16) * 16, 256), bf16),
            pltpu.VMEM((requests * rows, 128), f32),
            pltpu.VMEM((requests * rows, 128), f32),
            pltpu.VMEM((requests * rows, 256), f32),
            pltpu.SMEM(slots.shape, jnp.int32),
            pltpu.SemaphoreType.DMA,
            pltpu.SemaphoreType.DMA((len(chunk_bounds(pages, chunk)) - 1,)),
        ],
        compiler_params=pltpu.CompilerParams(vmem_limit_bytes=20 * 1024 * 1024),
        cost_estimate=pl.CostEstimate(flops=0, bytes_accessed=1024, transcendentals=0),
        name="page_attention",
    )(slots, cosine, sine, *pieces, pool)


def project_kernel(count, joined, mine, other, *refs):
    blocks, out, scratch = refs[:count], refs[count], refs[count + 1]
    core, plane = lax.axis_index("seq") % 2, lax.axis_index("dp")
    low = jnp.where(core == 0, mine[...], other[...])
    high = jnp.where(core == 0, other[...], mine[...])
    attended = jnp.concatenate([low, high], axis=0)
    if joined:
        rows = blocks[0].shape[0]
        for k, block in enumerate(blocks):
            span = pl.ds(pl.multiple_of((plane ^ k) * rows, 16), rows)
            scratch[span, :] = block[...]
        out[...] = lax.dot_general(
            attended, scratch[...], contract, preferred_element_type=f32
        ).astype(bf16)
        return
    products = [
        lax.dot_general(attended, block[...], contract, preferred_element_type=f32)
        for block in blocks
    ]
    columns = []
    for j in range(count):
        column = products[0]
        for k in range(1, count):
            column = jnp.where((plane ^ k) == j, products[k], column)
        columns.append(column)
    out[...] = jnp.concatenate(columns, axis=1).astype(bf16)


def project_out(mine, other, blocks):
    vmem = pl.BlockSpec(memory_space=pltpu.VMEM)
    rows, width = blocks[0].shape
    total = len(blocks) * rows
    return pl.pallas_call(
        functools.partial(project_kernel, len(blocks), rows % 16 == 0),
        out_shape=jax.ShapeDtypeStruct((2 * mine.shape[0], total), bf16),
        in_specs=[vmem] * (2 + len(blocks)),
        out_specs=vmem,
        scratch_shapes=[pltpu.VMEM((-(-total // 16) * 16, width), bf16)],
        compiler_params=pltpu.CompilerParams(vmem_limit_bytes=8 * 1024 * 1024),
        name="project_out",
    )(mine, other, *blocks)


def fetch_kernel(parts, gate_up, down, after, gates, downs, token, sems):
    units = down.shape[0]
    size = units // parts
    copies = []
    for i in range(parts):
        span = pl.ds(i * size, size)
        copies.append(pltpu.make_async_copy(gate_up.at[0, span], gates.at[0, span], sems.at[0, i]))
        copies.append(pltpu.make_async_copy(gate_up.at[1, span], gates.at[1, span], sems.at[1, i]))
        copies.append(pltpu.make_async_copy(down.at[span], downs.at[span], sems.at[2, i]))
    for copy in copies:
        copy.start()
    token[...] = jnp.zeros(token.shape, f32)
    for copy in copies:
        copy.wait()


def fetch_weights(gate_up, down, after):
    parts = max(c for c in (1, 2, 3, 4) if down.shape[0] % (16 * c) == 0)
    hbm = pl.BlockSpec(memory_space=pltpu.HBM)
    anywhere = pl.BlockSpec(memory_space=pl.ANY)
    return pl.pallas_call(
        functools.partial(fetch_kernel, parts),
        out_shape=(
            jax.ShapeDtypeStruct(gate_up.shape, bf16),
            jax.ShapeDtypeStruct(down.shape, bf16),
            jax.ShapeDtypeStruct((8, 128), f32),
        ),
        in_specs=[hbm, hbm, anywhere],
        out_specs=(anywhere, anywhere, pl.BlockSpec(memory_space=pltpu.VMEM)),
        scratch_shapes=[pltpu.SemaphoreType.DMA((3, parts))],
        compiler_params=pltpu.CompilerParams(vmem_limit_bytes=2 * 1024 * 1024),
        cost_estimate=pl.CostEstimate(
            flops=0, bytes_accessed=2 * (gate_up.size + down.size), transcendentals=0
        ),
        name="fetch_weights",
    )(
        pltpu.with_memory_space_constraint(gate_up, pltpu.HBM),
        pltpu.with_memory_space_constraint(down, pltpu.HBM),
        after,
    )


def mlp_kernel(chunk, pieces, stream, gain, gates, downs, *refs):
    heads_out, refs = refs[:pieces], refs[pieces:]
    keep, give, kept_residual, residual, total, heads_scratch = refs
    units, width = downs.shape
    me = lax.axis_index("seq")
    heads_out = place_pieces(me, heads_out, heads_scratch)
    count = units // chunk
    gathered = jnp.concatenate(
        [heads_out[i].astype(f32) for i in range(heads_out.shape[0])], axis=1
    )
    summed = stream[...].astype(f32) + gathered
    residual[...] = summed.astype(bf16).astype(f32)
    floats = residual[...]
    spread = lax.rsqrt(jnp.mean(floats * floats, axis=-1, keepdims=True) + 1e-06)
    inputs = (floats * spread * gain[...]).astype(bf16)
    root = (2.0 / 3.141592653589793) ** 0.5

    def rise(c):
        span = slice(c * chunk, (c + 1) * chunk)
        gate = lax.dot_general(inputs, gates[0, span, :], contract, preferred_element_type=f32)
        up = lax.dot_general(inputs, gates[1, span, :], contract, preferred_element_type=f32)
        inner = root * (gate + 0.044715 * (gate * gate * gate))
        return (0.5 * gate * (1.0 + jnp.tanh(inner)) * up).astype(bf16)

    def fall(c, hidden):
        span = slice(c * chunk, (c + 1) * chunk)
        product = jnp.dot(hidden, downs[span, :], preferred_element_type=f32)
        if c == 0:
            total[...] = product
        else:
            total[...] += product

    before = rise(0)
    for c in range(1, count):
        after = rise(c)
        fall(c - 1, before)
        before = after
    fall(count - 1, before)
    half = total.shape[0] // 2
    core = me % 2
    mine = pl.ds(pl.multiple_of(core * half, 8), half)
    keep[...] = total[mine, :]
    kept_residual[...] = residual[mine, :].astype(bf16)
    give[...] = total[pl.ds(pl.multiple_of((1 - core) * half, 8), half), :].astype(bf16)


def feed_forward(n_seq, stream, heads_out, gain, gates, downs):
    lines, width = stream.shape
    units = downs.shape[0]
    chunk = max(c for c in range(16, 512, 16) if units % c == 0)
    vmem = pl.BlockSpec(memory_space=pltpu.VMEM)
    return pl.pallas_call(
        functools.partial(mlp_kernel, chunk, len(heads_out)),
        out_shape=(
            jax.ShapeDtypeStruct((lines // 2, width), f32),
            jax.ShapeDtypeStruct((lines // 2, width), bf16),
            jax.ShapeDtypeStruct((lines // 2, width), bf16),
        ),
        in_specs=[vmem] * (4 + len(heads_out)),
        out_specs=(vmem, vmem, vmem),
        scratch_shapes=[
            pltpu.VMEM((lines, width), f32),
            pltpu.VMEM((lines, width), f32),
            pltpu.VMEM((n_seq, lines, width // n_seq), bf16),
        ],
        compiler_params=pltpu.CompilerParams(vmem_limit_bytes=12 * 1024 * 1024),
        name="feed_forward",
    )(stream, gain.reshape(1, width), gates, downs, *heads_out)


def half_kernel(flip, part, *refs):
    target, sem = refs[-2], refs[-1]
    count = part.shape[0]
    side = jnp.bitwise_xor(lax.axis_index("seq") % 2, flip)
    copy = pltpu.make_async_copy(part, target.at[pl.ds(side * count, count)], sem)
    copy.start()
    copy.wait()


def write_half(flip, part, started=None):
    hbm = pl.BlockSpec(memory_space=pltpu.HBM)
    earlier = [] if started is None else [started]
    return pl.pallas_call(
        functools.partial(half_kernel, flip),
        out_shape=pltpu.HBM((2 * part.shape[0], *part.shape[1:]), part.dtype),
        in_specs=[pl.BlockSpec(memory_space=pltpu.VMEM), *[hbm for _ in earlier]],
        out_specs=hbm,
        scratch_shapes=[pltpu.SemaphoreType.DMA],
        input_output_aliases={} if started is None else {1: 0},
        compiler_params=pltpu.CompilerParams(vmem_limit_bytes=2 * 1024 * 1024),
        cost_estimate=pl.CostEstimate(flops=0, bytes_accessed=4 * part.size, transcendentals=0),
        name="write_half",
    )(part, *earlier)


def body(
    n_dp,
    n_seq,
    tokens,
    attn_gain,
    qkv_weight,
    out_weight,
    mlp_gain,
    gate_up,
    down_weight,
    kv_pool,
    cache_len,
    page_table,
):
    seq_index = lax.axis_index("seq")
    dp_index = lax.axis_index("dp")
    core = seq_index % 2
    chips = n_seq // 2
    requests, new_count, width = tokens.shape
    pages, page_len, pair_width = kv_pool.shape
    head_dim = pair_width // 2
    heads = out_weight.shape[1] // head_dim
    page_count = page_table.shape[1]
    window = page_count * page_len
    lines = requests * new_count
    half = lines // 2
    rows = new_count * heads

    stream = tokens.reshape(lines, width)
    partner_weight = swap(qkv_weight, "dp", n_dp, 1)
    far = list(range(2, n_dp, 2))
    quarter_lines = lines // 4
    quarter_index = seq_index % 4
    some = requests // 4
    my_quarter = lax.dynamic_slice_in_dim(tokens, quarter_index * some, some)
    far_parts = jnp.concatenate([swap(my_quarter, "dp", n_dp, k) for k in far], axis=0)
    cache_len, page_table, far_parts = lax.optimization_barrier((cache_len, page_table, far_parts))
    far_pairs = [far_parts, swap(far_parts, "seq", n_seq, 2)]
    far_mine = jnp.concatenate(far_pairs, axis=0)
    far_other = swap(far_mine, "seq", n_seq, 1).reshape(-1, width)
    far_mine = far_mine.reshape(-1, width)
    held_pool = pltpu.with_memory_space_constraint(kv_pool, pltpu.HBM)
    groups = [stream]
    stride = len(far) * quarter_lines
    for i in range(len(far)):
        for source in (far_mine, far_other):
            for start in (i * quarter_lines, stride + i * quarter_lines):
                groups.append(source[start : start + quarter_lines])
    normed = rms_norm(jnp.concatenate(groups, axis=0), attn_gain).astype(bf16)
    by_mine = lax.dot_general(normed, qkv_weight, contract, preferred_element_type=f32)
    by_partner = lax.dot_general(normed, partner_weight, contract, preferred_element_type=f32)
    products = jnp.where(
        dp_index % 2 == 0,
        jnp.concatenate([by_mine, by_partner], axis=1),
        jnp.concatenate([by_partner, by_mine], axis=1),
    ).astype(bf16)
    out_early, products = lax.optimization_barrier((out_weight, products))
    out_blocks = {k: swap(out_early, "dp", n_dp, k) for k in [1, *far]}
    blocks = [products[:lines]]
    for i, k in enumerate(far):
        back = swap(products[(i + 1) * lines : (i + 2) * lines], "dp", n_dp, k)
        pieces = {
            m: back[n * quarter_lines : (n + 1) * quarter_lines] for n, m in enumerate((0, 2, 1, 3))
        }
        natural = []
        for j in range(4):
            piece = pieces[0]
            for m in (1, 2, 3):
                piece = jnp.where((quarter_index ^ m) == j, pieces[m], piece)
            natural.append(piece)
        blocks.append(jnp.concatenate(natural, axis=0))
    pair = dp_index // 2
    columns = []
    for j in range(n_dp // 2):
        block = blocks[0]
        for k in range(1, n_dp // 2):
            block = jnp.where((pair ^ k) == j, blocks[k], block)
        columns.append(block)
    pieces = gather_pieces(jnp.concatenate(columns, axis=1), n_seq)
    out_blocks[0] = out_weight

    positions_int = cache_len[:, None] + jnp.arange(new_count, dtype=jnp.int32)[None, :]
    quarter = head_dim // 4
    inverse = 10000.0 ** (-jnp.arange(quarter).astype(f32) / quarter)
    angles = positions_int.reshape(lines, 1).astype(f32) * inverse
    cosine = jnp.cos(angles)
    sine = jnp.sin(angles)
    cosine = jnp.concatenate([cosine, cosine], axis=1)
    sine = jnp.concatenate([-sine, sine], axis=1)
    slot_ids = seq_index * pages + jnp.arange(pages, dtype=jnp.int32)
    matches = page_table[None, :, :] == slot_ids[:, None, None]
    number = jnp.arange(page_count, dtype=jnp.int32)[None, None, :]
    owner = jnp.arange(requests, dtype=jnp.int32)[None, :, None]
    slots = jnp.stack(
        [
            jnp.sum(jnp.where(matches, owner, 0), axis=(1, 2)),
            jnp.sum(jnp.where(matches, cache_len[None, :, None], 0), axis=(1, 2)),
            jnp.sum(jnp.where(matches, number, 0), axis=(1, 2)),
        ]
    )
    ends = jnp.stack([cache_len, cache_len + (new_count - 1)], axis=1)
    end_page = (ends // page_len) % page_count
    end_block = (ends % page_len) // 16
    hit = end_page[:, :, None] == jnp.arange(page_count, dtype=jnp.int32)[None, None, :]
    end_slot = jnp.sum(jnp.where(hit, page_table[:, None, :], 0), axis=2) - seq_index * pages
    good = (end_slot >= 0) & (end_slot < pages)
    same = (end_page[:, 0] == end_page[:, 1]) & (end_block[:, 0] == end_block[:, 1])
    good = good & jnp.stack([jnp.ones_like(same), ~same], axis=1)
    patches = jnp.stack(
        [
            jnp.where(good, end_slot, -1).reshape(-1),
            end_block.reshape(-1),
            end_page.reshape(-1),
            jnp.repeat(cache_len, 2),
        ]
    )

    dims = (requests, new_count, heads, pages, page_len, window, min(16, pages), n_seq)
    slots, patches = lax.optimization_barrier((slots, patches))
    mine, theirs, fresh = attention(dims, slots, cosine, sine, pieces, held_pool)
    written_pool = write_pool(dims, patches, fresh, held_pool)

    side = requests // 2
    merged = merge_pair(mine, swap(theirs, "seq", n_seq, 1), side, rows)
    merged, *early = lax.optimization_barrier((merged, *[out_blocks[k] for k in [1, *far]]))
    for k, block in zip([1, *far], early):
        out_blocks[k] = block
    for k in far:
        out_blocks[k ^ 1] = swap(out_blocks[k], "dp", n_dp, 1)
    packs = [merged] + [swap(merged, "seq", n_seq, 2 * c) for c in range(1, chips)]
    gates, downs, token = fetch_weights(gate_up, down_weight, merged)
    packs, late = lax.optimization_barrier((packs, [out_blocks[k ^ 1] for k in far]))
    for k, block in zip(far, late):
        out_blocks[k ^ 1] = block
    attended_half = merge_final(packs, token, side, rows, heads)
    heads_part = project_out(
        attended_half,
        swap(attended_half, "seq", n_seq, 1),
        [out_blocks[k] for k in range(n_dp)],
    )
    heads_out = gather_pieces(heads_part, n_seq)
    keep, give, my_residual = feed_forward(n_seq, stream, heads_out, mlp_gain, gates, downs)
    chip_sum = (keep + swap(give, "seq", n_seq, 1).astype(f32)).astype(bf16)
    terms = [chip_sum] + [swap(chip_sum, "seq", n_seq, 2 * c) for c in range(1, chips)]
    terms, written_pool = lax.optimization_barrier((terms, written_pool))
    full_half = tree_sum([term.astype(f32) for term in terms])
    out_half = (my_residual.astype(f32) + full_half).astype(bf16)
    out_half = out_half.reshape(requests // 2, new_count, width)
    started = write_half(0, out_half)
    layer_out = write_half(1, swap(out_half, "seq", n_seq, 1), started)
    return layer_out, written_pool


def solution(mesh):
    in_specs = (
        P("dp", None, None),
        P(),
        P(("seq", "dp"), None),
        P(("seq", "dp"), None),
        P(),
        P(None, "seq", None),
        P("seq", None),
        P(("dp", "seq"), None, None),
        P("dp"),
        P("dp", None),
    )
    out_specs = (P("dp", None, None), P(("dp", "seq"), None, None))
    return jax.shard_map(
        functools.partial(body, mesh.shape["dp"], mesh.shape["seq"]),
        mesh=mesh,
        in_specs=in_specs,
        out_specs=out_specs,
        check_vma=False,
    )
```

```python
import functools

import jax
import jax.numpy as jnp
from jax import lax
from jax.experimental import pallas as pl
from jax.experimental.pallas import tpu as pltpu
from jax.sharding import PartitionSpec as P

f32 = jnp.float32
bf16 = jnp.bfloat16
low_fill = -1e30
floor_peak = -1e29
contract = (((1,), (1,)), ((), ()))


def rms_norm(values, gains):
    floats = values.astype(f32)
    return floats * lax.rsqrt(jnp.mean(floats * floats, axis=-1, keepdims=True) + 1e-06) * gains


def swap(values, axis, size, mask):
    return lax.ppermute(values, axis, [(i, i ^ mask) for i in range(size)])


def tree_sum(terms):
    while len(terms) > 1:
        terms = [terms[i] + terms[i + 1] for i in range(0, len(terms), 2)]
    return terms[0]


def gather_pieces(values, n_seq):
    if n_seq > 8:
        return [lax.all_gather(values, "seq", axis=0)]
    pieces = {0: values}
    for mask in range(2, n_seq, 2):
        pieces[mask] = swap(values, "seq", n_seq, mask)
    for mask in range(0, n_seq, 2):
        pieces[mask + 1] = swap(pieces[mask], "seq", n_seq, 1)
    return [pieces[mask] for mask in range(n_seq)]


def place_pieces(me, refs, scratch):
    if len(refs) == 1:
        return refs[0]
    for mask, ref in enumerate(refs):
        scratch[jnp.bitwise_xor(me, mask)] = ref[...]
    return scratch


def write_kernel(dims, parts, patch_source, fresh, source, target, buffer, patches, *sems):
    patch_sem, in_sems, out_sems = sems
    requests, new_count, heads, pages, page_len, window, chunk, n_seq = dims
    lines = requests * new_count
    count = pages // parts
    spans = [pl.ds(i * count, count) for i in range(parts)]
    loads = [
        pltpu.make_async_copy(source.at[span], buffer.at[span], in_sems.at[i])
        for i, span in enumerate(spans)
    ]
    stores = [
        pltpu.make_async_copy(buffer.at[span], target.at[span], out_sems.at[i])
        for i, span in enumerate(spans)
    ]
    patch_load = pltpu.make_async_copy(patch_source, patches, patch_sem)
    patch_load.start()
    for load in loads:
        load.start()
    patch_load.wait()

    def write_patch(part, i):
        slot = patches[0, i]

        @pl.when((slot >= part * count) & (slot < (part + 1) * count))
        def _():
            r = i // 2
            row = pl.multiple_of(patches[1, i] * 16, 16)
            old = buffer[slot, pl.ds(row, 16), :]
            first = patches[2, i] * page_len + row - patches[3, i]
            line = lax.broadcasted_iota(jnp.int32, (16, lines), 0)
            token = jnp.bitwise_and(first + line, window - 1)
            column = lax.broadcasted_iota(jnp.int32, (16, lines), 1)
            pick = (token < new_count) & (column == r * new_count + token)
            new = jnp.dot(pick.astype(f32).astype(bf16), fresh[...], preferred_element_type=f32)
            row_token = jnp.bitwise_and(
                first + lax.broadcasted_iota(jnp.int32, (16, 1), 0), window - 1
            )
            buffer[slot, pl.ds(row, 16), :] = jnp.where(
                row_token < new_count, new, old.astype(f32)
            ).astype(bf16)

    for part, (load, store) in enumerate(zip(loads, stores)):
        load.wait()
        pl.loop(0, 2 * requests)(functools.partial(write_patch, part))
        store.start()
    for store in stores:
        store.wait()


def write_pool(dims, patches, fresh, kv_pool):
    parts = 4
    hbm = pl.BlockSpec(memory_space=pltpu.HBM)
    return pl.pallas_call(
        functools.partial(write_kernel, dims, parts),
        out_shape=pltpu.HBM(kv_pool.shape, kv_pool.dtype),
        in_specs=[
            pl.BlockSpec(memory_space=pl.ANY),
            pl.BlockSpec(memory_space=pltpu.VMEM),
            hbm,
        ],
        out_specs=hbm,
        scratch_shapes=[
            pltpu.VMEM(kv_pool.shape, kv_pool.dtype),
            pltpu.SMEM(patches.shape, jnp.int32),
            pltpu.SemaphoreType.DMA,
            pltpu.SemaphoreType.DMA((parts,)),
            pltpu.SemaphoreType.DMA((parts,)),
        ],
        compiler_params=pltpu.CompilerParams(vmem_limit_bytes=12 * 1024 * 1024),
        cost_estimate=pl.CostEstimate(
            flops=0, bytes_accessed=2 * kv_pool.size * 2, transcendentals=0
        ),
        name="write_pool",
    )(patches, fresh, kv_pool)


def split_three(values):
    high = values.astype(bf16).astype(f32)
    middle = (values - high).astype(bf16).astype(f32)
    low = (values - high - middle).astype(bf16).astype(f32)
    return high, middle, low


def diagonal(rows):
    return lax.broadcasted_iota(jnp.int32, (rows, 128), 0) == lax.broadcasted_iota(
        jnp.int32, (rows, 128), 1
    )


def pack_logs(columns, rows):
    eye = diagonal(rows)
    lines = [
        jnp.sum(jnp.where(eye, jnp.broadcast_to(c, (rows, 128)), 0.0), axis=0, keepdims=True)
        for c in columns
    ]
    lines += [jnp.zeros((1, 128), f32)] * (8 - len(lines))
    high, middle, low = split_three(jnp.concatenate(lines, axis=0))
    return jnp.concatenate(
        [
            jnp.concatenate([high, middle], axis=1),
            jnp.concatenate([low, jnp.zeros((8, 128), f32)], axis=1),
        ],
        axis=0,
    )


def unpack_logs(block):
    return block[0:8, 0:128] + block[0:8, 128:256] + block[8:16, 0:128]


def merge_parts(packs, requests, rows):
    total = requests * rows
    bodies = [ref[...].astype(f32) for ref in packs]
    logs = [unpack_logs(body[total : total + 16]) for body in bodies]
    eye = diagonal(rows)
    results, columns = [], []
    for r in range(requests):
        cols = [
            jnp.sum(
                jnp.where(eye, jnp.broadcast_to(log[r : r + 1, :], (rows, 128)), 0.0),
                axis=1,
                keepdims=True,
            )
            for log in logs
        ]
        top = functools.reduce(jnp.maximum, cols)
        scales = [jnp.exp(c - top) for c in cols]
        norm = functools.reduce(jnp.add, scales)
        parts = [
            body[r * rows : (r + 1) * rows] * scale for body, scale in zip(bodies, scales)
        ]
        results.append(functools.reduce(jnp.add, parts) / norm)
        columns.append(top + jnp.log(norm))
    return results, columns


def pair_kernel(requests, rows, mine, other, out):
    results, columns = merge_parts([mine, other], requests, rows)
    body = jnp.concatenate(results + [pack_logs(columns, rows)], axis=0)
    out[...] = body.astype(bf16)


def merge_pair(mine, other, requests, rows):
    return pl.pallas_call(
        functools.partial(pair_kernel, requests, rows),
        out_shape=jax.ShapeDtypeStruct(mine.shape, bf16),
        in_specs=[pl.BlockSpec(memory_space=pltpu.VMEM)] * 2,
        out_specs=pl.BlockSpec(memory_space=pltpu.VMEM),
        compiler_params=pltpu.CompilerParams(vmem_limit_bytes=8 * 1024 * 1024),
        name="merge_pair",
    )(mine, other)


def final_kernel(count, requests, rows, heads, *refs):
    packs, out, scratch_low, scratch_high = refs[:count], refs[count + 1], refs[-2], refs[-1]
    results, unused = merge_parts(packs, requests, rows)
    body = jnp.concatenate(results, axis=0)
    scratch_low[...] = body[:, 0:128]
    scratch_high[...] = body[:, 128:256]
    lines = requests * rows // heads
    for h in range(heads):
        low = scratch_low[pl.ds(h, lines, stride=heads), :]
        high = scratch_high[pl.ds(h, lines, stride=heads), :]
        out[:, h * 256 : (h + 1) * 256] = jnp.concatenate([low, high], axis=1).astype(bf16)


def merge_final(packs, token, requests, rows, heads):
    lines = requests * rows // heads
    return pl.pallas_call(
        functools.partial(final_kernel, len(packs), requests, rows, heads),
        out_shape=jax.ShapeDtypeStruct((lines, heads * 256), bf16),
        in_specs=[pl.BlockSpec(memory_space=pltpu.VMEM)] * (len(packs) + 1),
        out_specs=pl.BlockSpec(memory_space=pltpu.VMEM),
        scratch_shapes=[pltpu.VMEM((requests * rows, 128), f32)] * 2,
        compiler_params=pltpu.CompilerParams(vmem_limit_bytes=8 * 1024 * 1024),
        name="merge_final",
    )(*packs, token)


def chunk_bounds(pages, chunk):
    if pages < 4 * chunk:
        return [*range(0, pages, chunk), pages]
    cut = chunk // 4
    first, last = chunk - cut, pages - chunk + cut
    count = pages // chunk - 2
    return [0, *[first + (last - first) * i // count for i in range(count + 1)], pages]


def attention_kernel(dims, count, slot_source, cosine, sine, *refs):
    requests, new_count, heads, pages, page_len, window, chunk, n_seq = dims
    pieces, refs = refs[:count], refs[count:]
    pool, mine, theirs, fresh, buffer, gathered, projected = refs[:7]
    query_low, query_high, queries, peak, norm, total, slots, slot_sem, in_sems = refs[7:]
    slot_load = pltpu.make_async_copy(slot_source, slots, slot_sem)
    slot_load.start()
    rows = new_count * heads
    lines = requests * new_count

    bounds = chunk_bounds(pages, chunk)

    def load(c):
        span = pl.ds(bounds[c], bounds[c + 1] - bounds[c])
        return pltpu.make_async_copy(pool.at[span], buffer.at[span], in_sems.at[c])

    for c in range(len(bounds) - 1):
        load(c).start()

    me = lax.axis_index("seq")
    ordered_pieces = place_pieces(me, pieces, gathered)
    part_columns = projected.shape[1] // n_seq
    for i in range(n_seq):
        projected[:, i * part_columns : (i + 1) * part_columns] = ordered_pieces[i]
    cos = cosine[...]
    sin = sine[...]

    def turned(block):
        x = projected[:, block * 128 : (block + 1) * 128].astype(f32)
        return (x * cos + pltpu.roll(x, 64, 1) * sin).astype(bf16).astype(f32)

    for h in range(heads):
        query_low[pl.ds(h, lines, stride=heads), :] = turned(2 * h)
        query_high[pl.ds(h, lines, stride=heads), :] = projected[
            :, h * 256 + 128 : h * 256 + 256
        ].astype(f32)
    fresh[:, 0:128] = turned(2 * heads).astype(bf16)
    fresh[:, 128:512] = projected[:, heads * 256 + 128 : heads * 256 + 512]

    peak[...] = jnp.full(peak.shape, floor_peak, f32)
    norm[...] = jnp.zeros(norm.shape, f32)
    total[...] = jnp.zeros(total.shape, f32)

    token_of = lax.broadcasted_iota(jnp.int32, (rows, 1), 0) // heads
    lane = lax.broadcasted_iota(jnp.int32, (1, page_len), 1)
    scale = 256.0 ** (-0.5)

    for r in range(requests):
        span = slice(r * rows, (r + 1) * rows)
        queries[r, 0:rows, :] = jnp.concatenate(
            [query_low[span, :], query_high[span, :]], axis=1
        ).astype(bf16)

    def score(r, keys):
        return lax.dot_general(queries[r, 0:rows, :], keys, contract, preferred_element_type=f32)

    def weigh(scores, visible):
        scores = jnp.where(visible, scores * scale, low_fill)
        top = jnp.maximum(jnp.max(scores, axis=1, keepdims=True), floor_peak)
        weights = jnp.exp(scores - top)
        return top, jnp.sum(weights, axis=1, keepdims=True), weights.astype(bf16)

    def mix(weights, values):
        return jnp.dot(weights, values, preferred_element_type=f32)

    def add(r, top, amount, mixed):
        span = pl.ds(pl.multiple_of(r * rows, 8), rows)
        old = peak[span, :]
        high = jnp.maximum(old, top)
        keep = jnp.exp(old - high)
        take = jnp.exp(top - high)
        peak[span, :] = high
        norm[span, :] = norm[span, :] * keep + amount * take
        total[span, :] = total[span, :] * jnp.concatenate(
            [keep, keep], axis=1
        ) + mixed * jnp.concatenate([take, take], axis=1)

    fresh_lane = lax.broadcasted_iota(jnp.int32, (1, lines), 1)
    for step in range(-(-requests // n_seq)):
        r = me + step * n_seq

        @pl.when(r < requests)
        def _():
            index = fresh_lane - r * new_count
            seen = (index >= 0) & (index <= token_of)
            top, amount, weights = weigh(score(r, fresh[:, 0:256]), seen)
            add(r, top, amount, mix(weights, fresh[:, 256:512]))

    slot_load.wait()

    def chunk_scores(c):
        load(c).wait()
        numbers = range(bounds[c], bounds[c + 1])
        return [score(slots[0, page], buffer[page, :, 0:256]) for page in numbers]

    ahead = chunk_scores(0)
    for c in range(len(bounds) - 1):
        scores = ahead
        if c + 2 < len(bounds):
            ahead = chunk_scores(c + 1)
        numbers = range(bounds[c], bounds[c + 1])
        weighed = []
        for page, values in zip(numbers, scores):
            length = slots[1, page]
            start = slots[2, page] * page_len
            age = jnp.bitwise_and(length - 1 - start - lane, window - 1)
            limit = jnp.minimum(length - 1, window - 2 - token_of)
            weighed.append(weigh(values, age <= limit))
        mixed = [
            mix(weights, buffer[page, :, 256:512])
            for page, (top, amount, weights) in zip(numbers, weighed)
        ]
        for page, (top, amount, weights), values in zip(numbers, weighed, mixed):
            add(slots[0, page], top, amount, values)

    half = requests // 2
    core = me % 2
    for side, out in ((core, mine), (1 - core, theirs)):
        logs = []
        for k in range(half):
            span = pl.ds(pl.multiple_of((side * half + k) * rows, 8), rows)
            amount = norm[span, :]
            some = amount > 0.0
            safe = jnp.where(some, amount, 1.0)
            logs.append(jnp.where(some, peak[span, :] + jnp.log(safe), low_fill))
            inverse = jnp.where(some, 1.0 / safe, 0.0)
            total[span, :] = total[span, :] * jnp.concatenate([inverse, inverse], axis=1)
        span = pl.ds(pl.multiple_of(side * half * rows, 8), half * rows)
        out[0 : half * rows, :] = total[span, :].astype(bf16)
        out[half * rows : half * rows + 16, :] = pack_logs(logs, rows).astype(bf16)


def attention(dims, slots, cosine, sine, pieces, pool):
    requests, new_count, heads, pages, page_len, window, chunk, n_seq = dims
    part_columns = pieces[0].shape[-1]
    lines = requests * new_count
    rows = new_count * heads
    vmem = pl.BlockSpec(memory_space=pltpu.VMEM)
    pack = jax.ShapeDtypeStruct((requests // 2 * rows + 16, 256), bf16)
    return pl.pallas_call(
        functools.partial(attention_kernel, dims, len(pieces)),
        out_shape=(pack, pack, jax.ShapeDtypeStruct((requests * new_count, 512), bf16)),
        in_specs=[pl.BlockSpec(memory_space=pl.ANY), vmem, vmem]
        + [vmem] * len(pieces)
        + [pl.BlockSpec(memory_space=pltpu.HBM)],
        out_specs=(vmem, vmem, vmem),
        scratch_shapes=[
            pltpu.VMEM(pool.shape, bf16),
            pltpu.VMEM((n_seq, lines, part_columns), bf16),
            pltpu.VMEM((lines, n_seq * part_columns), bf16),
            pltpu.VMEM((requests * rows, 128), f32),
            pltpu.VMEM((requests * rows, 128), f32),
            pltpu.VMEM((requests, -(-rows // 16) * 16, 256), bf16),
            pltpu.VMEM((requests * rows, 128), f32),
            pltpu.VMEM((requests * rows, 128), f32),
            pltpu.VMEM((requests * rows, 256), f32),
            pltpu.SMEM(slots.shape, jnp.int32),
            pltpu.SemaphoreType.DMA,
            pltpu.SemaphoreType.DMA((len(chunk_bounds(pages, chunk)) - 1,)),
        ],
        compiler_params=pltpu.CompilerParams(vmem_limit_bytes=20 * 1024 * 1024),
        cost_estimate=pl.CostEstimate(flops=0, bytes_accessed=1024, transcendentals=0),
        name="page_attention",
    )(slots, cosine, sine, *pieces, pool)


def project_kernel(count, joined, mine, other, *refs):
    blocks, out, scratch = refs[:count], refs[count], refs[count + 1]
    core, plane = lax.axis_index("seq") % 2, lax.axis_index("dp")
    low = jnp.where(core == 0, mine[...], other[...])
    high = jnp.where(core == 0, other[...], mine[...])
    attended = jnp.concatenate([low, high], axis=0)
    if joined:
        rows = blocks[0].shape[0]
        for k, block in enumerate(blocks):
            span = pl.ds(pl.multiple_of((plane ^ k) * rows, 16), rows)
            scratch[span, :] = block[...]
        out[...] = lax.dot_general(
            attended, scratch[...], contract, preferred_element_type=f32
        ).astype(bf16)
        return
    products = [
        lax.dot_general(attended, block[...], contract, preferred_element_type=f32)
        for block in blocks
    ]
    columns = []
    for j in range(count):
        column = products[0]
        for k in range(1, count):
            column = jnp.where((plane ^ k) == j, products[k], column)
        columns.append(column)
    out[...] = jnp.concatenate(columns, axis=1).astype(bf16)


def project_out(mine, other, blocks):
    vmem = pl.BlockSpec(memory_space=pltpu.VMEM)
    rows, width = blocks[0].shape
    total = len(blocks) * rows
    return pl.pallas_call(
        functools.partial(project_kernel, len(blocks), rows % 16 == 0),
        out_shape=jax.ShapeDtypeStruct((2 * mine.shape[0], total), bf16),
        in_specs=[vmem] * (2 + len(blocks)),
        out_specs=vmem,
        scratch_shapes=[pltpu.VMEM((-(-total // 16) * 16, width), bf16)],
        compiler_params=pltpu.CompilerParams(vmem_limit_bytes=8 * 1024 * 1024),
        name="project_out",
    )(mine, other, *blocks)


def fetch_kernel(parts, gate_up, down, after, gates, downs, token, sems):
    units = down.shape[0]
    size = units // parts
    copies = []
    for i in range(parts):
        span = pl.ds(i * size, size)
        copies.append(pltpu.make_async_copy(gate_up.at[0, span], gates.at[0, span], sems.at[0, i]))
        copies.append(pltpu.make_async_copy(gate_up.at[1, span], gates.at[1, span], sems.at[1, i]))
        copies.append(pltpu.make_async_copy(down.at[span], downs.at[span], sems.at[2, i]))
    for copy in copies:
        copy.start()
    token[...] = jnp.zeros(token.shape, f32)
    for copy in copies:
        copy.wait()


def fetch_weights(gate_up, down, after):
    parts = max(c for c in (1, 2, 3, 4) if down.shape[0] % (16 * c) == 0)
    hbm = pl.BlockSpec(memory_space=pltpu.HBM)
    anywhere = pl.BlockSpec(memory_space=pl.ANY)
    return pl.pallas_call(
        functools.partial(fetch_kernel, parts),
        out_shape=(
            jax.ShapeDtypeStruct(gate_up.shape, bf16),
            jax.ShapeDtypeStruct(down.shape, bf16),
            jax.ShapeDtypeStruct((8, 128), f32),
        ),
        in_specs=[hbm, hbm, anywhere],
        out_specs=(anywhere, anywhere, pl.BlockSpec(memory_space=pltpu.VMEM)),
        scratch_shapes=[pltpu.SemaphoreType.DMA((3, parts))],
        compiler_params=pltpu.CompilerParams(vmem_limit_bytes=2 * 1024 * 1024),
        cost_estimate=pl.CostEstimate(
            flops=0, bytes_accessed=2 * (gate_up.size + down.size), transcendentals=0
        ),
        name="fetch_weights",
    )(
        pltpu.with_memory_space_constraint(gate_up, pltpu.HBM),
        pltpu.with_memory_space_constraint(down, pltpu.HBM),
        after,
    )


def mlp_kernel(chunk, pieces, stream, gain, gates, downs, *refs):
    heads_out, refs = refs[:pieces], refs[pieces:]
    keep, give, kept_residual, residual, total, heads_scratch = refs
    units, width = downs.shape
    me = lax.axis_index("seq")
    heads_out = place_pieces(me, heads_out, heads_scratch)
    count = units // chunk
    gathered = jnp.concatenate(
        [heads_out[i].astype(f32) for i in range(heads_out.shape[0])], axis=1
    )
    summed = stream[...].astype(f32) + gathered
    residual[...] = summed.astype(bf16).astype(f32)
    floats = residual[...]
    spread = lax.rsqrt(jnp.mean(floats * floats, axis=-1, keepdims=True) + 1e-06)
    inputs = (floats * spread * gain[...]).astype(bf16)
    root = (2.0 / 3.141592653589793) ** 0.5

    def rise(c):
        span = slice(c * chunk, (c + 1) * chunk)
        gate = lax.dot_general(inputs, gates[0, span, :], contract, preferred_element_type=f32)
        up = lax.dot_general(inputs, gates[1, span, :], contract, preferred_element_type=f32)
        inner = root * (gate + 0.044715 * (gate * gate * gate))
        return (0.5 * gate * (1.0 + jnp.tanh(inner)) * up).astype(bf16)

    def fall(c, hidden):
        span = slice(c * chunk, (c + 1) * chunk)
        product = jnp.dot(hidden, downs[span, :], preferred_element_type=f32)
        if c == 0:
            total[...] = product
        else:
            total[...] += product

    before = rise(0)
    for c in range(1, count):
        after = rise(c)
        fall(c - 1, before)
        before = after
    fall(count - 1, before)
    half = total.shape[0] // 2
    core = me % 2
    mine = pl.ds(pl.multiple_of(core * half, 8), half)
    keep[...] = total[mine, :]
    kept_residual[...] = residual[mine, :].astype(bf16)
    give[...] = total[pl.ds(pl.multiple_of((1 - core) * half, 8), half), :].astype(bf16)


def feed_forward(n_seq, stream, heads_out, gain, gates, downs):
    lines, width = stream.shape
    units = downs.shape[0]
    chunk = max(c for c in range(16, 512, 16) if units % c == 0)
    vmem = pl.BlockSpec(memory_space=pltpu.VMEM)
    return pl.pallas_call(
        functools.partial(mlp_kernel, chunk, len(heads_out)),
        out_shape=(
            jax.ShapeDtypeStruct((lines // 2, width), f32),
            jax.ShapeDtypeStruct((lines // 2, width), bf16),
            jax.ShapeDtypeStruct((lines // 2, width), bf16),
        ),
        in_specs=[vmem] * (4 + len(heads_out)),
        out_specs=(vmem, vmem, vmem),
        scratch_shapes=[
            pltpu.VMEM((lines, width), f32),
            pltpu.VMEM((lines, width), f32),
            pltpu.VMEM((n_seq, lines, width // n_seq), bf16),
        ],
        compiler_params=pltpu.CompilerParams(vmem_limit_bytes=12 * 1024 * 1024),
        name="feed_forward",
    )(stream, gain.reshape(1, width), gates, downs, *heads_out)


def half_kernel(flip, part, *refs):
    target, sem = refs[-2], refs[-1]
    count = part.shape[0]
    side = jnp.bitwise_xor(lax.axis_index("seq") % 2, flip)
    copy = pltpu.make_async_copy(part, target.at[pl.ds(side * count, count)], sem)
    copy.start()
    copy.wait()


def write_half(flip, part, started=None):
    hbm = pl.BlockSpec(memory_space=pltpu.HBM)
    earlier = [] if started is None else [started]
    return pl.pallas_call(
        functools.partial(half_kernel, flip),
        out_shape=pltpu.HBM((2 * part.shape[0], *part.shape[1:]), part.dtype),
        in_specs=[pl.BlockSpec(memory_space=pltpu.VMEM), *[hbm for _ in earlier]],
        out_specs=hbm,
        scratch_shapes=[pltpu.SemaphoreType.DMA],
        input_output_aliases={} if started is None else {1: 0},
        compiler_params=pltpu.CompilerParams(vmem_limit_bytes=2 * 1024 * 1024),
        cost_estimate=pl.CostEstimate(flops=0, bytes_accessed=4 * part.size, transcendentals=0),
        name="write_half",
    )(part, *earlier)


def body(
    n_dp,
    n_seq,
    tokens,
    attn_gain,
    qkv_weight,
    out_weight,
    mlp_gain,
    gate_up,
    down_weight,
    kv_pool,
    cache_len,
    page_table,
):
    seq_index = lax.axis_index("seq")
    dp_index = lax.axis_index("dp")
    core = seq_index % 2
    chips = n_seq // 2
    requests, new_count, width = tokens.shape
    pages, page_len, pair_width = kv_pool.shape
    head_dim = pair_width // 2
    heads = out_weight.shape[1] // head_dim
    page_count = page_table.shape[1]
    window = page_count * page_len
    lines = requests * new_count
    half = lines // 2
    rows = new_count * heads

    stream = tokens.reshape(lines, width)
    partner_weight = swap(qkv_weight, "dp", n_dp, 1)
    far = list(range(2, n_dp, 2))
    quarter_lines = lines // 4
    quarter_index = seq_index % 4
    some = requests // 4
    my_quarter = lax.dynamic_slice_in_dim(tokens, quarter_index * some, some)
    far_parts = jnp.concatenate([swap(my_quarter, "dp", n_dp, k) for k in far], axis=0)
    cache_len, page_table, far_parts = lax.optimization_barrier((cache_len, page_table, far_parts))
    far_pairs = [far_parts, swap(far_parts, "seq", n_seq, 2)]
    far_mine = jnp.concatenate(far_pairs, axis=0)
    far_other = swap(far_mine, "seq", n_seq, 1).reshape(-1, width)
    far_mine = far_mine.reshape(-1, width)
    held_pool = pltpu.with_memory_space_constraint(kv_pool, pltpu.HBM)
    groups = [stream]
    stride = len(far) * quarter_lines
    for i in range(len(far)):
        for source in (far_mine, far_other):
            for start in (i * quarter_lines, stride + i * quarter_lines):
                groups.append(source[start : start + quarter_lines])
    normed = rms_norm(jnp.concatenate(groups, axis=0), attn_gain).astype(bf16)
    by_mine = lax.dot_general(normed, qkv_weight, contract, preferred_element_type=f32)
    by_partner = lax.dot_general(normed, partner_weight, contract, preferred_element_type=f32)
    products = jnp.where(
        dp_index % 2 == 0,
        jnp.concatenate([by_mine, by_partner], axis=1),
        jnp.concatenate([by_partner, by_mine], axis=1),
    ).astype(bf16)
    out_early, products = lax.optimization_barrier((out_weight, products))
    out_blocks = {k: swap(out_early, "dp", n_dp, k) for k in [1, *far]}
    blocks = [products[:lines]]
    for i, k in enumerate(far):
        back = swap(products[(i + 1) * lines : (i + 2) * lines], "dp", n_dp, k)
        pieces = {
            m: back[n * quarter_lines : (n + 1) * quarter_lines] for n, m in enumerate((0, 2, 1, 3))
        }
        natural = []
        for j in range(4):
            piece = pieces[0]
            for m in (1, 2, 3):
                piece = jnp.where((quarter_index ^ m) == j, pieces[m], piece)
            natural.append(piece)
        blocks.append(jnp.concatenate(natural, axis=0))
    pair = dp_index // 2
    columns = []
    for j in range(n_dp // 2):
        block = blocks[0]
        for k in range(1, n_dp // 2):
            block = jnp.where((pair ^ k) == j, blocks[k], block)
        columns.append(block)
    pieces = gather_pieces(jnp.concatenate(columns, axis=1), n_seq)
    out_blocks[0] = out_weight

    positions_int = cache_len[:, None] + jnp.arange(new_count, dtype=jnp.int32)[None, :]
    quarter = head_dim // 4
    inverse = 10000.0 ** (-jnp.arange(quarter).astype(f32) / quarter)
    angles = positions_int.reshape(lines, 1).astype(f32) * inverse
    cosine = jnp.cos(angles)
    sine = jnp.sin(angles)
    cosine = jnp.concatenate([cosine, cosine], axis=1)
    sine = jnp.concatenate([-sine, sine], axis=1)
    slot_ids = seq_index * pages + jnp.arange(pages, dtype=jnp.int32)
    matches = page_table[None, :, :] == slot_ids[:, None, None]
    number = jnp.arange(page_count, dtype=jnp.int32)[None, None, :]
    owner = jnp.arange(requests, dtype=jnp.int32)[None, :, None]
    slots = jnp.stack(
        [
            jnp.sum(jnp.where(matches, owner, 0), axis=(1, 2)),
            jnp.sum(jnp.where(matches, cache_len[None, :, None], 0), axis=(1, 2)),
            jnp.sum(jnp.where(matches, number, 0), axis=(1, 2)),
        ]
    )
    ends = jnp.stack([cache_len, cache_len + (new_count - 1)], axis=1)
    end_page = (ends // page_len) % page_count
    end_block = (ends % page_len) // 16
    hit = end_page[:, :, None] == jnp.arange(page_count, dtype=jnp.int32)[None, None, :]
    end_slot = jnp.sum(jnp.where(hit, page_table[:, None, :], 0), axis=2) - seq_index * pages
    good = (end_slot >= 0) & (end_slot < pages)
    same = (end_page[:, 0] == end_page[:, 1]) & (end_block[:, 0] == end_block[:, 1])
    good = good & jnp.stack([jnp.ones_like(same), ~same], axis=1)
    patches = jnp.stack(
        [
            jnp.where(good, end_slot, -1).reshape(-1),
            end_block.reshape(-1),
            end_page.reshape(-1),
            jnp.repeat(cache_len, 2),
        ]
    )

    dims = (requests, new_count, heads, pages, page_len, window, min(16, pages), n_seq)
    slots, patches = lax.optimization_barrier((slots, patches))
    mine, theirs, fresh = attention(dims, slots, cosine, sine, pieces, held_pool)
    written_pool = write_pool(dims, patches, fresh, held_pool)

    side = requests // 2
    merged = merge_pair(mine, swap(theirs, "seq", n_seq, 1), side, rows)
    merged, *early = lax.optimization_barrier((merged, *[out_blocks[k] for k in [1, *far]]))
    for k, block in zip([1, *far], early):
        out_blocks[k] = block
    for k in far:
        out_blocks[k ^ 1] = swap(out_blocks[k], "dp", n_dp, 1)
    packs = [merged] + [swap(merged, "seq", n_seq, 2 * c) for c in range(1, chips)]
    gates, downs, token = fetch_weights(gate_up, down_weight, merged)
    packs, late = lax.optimization_barrier((packs, [out_blocks[k ^ 1] for k in far]))
    for k, block in zip(far, late):
        out_blocks[k ^ 1] = block
    attended_half = merge_final(packs, token, side, rows, heads)
    heads_part = project_out(
        attended_half,
        swap(attended_half, "seq", n_seq, 1),
        [out_blocks[k] for k in range(n_dp)],
    )
    heads_out = gather_pieces(heads_part, n_seq)
    keep, give, my_residual = feed_forward(n_seq, stream, heads_out, mlp_gain, gates, downs)
    chip_sum = (keep + swap(give, "seq", n_seq, 1).astype(f32)).astype(bf16)
    terms = [chip_sum] + [swap(chip_sum, "seq", n_seq, 2 * c) for c in range(1, chips)]
    terms, written_pool = lax.optimization_barrier((terms, written_pool))
    full_half = tree_sum([term.astype(f32) for term in terms])
    out_half = (my_residual.astype(f32) + full_half).astype(bf16)
    out_half = out_half.reshape(requests // 2, new_count, width)
    started = write_half(0, out_half)
    layer_out = write_half(1, swap(out_half, "seq", n_seq, 1), started)
    return layer_out, written_pool


def solution(mesh):
    in_specs = (
        P("dp", None, None),
        P(),
        P(("seq", "dp"), None),
        P(("seq", "dp"), None),
        P(),
        P(None, "seq", None),
        P("seq", None),
        P(("dp", "seq"), None, None),
        P("dp"),
        P("dp", None),
    )
    out_specs = (P("dp", None, None), P(("dp", "seq"), None, None))
    return jax.shard_map(
        functools.partial(body, mesh.shape["dp"], mesh.shape["seq"]),
        mesh=mesh,
        in_specs=in_specs,
        out_specs=out_specs,
        check_vma=False,
    )
```
